256 devices in a mesh: pipe: 4 (over x), expert: 16 (over z, core), dp: 4 (over y).
Axes of the slice: x: 4, y: 4, z: 8, core: 2. Of those that a mesh axis runs over, the one named last changes fastest.
Arguments:
- seed_grads: bfloat16 [2, 4096, 3584], P(None, ('expert', 'dp')), may hold values from -6 to 6
- expert_routes: int32 [2, 4, 4096, 2], P(None, 'pipe', ('expert', 'dp')), may hold values from 0 to 15, all different within a row; in each aligned block of 64 rows (0 to 63, 64 to 127, ..., all dimensions but the last counted through in order) at most 9 rows name the same one
- route_weights: float32 [2, 4, 4096, 2], P(None, 'pipe', ('expert', 'dp')), may hold values from 0.1 to 1
- saved_gate: bfloat16 [2, 4, 4, 16, 144, 1024], P(None, 'pipe', 'dp', 'expert'), may hold values from -6 to 6
- saved_up: bfloat16 [2, 4, 4, 16, 144, 1024], P(None, 'pipe', 'dp', 'expert'), may hold values from -6 to 6
- w_gate: bfloat16 [4, 16, 3584, 1024], P('pipe', 'expert', 'dp'), may hold values from -0.09375 to 0.09375
- w_up: bfloat16 [4, 16, 3584, 1024], P('pipe', 'expert', 'dp'), may hold values from -0.09375 to 0.09375
- w_down: bfloat16 [4, 16, 1024, 3584], P('pipe', 'expert', 'dp'), may hold values from -0.1875 to 0.1875
Outputs:
- input_grads: bfloat16 [2, 4, 4096, 3584], P(None, 'pipe', ('expert', 'dp'))
- down_grads: bfloat16 [4, 16, 1024, 3584], P('pipe', 'expert', 'dp')
The draws below stay inside these ranges and needn't reach their ends.
Inputs may be any that keep to these rules, and one draw needn't show every extreme that they name: `expert_routes`: each row names 2 different experts; among the 64 rows of one device no expert is named more than 9 times, and in every draw some device names some expert exactly 9 times.
All inputs are finite; a program needn't handle non-finite values.
Results may differ from the reference program's by a relative error of at most 0.015.
Values may be sent and summed in bfloat16 or wider, within the bound.
No kernel may reach another device: no remote copies, remote signals or barrier semaphores. Data moves between devices by JAX's collectives and lax.ppermute only.
A program may use at most 320 MiB of HBM per device.

```python
import math
import jax
import jax.numpy as jnp
import numpy as np
from jax import lax

D = 3584
FF = 1024
TOP = 2
TOK_DEV = 64
EXPERTS = 16
CAP = 9
SLOTS = 144
LAYERS = 4
REPLICAS = 4
TOKENS = 4096


def levels(key, extent, shards, smallest, largest):
    def one(position, parts):
        steps = jax.random.uniform(jax.random.fold_in(jax.random.fold_in(key, 6), position), (parts,), jnp.float32, smallest / len(shards), largest / len(shards))
        return jnp.repeat(jnp.exp(steps), extent[position] // parts).reshape((-1,) + (1,) * (len(extent) - position - 1))

    gain = one(*shards[0])
    for cut in shards[1:]:
        gain = gain * one(*cut)
    return gain


def deal_out(stream_key, own, number, rows, amount, top, most, skew):
    ranking = jax.random.permutation(stream_key, amount)
    packed, ordinary = portions_of(amount, rows * top, most, skew, True), portions_of(amount, rows * top, most, skew, False)
    places = jnp.arange(amount)

    def named(sizes, rotation):
        used = int((sizes > 0).sum())
        fixed = max(1, used // 4)
        shifted = fixed + (places - fixed + rotation * (used - fixed)) % max(1, amount - fixed)
        return jnp.zeros((amount,), jnp.int32).at[ranking[jnp.where(places < fixed, places, shifted)]].set(jnp.asarray(sizes, jnp.int32))

    sizes = jnp.where(number % 4 == 0, named(packed, number // 4), named(ordinary, number - number // 4 - 1))
    mixed = jax.random.permutation(jax.random.fold_in(own, 3), amount)
    donor, sink = mixed[0:amount // 2 * 2:2], mixed[1:amount // 2 * 2:2]
    room = jnp.minimum(sizes[donor] - 1, most - sizes[sink]) // 2
    room = jnp.where((donor == ranking[0]) | (sink == ranking[0]) | (sizes[sink] == 0), 0, jnp.maximum(room, 0))
    shifted = jax.random.randint(jax.random.fold_in(own, 4), (amount // 2,), 0, 1 << 20) % (room + 1)
    sizes = sizes.at[donor].add(-shifted).at[sink].add(shifted)
    labels = jnp.searchsorted(jnp.cumsum(sizes), jnp.arange(rows * top), side="right").astype(jnp.int32)
    grid = labels.reshape(top, rows).T
    grid = grid[jax.random.permutation(jax.random.fold_in(own, 1), rows)]
    rotation = jax.random.randint(jax.random.fold_in(own, 2), (rows, 1), 0, top)
    return jnp.take_along_axis(grid, (jnp.arange(top)[None, :] + rotation) % top, axis=1)


def portions_of(count, total, limit, lean, full):
    portions = [(1 << 20) // math.isqrt(rank ** lean) + 1 for rank in range(1, count + 1)]
    largest = limit if full else min(limit, max(-(-total // count), total * portions[0] // sum(portions)))
    least = 1 if total - largest >= count - 1 else 0
    holding, surplus = [largest] + [least] * (count - 1), total - largest - least * (count - 1)
    while surplus > 0:
        candidates = [i for i in range(1, count) if holding[i] < largest] or [i for i in range(1, count) if holding[i] < limit]
        mass, budget = sum([portions[i] for i in candidates]), surplus
        for i in candidates:
            more = min(limit - holding[i], max(1, budget * portions[i] // mass), surplus)
            holding[i] = holding[i] + more
            surplus = surplus - more
    return np.array(holding)


def centred(key, shape, deviation, reach, split=(), kind=jnp.bfloat16):
    drawn = deviation * jax.random.normal(key, shape, jnp.float32)
    if split:
        drawn = drawn * levels(key, shape, split, -0.22, 0.18)
    return jnp.clip(drawn, -reach, reach).astype(kind)


def setup_inputs(seed: int = 0) -> dict:
    streams_of = jax.random.split(jax.random.key(seed), 9)
    seed_grads = centred(streams_of[0], (2, TOKENS, D), 1.0, 6.0, ((1, 64),))
    expert_routes_keys = jax.random.split(jax.random.fold_in(streams_of[1], 1), 2 * LAYERS * TOKENS // TOK_DEV)
    expert_routes_turns = jax.random.permutation(jax.random.fold_in(streams_of[1], 3), 2 * LAYERS * TOKENS // TOK_DEV)
    expert_routes = jax.vmap(lambda own, number: deal_out(jax.random.fold_in(streams_of[1], 2), own, number, TOK_DEV, EXPERTS, TOP, CAP, 2))(expert_routes_keys, expert_routes_turns).reshape((2, LAYERS, TOKENS, TOP))
    route_weights = jnp.clip(jnp.exp(math.log(1.0) - 2.3025851 * jax.random.uniform(streams_of[2], (2, LAYERS, TOKENS, TOP), jnp.float32) ** levels(streams_of[2], (2, LAYERS, TOKENS, TOP), ((1, 4), (2, 64)), -0.2, 0.2)), 0.1, 1.0)
    saved_gate = centred(streams_of[3], (2, LAYERS, REPLICAS, EXPERTS, SLOTS, FF), 1.0, 6.0, ((1, 4), (2, 4), (3, 16)))
    saved_up = centred(streams_of[4], (2, LAYERS, REPLICAS, EXPERTS, SLOTS, FF), 1.0, 6.0, ((1, 4), (2, 4), (3, 16)))
    w_gate = centred(streams_of[5], (LAYERS, EXPERTS, D, FF), D ** -0.5, 0.09375, ((0, 4), (1, 16), (2, 4)))
    w_up = centred(streams_of[6], (LAYERS, EXPERTS, D, FF), D ** -0.5, 0.09375, ((0, 4), (1, 16), (2, 4)))
    w_down = centred(streams_of[7], (LAYERS, EXPERTS, FF, D), FF ** -0.5, 0.1875, ((0, 4), (1, 16), (2, 4)))
    return dict(seed_grads=seed_grads, expert_routes=expert_routes, route_weights=route_weights, saved_gate=saved_gate, saved_up=saved_up, w_gate=w_gate, w_up=w_up, w_down=w_down)


def slot_index(routes_layer):
    blocks = TOKENS // TOK_DEV
    flattened = routes_layer.reshape(blocks, TOK_DEV * TOP)
    experts = jnp.arange(EXPERTS, dtype=jnp.int32)
    onehot = (flattened[:, :, None] == experts[None, None, :]).astype(jnp.int32)
    rank_in = jnp.sum((jnp.cumsum(onehot, axis=1) - onehot) * onehot, axis=2)
    source = jnp.arange(blocks, dtype=jnp.int32) // REPLICAS
    return (source[:, None] * CAP + rank_in).reshape(TOKENS, TOP).astype(jnp.int32)


def expert_step(operands):
    gate_e, up_e, scaled_e, gate_w, up_w, down_w = operands
    gate_pre = gate_e.reshape(-1, FF).astype(jnp.float32)
    up_pre = up_e.reshape(-1, FF).astype(jnp.float32)
    rows_grad = scaled_e.reshape(-1, D)
    contract = (((1,), (1,)), ((), ()))
    d_hidden = lax.dot_general(rows_grad, down_w, contract, preferred_element_type=jnp.float32)
    sigmoid_gate = jax.nn.sigmoid(gate_pre)
    activated = gate_pre * sigmoid_gate
    hidden = (activated * up_pre).astype(jnp.bfloat16)
    d_up = (d_hidden * activated).astype(jnp.bfloat16)
    d_gate = (d_hidden * up_pre * sigmoid_gate * (1.0 + gate_pre * (1.0 - sigmoid_gate))).astype(jnp.bfloat16)
    d_input = lax.dot_general(d_gate, gate_w, contract, preferred_element_type=jnp.float32)
    d_input = d_input + lax.dot_general(d_up, up_w, contract, preferred_element_type=jnp.float32)
    return d_input.astype(jnp.bfloat16).reshape(scaled_e.shape), hidden.reshape(REPLICAS, SLOTS, FF)


def layer_back(grad_out, routes_layer, weights_layer, gate_layer_saved, up_layer_saved, gate_layer, up_layer, down_layer):
    slot_of = slot_index(routes_layer)
    replica = (jnp.arange(TOKENS, dtype=jnp.int32) // TOK_DEV) % REPLICAS
    scaled = (weights_layer[:, :, None] * grad_out[:, None, :].astype(jnp.float32)).astype(jnp.bfloat16)
    scaled_rows = jnp.zeros((EXPERTS, REPLICAS, SLOTS, D), jnp.bfloat16)
    scaled_rows = scaled_rows.at[routes_layer, replica[:, None], slot_of].set(scaled)
    gate_moved = jnp.swapaxes(gate_layer_saved, 0, 1)
    up_moved = jnp.swapaxes(up_layer_saved, 0, 1)
    slot_grads, hidden = lax.map(expert_step, (gate_moved, up_moved, scaled_rows, gate_layer, up_layer, down_layer))
    returned = slot_grads[routes_layer, replica[:, None], slot_of]
    grad_in = grad_out.astype(jnp.float32) + jnp.sum(returned.astype(jnp.float32), axis=1)
    return grad_in.astype(jnp.bfloat16), scaled_rows, hidden


def down_term(operands):
    hidden_pair, scaled_pair = operands
    contract_rows = (((0,), (0,)), ((), ()))
    total = jnp.zeros((FF, D), jnp.float32)
    for replica_at in range(REPLICAS):
        partial_sum = jnp.zeros((FF, D), jnp.float32)
        for direction in range(2):
            partial_sum = partial_sum + lax.dot_general(hidden_pair[direction, replica_at], scaled_pair[direction, replica_at], contract_rows, preferred_element_type=jnp.float32)
        rounded = lax.optimization_barrier(partial_sum.astype(jnp.bfloat16))
        total = total + rounded.astype(jnp.float32)
    return total.astype(jnp.bfloat16)


def reference(seed_grads, expert_routes, route_weights, saved_gate, saved_up, w_gate, w_up, w_down):
    grads_all = [[None] * LAYERS, [None] * LAYERS]
    scaled_all = [[None] * LAYERS, [None] * LAYERS]
    hidden_all = [[None] * LAYERS, [None] * LAYERS]
    for direction in range(2):
        current = seed_grads[direction]
        if direction == 0:
            layer_order = list(range(LAYERS - 1, -1, -1))
        else:
            layer_order = list(range(LAYERS))
        for layer_at in layer_order:
            current, scaled_rows, hidden = layer_back(current, expert_routes[direction, layer_at], route_weights[direction, layer_at], saved_gate[direction, layer_at], saved_up[direction, layer_at], w_gate[layer_at], w_up[layer_at], w_down[layer_at])
            grads_all[direction][layer_at] = current
            scaled_all[direction][layer_at] = scaled_rows
            hidden_all[direction][layer_at] = hidden
    input_grads = jnp.stack([jnp.stack(grads_all[0]), jnp.stack(grads_all[1])])
    down_list = []
    for layer_at in range(LAYERS):
        hidden_pair = jnp.stack([hidden_all[0][layer_at], hidden_all[1][layer_at]], axis=1)
        scaled_pair = jnp.stack([scaled_all[0][layer_at], scaled_all[1][layer_at]], axis=1)
        down_list.append(lax.map(down_term, (hidden_pair, scaled_pair)))
    down_grads = jnp.stack(down_list)
    return input_grads, down_grads
```

```python
import functools
import jax
import jax.numpy as jnp
from jax import lax
from jax.experimental import pallas as pl
from jax.experimental.pallas import tpu as pltpu
from jax.sharding import PartitionSpec as P

BF = jnp.bfloat16
F32 = jnp.float32
I32 = jnp.int32
D = 3584
FF = 1024
TOK = 64
EXP = 16
CAP = 9
SLOTS = 144
MAIN = 128
CH = 896
PCH = 1024
NCH = 4
PIECES = 7
NT = (((1,), (1,)), ((), ()))
NN = (((1,), (0,)), ((), ()))


def dot(a, b, dims=NN):
    return lax.dot_general(a, b, dims, preferred_element_type=F32)


def ones_where(mask):
    return jnp.where(mask, 1.0, 0.0).astype(BF)


def prep_kernel(order_ref, gate_ref, up_ref, fup_ref, fgate_ref, hidden_ref):
    row = lax.broadcasted_iota(I32, (SLOTS, SLOTS), 0)
    col = lax.broadcasted_iota(I32, (SLOTS, SLOTS), 1)
    slot = jnp.where(row < MAIN, (row >> 3) * CAP + (row & 7), (row - MAIN) * CAP + 8)
    perm = ones_where(col == slot)
    gate = dot(perm, gate_ref[0])
    up = dot(perm, up_ref[0])
    sig = 1.0 / (1.0 + jnp.exp(-gate))
    act = gate * sig
    fup_ref[0] = act
    fgate_ref[0] = up * sig * (1.0 + gate * (1.0 - sig))
    hidden_ref[0] = (act * up).astype(BF)


def prep(order, gate, up):
    spec_in = pl.BlockSpec((1, SLOTS, FF), lambda i, o: (o[i], 0, 0))
    spec_out = pl.BlockSpec((1, SLOTS, FF), lambda i, o: (i, 0, 0))
    return pl.pallas_call(
        prep_kernel,
        out_shape=(
            jax.ShapeDtypeStruct((2, SLOTS, FF), F32),
            jax.ShapeDtypeStruct((2, SLOTS, FF), F32),
            jax.ShapeDtypeStruct((2, SLOTS, FF), BF),
        ),
        grid_spec=pltpu.PrefetchScalarGridSpec(
            num_scalar_prefetch=1,
            grid=(2,),
            in_specs=[spec_in, spec_in],
            out_specs=[spec_out, spec_out, spec_out],
        ),
        compiler_params=pltpu.CompilerParams(vmem_limit_bytes=24 << 20),
        cost_estimate=pl.CostEstimate(flops=170_000_000, bytes_accessed=4_700_000, transcendentals=300_000),
        name="prep",
    )(order, gate, up)


def pre_kernel(t_ref, w_ref, cur_ref, out_ref):
    c = lax.broadcasted_iota(I32, (MAIN, TOK), 0)
    e9 = (c >> 3) * CAP
    t0 = t_ref[0:1, :]
    t1 = t_ref[1:2, :]
    w0 = w_ref[0:1, :]
    w1 = w_ref[1:2, :]

    def pick(slot):
        m0 = t0 == slot
        m1 = t1 == slot
        scale = jnp.sum(jnp.where(m0, w0, 0.0) + jnp.where(m1, w1, 0.0), axis=1, keepdims=True)
        return ones_where(jnp.logical_or(m0, m1)), scale

    main, scale_main = pick(e9 + (c & 7))
    last, scale_last = pick(e9 + 8)
    piece = lax.broadcasted_iota(I32, (MAIN, 128), 0) & 7
    for j in range(NCH):
        x = cur_ref[:, j * CH : (j + 1) * CH]
        out_ref[:, j * PCH : j * PCH + CH] = (dot(main, x) * scale_main).astype(BF)
        full = dot(last, x)
        part = jnp.zeros((MAIN, 128), F32)
        for k in range(PIECES):
            part = jnp.where(piece == k, full[:, k * 128 : (k + 1) * 128], part)
        out_ref[:, j * PCH + CH : (j + 1) * PCH] = (part * scale_last).astype(BF)


def pre(targets_t, weights_t, cur):
    return pl.pallas_call(
        pre_kernel,
        out_shape=jax.ShapeDtypeStruct((MAIN, NCH * PCH), BF),
        compiler_params=pltpu.CompilerParams(vmem_limit_bytes=16 << 20),
        cost_estimate=pl.CostEstimate(flops=120_000_000, bytes_accessed=1_600_000, transcendentals=0),
        name="pre",
    )(targets_t, weights_t, cur)


def post_kernel(t_ref, cur_ref, buf_ref, out_ref):
    c = lax.broadcasted_iota(I32, (TOK, MAIN), 1)
    e9 = (c >> 3) * CAP
    s = c & 7
    t0 = t_ref[:, 0:1]
    t1 = t_ref[:, 1:2]

    def pick(slot):
        return jnp.logical_or(t0 == slot, t1 == slot)

    main = ones_where(pick(e9 + s))
    last = pick(e9 + 8)
    tail = jnp.concatenate(
        [ones_where(jnp.logical_and(last, s == k)) for k in range(PIECES)], axis=0
    )
    for j in range(NCH):
        if len(buf_ref.shape) == 3:
            packed = buf_ref[j]
        else:
            packed = buf_ref[:, j * PCH : (j + 1) * PCH]
        acc = dot(main, packed[:, :CH])
        nin = dot(tail, packed[:, CH:])
        for k in range(PIECES):
            lo = j * CH + k * 128
            out_ref[:, lo : lo + 128] = (
                cur_ref[:, lo : lo + 128].astype(F32)
                + (acc[:, k * 128 : (k + 1) * 128] + nin[k * TOK : (k + 1) * TOK, :])
            ).astype(BF)


def post(targets, cur, buf):
    return pl.pallas_call(
        post_kernel,
        out_shape=jax.ShapeDtypeStruct((TOK, D), BF),
        compiler_params=pltpu.CompilerParams(vmem_limit_bytes=16 << 20),
        cost_estimate=pl.CostEstimate(flops=120_000_000, bytes_accessed=2_000_000, transcendentals=0),
        name="post",
    )(targets, cur, buf)


def unpack_rows(buf_ref, rows_ref):
    r = lax.broadcasted_iota(I32, (128, MAIN), 0)
    c = lax.broadcasted_iota(I32, (128, MAIN), 1)
    spread = ones_where(c == (r & 15) * 8 + (r >> 4))
    for j in range(NCH):
        rows_ref[0:MAIN, j * CH : (j + 1) * CH] = buf_ref[:, j * PCH : j * PCH + CH]
        nin = dot(spread, buf_ref[:, j * PCH + CH : (j + 1) * PCH]).astype(BF)
        for k in range(PIECES):
            lo = j * CH + k * 128
            rows_ref[MAIN:SLOTS, lo : lo + 128] = nin[k * 16 : (k + 1) * 16, :]


def pack_chunk(grads, out_ref):
    c = lax.broadcasted_iota(I32, (MAIN, 128), 0)
    r = lax.broadcasted_iota(I32, (MAIN, 128), 1)
    fold = ones_where(r == (c & 7) * 16 + (c >> 3))
    out_ref[:, 0:CH] = grads[0:MAIN]
    pieces = [grads[MAIN:SLOTS, k * 128 : (k + 1) * 128] for k in range(PIECES)]
    pieces.append(jnp.zeros((16, 128), BF))
    out_ref[:, CH:PCH] = dot(fold, jnp.concatenate(pieces, axis=0)).astype(BF)


def hidden_block(rows_ref, wd_ref, fup_ref, fgate_ref):
    d_hidden = dot(rows_ref[...], wd_ref[...], NT)
    return (d_hidden * fgate_ref[...]).astype(BF), (d_hidden * fup_ref[...]).astype(BF)


def grads_block(dg, du, wg_ref, wu_ref):
    total = None
    for q in range(4):
        cols = slice(q * 256, (q + 1) * 256)
        term = dot(dg[q], wg_ref[:, cols], NT) + dot(du[q], wu_ref[:, cols], NT)
        total = term if total is None else total + term
    return total.astype(BF)


def hidden_kernel(buf_ref, wd_ref, fup_ref, fgate_ref, rows_ref, dg_ref, du_ref):
    @pl.when(pl.program_id(0) == 0)
    def _():
        unpack_rows(buf_ref, rows_ref)

    dg_ref[0], du_ref[0] = hidden_block(rows_ref, wd_ref, fup_ref, fgate_ref)


def hidden_pass(buf, wd, fup, fgate):
    return pl.pallas_call(
        hidden_kernel,
        grid=(4,),
        in_specs=[
            pl.BlockSpec((MAIN, NCH * PCH), lambda i: (0, 0)),
            pl.BlockSpec((256, D), lambda i: (i, 0)),
            pl.BlockSpec((SLOTS, 256), lambda i: (0, i)),
            pl.BlockSpec((SLOTS, 256), lambda i: (0, i)),
        ],
        out_specs=[
            pl.BlockSpec((SLOTS, D), lambda i: (0, 0)),
            pl.BlockSpec((1, SLOTS, 256), lambda i: (i, 0, 0)),
            pl.BlockSpec((1, SLOTS, 256), lambda i: (i, 0, 0)),
        ],
        out_shape=(
            jax.ShapeDtypeStruct((SLOTS, D), BF),
            jax.ShapeDtypeStruct((4, SLOTS, 256), BF),
            jax.ShapeDtypeStruct((4, SLOTS, 256), BF),
        ),
        compiler_params=pltpu.CompilerParams(vmem_limit_bytes=24 << 20),
        cost_estimate=pl.CostEstimate(flops=1_060_000_000, bytes_accessed=11_000_000, transcendentals=0),
        name="hidden_pass",
    )(buf, wd, fup, fgate)


def grads_kernel(dg_ref, du_ref, wg_ref, wu_ref, out_ref):
    dg = [dg_ref[q] for q in range(4)]
    du = [du_ref[q] for q in range(4)]
    pack_chunk(grads_block(dg, du, wg_ref, wu_ref), out_ref)


def grads_pass(dg, du, wg, wu):
    return pl.pallas_call(
        grads_kernel,
        grid=(4,),
        in_specs=[
            pl.BlockSpec((4, SLOTS, 256), lambda i: (0, 0, 0)),
            pl.BlockSpec((4, SLOTS, 256), lambda i: (0, 0, 0)),
            pl.BlockSpec((CH, FF), lambda i: (i, 0)),
            pl.BlockSpec((CH, FF), lambda i: (i, 0)),
        ],
        out_specs=pl.BlockSpec((MAIN, PCH), lambda i: (0, i)),
        out_shape=jax.ShapeDtypeStruct((MAIN, NCH * PCH), BF),
        compiler_params=pltpu.CompilerParams(vmem_limit_bytes=28 << 20),
        cost_estimate=pl.CostEstimate(flops=2_120_000_000, bytes_accessed=17_000_000, transcendentals=0),
        name="grads_pass",
    )(dg, du, wg, wu)


def expert_kernel(
    buf_ref, wd_ref, fup_ref, fgate_ref, wg_ref, wu_ref, rows_ref, out_ref, dg_ref, du_ref
):
    i = pl.program_id(0)

    @pl.when(i == 0)
    def _():
        unpack_rows(buf_ref, rows_ref)

    @pl.when(i < 4)
    def _():
        dg_ref[i], du_ref[i] = hidden_block(rows_ref, wd_ref, fup_ref, fgate_ref)

    @pl.when(i >= 4)
    def _():
        dg = [dg_ref[q] for q in range(4)]
        du = [du_ref[q] for q in range(4)]
        pack_chunk(grads_block(dg, du, wg_ref, wu_ref), out_ref)


def expert_pass(buf, wd, fup, fgate, wg, wu):
    first = lambda i: jnp.minimum(i, 3)
    second = lambda i: jnp.maximum(i - 4, 0)
    return pl.pallas_call(
        expert_kernel,
        grid=(8,),
        in_specs=[
            pl.BlockSpec((MAIN, NCH * PCH), lambda i: (0, 0)),
            pl.BlockSpec((256, D), lambda i: (first(i), 0)),
            pl.BlockSpec((SLOTS, 256), lambda i: (0, first(i))),
            pl.BlockSpec((SLOTS, 256), lambda i: (0, first(i))),
            pl.BlockSpec((CH, FF), lambda i: (second(i), 0)),
            pl.BlockSpec((CH, FF), lambda i: (second(i), 0)),
        ],
        out_specs=[
            pl.BlockSpec((SLOTS, D), lambda i: (0, 0)),
            pl.BlockSpec((MAIN, PCH), lambda i: (0, second(i))),
        ],
        out_shape=(
            jax.ShapeDtypeStruct((SLOTS, D), BF),
            jax.ShapeDtypeStruct((MAIN, NCH * PCH), BF),
        ),
        scratch_shapes=[pltpu.VMEM((4, SLOTS, 256), BF), pltpu.VMEM((4, SLOTS, 256), BF)],
        compiler_params=pltpu.CompilerParams(vmem_limit_bytes=36 << 20),
        cost_estimate=pl.CostEstimate(flops=3_200_000_000, bytes_accessed=28_000_000, transcendentals=0),
        name="expert_pass",
    )(buf, wd, fup, fgate, wg, wu)


def exchange(buf):
    return lax.all_to_all(
        buf.reshape(EXP, 8, NCH * PCH), "expert", split_axis=0, concat_axis=0, tiled=True
    ).reshape(MAIN, NCH * PCH)


def slot_targets(routes):
    flat = routes.reshape(2, TOK * 2)
    n = TOK * 2
    row = lax.broadcasted_iota(I32, (n, n), 0)
    col = lax.broadcasted_iota(I32, (n, n), 1)
    same = jnp.logical_and(flat[:, :, None] == flat[:, None, :], (col < row)[None])
    return (flat * CAP + jnp.sum(same.astype(I32), axis=2)).reshape(2, TOK, 2)


def per_device(
    seed_grads, expert_routes, route_weights, saved_gate, saved_up, w_gate, w_up, w_down
):
    section = lax.axis_index("pipe")
    first_up = section < 2
    first = jnp.where(first_up, 1, 0).astype(I32)
    order = jnp.stack([first, 1 - first])

    def gather(x):
        return lax.all_gather(x, "dp", axis=0, tiled=True)

    wd_full = gather(w_down[0, 0])
    wg_in, wu_in = w_gate[0, 0], w_up[0, 0]
    wg_full = gather(wg_in)
    wu_full = gather(wu_in)

    def ordered(x):
        return jnp.where(first_up, x[1], x[0]), jnp.where(first_up, x[0], x[1])

    targets = slot_targets(expert_routes[:, 0])
    tgt = ordered(targets)
    wts = ordered(route_weights[:, 0])
    tgt_t = [t.T for t in tgt]
    wts_t = [w.T for w in wts]
    cur = jnp.where(first_up, seed_grads[1], seed_grads[0])
    fup, fgate, hidden = prep(order, saved_gate[:, 0, 0, 0], saved_up[:, 0, 0, 0])

    moves = [[(0, 1), (3, 2)], [(1, 2), (2, 1)], [(2, 3), (1, 0)]]
    results = []
    held_rows = []
    for step in range(4):
        at = step // 2
        buf = exchange(pre(tgt_t[at], wts_t[at], cur))
        if step == 0:
            rows, dg, du = hidden_pass(buf, wd_full, fup[at], fgate[at])
            packed = grads_pass(dg, du, wg_full, wu_full)
        else:
            rows, packed = expert_pass(buf, wd_full, fup[at], fgate[at], wg_full, wu_full)
        held_rows.append(rows)
        result = post(tgt[at], cur, exchange(packed))
        results.append(result)
        if step < 3:
            cur = lax.ppermute(result, "pipe", moves[step])

    edge = jnp.logical_or(section == 0, section == 3)
    res_first = jnp.where(edge, results[0], results[1])
    res_second = jnp.where(edge, results[3], results[2])
    input_grads = jnp.where(
        first_up, jnp.stack([res_second, res_first]), jnp.stack([res_first, res_second])
    )[:, None]

    mine = lax.axis_index("dp") * 256
    hidden_all = lax.all_gather(hidden, "dp", axis=0)
    hidden_mine = lax.dynamic_slice_in_dim(hidden_all, mine, 256, axis=3)
    rows_first = jnp.where(edge, held_rows[0], held_rows[1])
    rows_second = jnp.where(edge, held_rows[3], held_rows[2])
    contract = (((0,), (0,)), ((), ()))
    total = dot(hidden_mine[:, 0].reshape(4 * SLOTS, 256), gather(rows_first), contract)
    total = total + dot(hidden_mine[:, 1].reshape(4 * SLOTS, 256), gather(rows_second), contract)
    return input_grads, total.astype(BF)[None, None]


def solution(mesh):
    return jax.shard_map(
        per_device,
        mesh=mesh,
        in_specs=(
            P(None, ("expert", "dp"), None),
            P(None, "pipe", ("expert", "dp"), None),
            P(None, "pipe", ("expert", "dp"), None),
            P(None, "pipe", "dp", "expert", None, None),
            P(None, "pipe", "dp", "expert", None, None),
            P("pipe", "expert", "dp", None),
            P("pipe", "expert", "dp", None),
            P("pipe", "expert", "dp", None),
        ),
        out_specs=(P(None, "pipe", ("expert", "dp"), None), P("pipe", "expert", "dp", None)),
        check_vma=False,
    )
```

```python
import functools
import jax
import jax.numpy as jnp
from jax import lax
from jax.experimental import pallas as pl
from jax.experimental.pallas import tpu as pltpu
from jax.sharding import PartitionSpec as P

BF = jnp.bfloat16
F32 = jnp.float32
I32 = jnp.int32
D = 3584
FF = 1024
TOK = 64
EXP = 16
CAP = 9
SLOTS = 144
MAIN = 128
CH = 896
PCH = 1024
NCH = 4
PIECES = 7
NT = (((1,), (1,)), ((), ()))
NN = (((1,), (0,)), ((), ()))


def dot(a, b, dims=NN):
    return lax.dot_general(a, b, dims, preferred_element_type=F32)


def ones_where(mask):
    return jnp.where(mask, 1.0, 0.0).astype(BF)


def prep_kernel(order_ref, gate_ref, up_ref, fup_ref, fgate_ref, hidden_ref):
    row = lax.broadcasted_iota(I32, (SLOTS, SLOTS), 0)
    col = lax.broadcasted_iota(I32, (SLOTS, SLOTS), 1)
    slot = jnp.where(row < MAIN, (row >> 3) * CAP + (row & 7), (row - MAIN) * CAP + 8)
    perm = ones_where(col == slot)
    gate = dot(perm, gate_ref[0])
    up = dot(perm, up_ref[0])
    sig = 1.0 / (1.0 + jnp.exp(-gate))
    act = gate * sig
    fup_ref[0] = act
    fgate_ref[0] = up * sig * (1.0 + gate * (1.0 - sig))
    hidden_ref[0] = (act * up).astype(BF)


def prep(order, gate, up):
    spec_in = pl.BlockSpec((1, SLOTS, FF), lambda i, o: (o[i], 0, 0))
    spec_out = pl.BlockSpec((1, SLOTS, FF), lambda i, o: (i, 0, 0))
    return pl.pallas_call(
        prep_kernel,
        out_shape=(
            jax.ShapeDtypeStruct((2, SLOTS, FF), F32),
            jax.ShapeDtypeStruct((2, SLOTS, FF), F32),
            jax.ShapeDtypeStruct((2, SLOTS, FF), BF),
        ),
        grid_spec=pltpu.PrefetchScalarGridSpec(
            num_scalar_prefetch=1,
            grid=(2,),
            in_specs=[spec_in, spec_in],
            out_specs=[spec_out, spec_out, spec_out],
        ),
        compiler_params=pltpu.CompilerParams(vmem_limit_bytes=24 << 20),
        cost_estimate=pl.CostEstimate(flops=170_000_000, bytes_accessed=4_700_000, transcendentals=300_000),
        name="prep",
    )(order, gate, up)


def pre_kernel(t_ref, w_ref, cur_ref, out_ref):
    c = lax.broadcasted_iota(I32, (MAIN, TOK), 0)
    e9 = (c >> 3) * CAP
    t0 = t_ref[0:1, :]
    t1 = t_ref[1:2, :]
    w0 = w_ref[0:1, :]
    w1 = w_ref[1:2, :]

    def pick(slot):
        m0 = t0 == slot
        m1 = t1 == slot
        scale = jnp.sum(jnp.where(m0, w0, 0.0) + jnp.where(m1, w1, 0.0), axis=1, keepdims=True)
        return ones_where(jnp.logical_or(m0, m1)), scale

    main, scale_main = pick(e9 + (c & 7))
    last, scale_last = pick(e9 + 8)
    piece = lax.broadcasted_iota(I32, (MAIN, 128), 0) & 7
    for j in range(NCH):
        x = cur_ref[:, j * CH : (j + 1) * CH]
        out_ref[:, j * PCH : j * PCH + CH] = (dot(main, x) * scale_main).astype(BF)
        full = dot(last, x)
        part = jnp.zeros((MAIN, 128), F32)
        for k in range(PIECES):
            part = jnp.where(piece == k, full[:, k * 128 : (k + 1) * 128], part)
        out_ref[:, j * PCH + CH : (j + 1) * PCH] = (part * scale_last).astype(BF)


def pre(targets_t, weights_t, cur):
    return pl.pallas_call(
        pre_kernel,
        out_shape=jax.ShapeDtypeStruct((MAIN, NCH * PCH), BF),
        compiler_params=pltpu.CompilerParams(vmem_limit_bytes=16 << 20),
        cost_estimate=pl.CostEstimate(flops=120_000_000, bytes_accessed=1_600_000, transcendentals=0),
        name="pre",
    )(targets_t, weights_t, cur)


def post_kernel(t_ref, cur_ref, buf_ref, out_ref):
    c = lax.broadcasted_iota(I32, (TOK, MAIN), 1)
    e9 = (c >> 3) * CAP
    s = c & 7
    t0 = t_ref[:, 0:1]
    t1 = t_ref[:, 1:2]

    def pick(slot):
        return jnp.logical_or(t0 == slot, t1 == slot)

    main = ones_where(pick(e9 + s))
    last = pick(e9 + 8)
    tail = jnp.concatenate(
        [ones_where(jnp.logical_and(last, s == k)) for k in range(PIECES)], axis=0
    )
    for j in range(NCH):
        if len(buf_ref.shape) == 3:
            packed = buf_ref[j]
        else:
            packed = buf_ref[:, j * PCH : (j + 1) * PCH]
        acc = dot(main, packed[:, :CH])
        nin = dot(tail, packed[:, CH:])
        for k in range(PIECES):
            lo = j * CH + k * 128
            out_ref[:, lo : lo + 128] = (
                cur_ref[:, lo : lo + 128].astype(F32)
                + (acc[:, k * 128 : (k + 1) * 128] + nin[k * TOK : (k + 1) * TOK, :])
            ).astype(BF)


def post(targets, cur, buf):
    return pl.pallas_call(
        post_kernel,
        out_shape=jax.ShapeDtypeStruct((TOK, D), BF),
        compiler_params=pltpu.CompilerParams(vmem_limit_bytes=16 << 20),
        cost_estimate=pl.CostEstimate(flops=120_000_000, bytes_accessed=2_000_000, transcendentals=0),
        name="post",
    )(targets, cur, buf)


def unpack_rows(buf_ref, rows_ref):
    r = lax.broadcasted_iota(I32, (128, MAIN), 0)
    c = lax.broadcasted_iota(I32, (128, MAIN), 1)
    spread = ones_where(c == (r & 15) * 8 + (r >> 4))
    for j in range(NCH):
        rows_ref[0:MAIN, j * CH : (j + 1) * CH] = buf_ref[:, j * PCH : j * PCH + CH]
        nin = dot(spread, buf_ref[:, j * PCH + CH : (j + 1) * PCH]).astype(BF)
        for k in range(PIECES):
            lo = j * CH + k * 128
            rows_ref[MAIN:SLOTS, lo : lo + 128] = nin[k * 16 : (k + 1) * 16, :]


def put_chunk(grads, out_ref, lead, base):
    c = lax.broadcasted_iota(I32, (MAIN, 128), 0)
    r = lax.broadcasted_iota(I32, (MAIN, 128), 1)
    fold = ones_where(r == (c & 7) * 16 + (c >> 3))
    pieces = [grads[MAIN:SLOTS, k * 128 : (k + 1) * 128] for k in range(PIECES)]
    pieces.append(jnp.zeros((16, 128), BF))
    tail = dot(fold, jnp.concatenate(pieces, axis=0)).astype(BF)
    if lead is None:
        out_ref[:, pl.ds(base, CH)] = grads[0:MAIN]
        out_ref[:, pl.ds(base + CH, 128)] = tail
    else:
        out_ref[lead, :, 0:CH] = grads[0:MAIN]
        out_ref[lead, :, CH:PCH] = tail


def hidden_part(rows_ref, wd, fup_ref, fgate_ref, lo, width):
    d_hidden = dot(rows_ref[...], wd, NT)
    cols = pl.ds(lo, width)
    return (d_hidden * fgate_ref[:, cols]).astype(BF), (d_hidden * fup_ref[:, cols]).astype(BF)


def shard_plan(shard):
    half = shard // 2
    return [(0, 0, shard), (3, 0, shard), (1, 0, shard), (2, 0, half), (2, half, half)]


def fetch(src, dst, sem):
    copy = pltpu.make_async_copy(src, dst, sem)
    copy.start()
    return copy


def fetch_shards(srcs, dst_ref, plan, sems):
    out = []
    at = 0
    for n, (_, _, width) in enumerate(plan):
        out.append((fetch(srcs[n], dst_ref.at[pl.ds(at, width)], sems.at[n]), at))
        at += width
    return out


def hidden_kernel(at_dir, me_ref, buf_hbm, fup_hbm, fgate_hbm, *rest):
    wd_refs, rest = rest[:5], rest[5:]
    rows_hbm, dgu_ref, buf_ref, rows_ref, wd_ref, fup_ref, fgate_ref, sems, f_sems = rest
    plan = shard_plan(256)
    buf_copy = fetch(buf_hbm, buf_ref, f_sems.at[2])
    f_copies = [
        fetch(fup_hbm.at[at_dir], fup_ref, f_sems.at[0]),
        fetch(fgate_hbm.at[at_dir], fgate_ref, f_sems.at[1]),
    ]
    copies = fetch_shards(wd_refs, wd_ref, plan, sems)
    buf_copy.wait()
    unpack_rows(buf_ref, rows_ref)
    rows_copy = fetch(rows_ref, rows_hbm, f_sems.at[3])
    for copy in f_copies:
        copy.wait()
    for n, (shift, row, width) in enumerate(plan):
        copy, at = copies[n]
        copy.wait()
        lo = pl.multiple_of(((me_ref[0] + shift) & 3) * 256 + row, 128)
        dg, du = hidden_part(rows_ref, wd_ref[at : at + width], fup_ref, fgate_ref, lo, width)
        dgu_ref[0, :, pl.ds(lo, width)] = dg
        dgu_ref[1, :, pl.ds(lo, width)] = du
    rows_copy.wait()


IN_HBM = pl.BlockSpec(memory_space=pl.ANY)
IN_SMEM = pl.BlockSpec(memory_space=pltpu.SMEM)
IN_VMEM = pl.BlockSpec(memory_space=pltpu.VMEM)


def hidden_pass(at_dir, me, buf, fup, fgate, wd):
    return pl.pallas_call(
        functools.partial(hidden_kernel, at_dir),
        in_specs=[IN_SMEM] + [IN_HBM] * 8,
        out_specs=[IN_HBM, IN_VMEM],
        out_shape=(
            jax.ShapeDtypeStruct((SLOTS, D), BF),
            jax.ShapeDtypeStruct((2, SLOTS, FF), BF),
        ),
        scratch_shapes=[
            pltpu.VMEM((MAIN, NCH * PCH), BF),
            pltpu.VMEM((SLOTS, D), BF),
            pltpu.VMEM((FF, D), BF),
            pltpu.VMEM((SLOTS, FF), F32),
            pltpu.VMEM((SLOTS, FF), F32),
            pltpu.SemaphoreType.DMA((5,)),
            pltpu.SemaphoreType.DMA((4,)),
        ],
        compiler_params=pltpu.CompilerParams(vmem_limit_bytes=60 << 20),
        cost_estimate=pl.CostEstimate(flops=1_060_000_000, bytes_accessed=11_000_000, transcendentals=0),
        name="hidden_pass",
    )(me, buf, fup, fgate, *wd)


def own_grads_kernel(me_ref, own, left, right, far_g, far_u, wg_hbm, wu_hbm, out_ref, d_ref, wg_ref, wu_ref, sems):
    weights = [fetch(wg_hbm, wg_ref, sems.at[0]), fetch(wu_hbm, wu_ref, sems.at[1])]
    copies = [
        [fetch(own, d_ref.at[0], sems.at[2])],
        [fetch(left, d_ref.at[1], sems.at[3])],
        [fetch(right, d_ref.at[2], sems.at[4])],
        [
            fetch(far_g, d_ref.at[3, pl.ds(0, 1)], sems.at[5]),
            fetch(far_u, d_ref.at[3, pl.ds(1, 1)], sems.at[6]),
        ],
    ]
    for copy in weights:
        copy.wait()
    for n, shift in enumerate((0, 3, 1, 2)):
        for copy in copies[n]:
            copy.wait()
        total = dot(d_ref[n, 0], wg_ref[...], NT) + dot(d_ref[n, 1], wu_ref[...], NT)
        put_chunk(total.astype(BF), out_ref, (me_ref[0] + shift) & 3, None)


def own_grads(me, own, left, right, far_g, far_u, wg, wu):
    return pl.pallas_call(
        own_grads_kernel,
        in_specs=[IN_SMEM] + [IN_HBM] * 7,
        out_specs=IN_VMEM,
        out_shape=jax.ShapeDtypeStruct((4, MAIN, PCH), BF),
        scratch_shapes=[
            pltpu.VMEM((4, 2, SLOTS, FF), BF),
            pltpu.VMEM((CH, FF), BF),
            pltpu.VMEM((CH, FF), BF),
            pltpu.SemaphoreType.DMA((7,)),
        ],
        compiler_params=pltpu.CompilerParams(vmem_limit_bytes=60 << 20),
        cost_estimate=pl.CostEstimate(flops=2_120_000_000, bytes_accessed=8_000_000, transcendentals=0),
        name="own_grads",
    )(me, own, left, right, far_g, far_u, wg, wu)


def expert_kernel(at_dir, whole, me_ref, buf_hbm, fup_hbm, fgate_hbm, *rest):
    wd_refs = rest[:5]
    me = me_ref[0]
    if whole:
        wg_full, wu_full = rest[5:7]
        rest = rest[7:]
        gplan = [(k, 0, CH) for k in range(4)]
        g_src = [wg_full.at[pl.ds(k * CH, CH)] for k in range(4)]
        u_src = [wu_full.at[pl.ds(k * CH, CH)] for k in range(4)]
    else:
        g_src, wu_full = rest[5:10], rest[10]
        rest = rest[11:]
        gplan = shard_plan(CH)
        u_src = [
            wu_full.at[pl.ds(pl.multiple_of(((me + shift) & 3) * CH + row, 64), width)]
            for shift, row, width in gplan
        ]
    (
        rows_hbm, out_ref, buf_ref, rows_ref, wd_ref, wg_ref, wu_ref, fup_ref, fgate_ref, dg_ref, du_ref,
        f_sems, d_sems, g_sems, u_sems,
    ) = rest
    plan = shard_plan(256)
    buf_copy = fetch(buf_hbm, buf_ref, f_sems.at[2])
    f_copies = [
        fetch(fup_hbm.at[at_dir], fup_ref, f_sems.at[0]),
        fetch(fgate_hbm.at[at_dir], fgate_ref, f_sems.at[1]),
    ]
    d_copies = fetch_shards(wd_refs, wd_ref, plan, d_sems)
    g_copies = fetch_shards(g_src, wg_ref, gplan, g_sems)
    u_copies = fetch_shards(u_src, wu_ref, gplan, u_sems)
    buf_copy.wait()
    unpack_rows(buf_ref, rows_ref)
    rows_copy = fetch(rows_ref, rows_hbm, f_sems.at[3])
    for copy in f_copies:
        copy.wait()
    for n, (shift, row, width) in enumerate(plan):
        copy, at = d_copies[n]
        copy.wait()
        lo = pl.multiple_of(((me + shift) & 3) * 256 + row, 128)
        dg, du = hidden_part(rows_ref, wd_ref[at : at + width], fup_ref, fgate_ref, lo, width)
        dg_ref[:, pl.ds(lo, width)] = dg
        du_ref[:, pl.ds(lo, width)] = du
    for n in range(4):
        shift = gplan[n][0]
        last = (n, 4) if n == 3 and not whole else (n,)
        for m in last:
            g_copies[m][0].wait()
            u_copies[m][0].wait()
        at = g_copies[n][1]
        total = dot(dg_ref[...], wg_ref[at : at + CH], NT) + dot(du_ref[...], wu_ref[at : at + CH], NT)
        base = shift * PCH if whole else pl.multiple_of(((me + shift) & 3) * PCH, 128)
        put_chunk(total.astype(BF), out_ref, None, base)
    rows_copy.wait()


def expert_pass(at_dir, me, buf, fup, fgate, wd, wg, wu):
    whole = len(wg) == 1
    return pl.pallas_call(
        functools.partial(expert_kernel, at_dir, whole),
        in_specs=[IN_SMEM] + [IN_HBM] * (9 + len(wg)),
        out_specs=[IN_HBM, IN_VMEM],
        out_shape=(
            jax.ShapeDtypeStruct((SLOTS, D), BF),
            jax.ShapeDtypeStruct((MAIN, NCH * PCH), BF),
        ),
        scratch_shapes=[
            pltpu.VMEM((MAIN, NCH * PCH), BF),
            pltpu.VMEM((SLOTS, D), BF),
            pltpu.VMEM((FF, D), BF),
            pltpu.VMEM((D, FF), BF),
            pltpu.VMEM((D, FF), BF),
            pltpu.VMEM((SLOTS, FF), F32),
            pltpu.VMEM((SLOTS, FF), F32),
            pltpu.VMEM((SLOTS, FF), BF),
            pltpu.VMEM((SLOTS, FF), BF),
            pltpu.SemaphoreType.DMA((4,)),
            pltpu.SemaphoreType.DMA((5,)),
            pltpu.SemaphoreType.DMA((5,)),
            pltpu.SemaphoreType.DMA((5,)),
        ],
        compiler_params=pltpu.CompilerParams(vmem_limit_bytes=60 << 20),
        cost_estimate=pl.CostEstimate(flops=3_200_000_000, bytes_accessed=28_000_000, transcendentals=0),
        name="expert_pass",
    )(me, buf, fup, fgate, *wd, *wg, wu)


def exchange(buf):
    return lax.all_to_all(
        buf.reshape(EXP, 8, NCH * PCH), "expert", split_axis=0, concat_axis=0, tiled=True
    ).reshape(MAIN, NCH * PCH)


def slot_targets(routes):
    flat = routes.reshape(2, TOK * 2)
    n = TOK * 2
    row = lax.broadcasted_iota(I32, (n, n), 0)
    col = lax.broadcasted_iota(I32, (n, n), 1)
    same = jnp.logical_and(flat[:, :, None] == flat[:, None, :], (col < row)[None])
    return (flat * CAP + jnp.sum(same.astype(I32), axis=2)).reshape(2, TOK, 2)


def shift_dp(value, step, sections):
    pairs = [(s * 4 + i, s * 4 + (i + step) % 4) for s in sections for i in range(4)]
    return lax.ppermute(value, ("pipe", "dp"), pairs)


def tie(value, *others):
    return lax.optimization_barrier((value,) + others)[0]


def per_device(
    seed_grads, expert_routes, route_weights, saved_gate, saved_up, w_gate, w_up, w_down
):
    section = lax.axis_index("pipe")
    dp = lax.axis_index("dp").astype(I32)
    me = dp.reshape(1)
    first_up = section < 2
    first = jnp.where(first_up, 1, 0).astype(I32)
    order = jnp.stack([first, 1 - first])
    every, outer, inner = (0, 1, 2, 3), (0, 3), (1, 2)

    def gather(x):
        return lax.all_gather(x, "dp", axis=0, tiled=True)

    def near(x, sections):
        return shift_dp(x, 1, sections), shift_dp(x, -1, sections)

    def far(left, right, sections):
        half = left.shape[0] // 2
        return shift_dp(left[:half], 1, sections), shift_dp(right[half:], -1, sections)

    wd_own, wg_own, wu_own = w_down[0, 0], w_gate[0, 0], w_up[0, 0]
    wd_near = near(wd_own, every)
    wg_near = near(tie(wg_own, *wd_near), inner)

    def ordered(x):
        return jnp.where(first_up, x[1], x[0]), jnp.where(first_up, x[0], x[1])

    targets = slot_targets(expert_routes[:, 0])
    tgt = ordered(targets)
    wts = ordered(route_weights[:, 0])
    tgt_t = [t.T for t in tgt]
    wts_t = [w.T for w in wts]
    cur = jnp.where(first_up, seed_grads[1], seed_grads[0])
    fup, fgate, hidden = prep(order, saved_gate[:, 0, 0, 0], saved_up[:, 0, 0, 0])

    moves = [[(0, 1), (3, 2)], [(1, 2), (2, 1)], [(2, 3), (1, 0)]]
    results = []
    held_rows = []
    wg = None
    for step in range(4):
        at = step // 2
        outgoing = pre(tgt_t[at], wts_t[at], cur)
        if step == 1:
            outgoing = tie(outgoing, *wg)
        buf = exchange(outgoing)
        if step == 0:
            wd = (wd_own,) + wd_near + far(*[tie(w, buf) for w in wd_near], every)
            rows, dgu = hidden_pass(at, me, buf, fup, fgate, wd)
            dgu_near = near(tie(dgu, *wg_near), outer)
            dgu_far = far(*dgu_near, outer)
            sent = own_grads(
                me, dgu, *dgu_near, *dgu_far, wg_own, wu_own
            )
            wu_full = gather(tie(wu_own, sent))
            wg = (wg_own,) + wg_near + far(*[tie(w, sent) for w in wg_near], inner)
            home = lax.all_to_all(
                sent.reshape(4 * EXP, 8, PCH), ("dp", "expert"), split_axis=0, concat_axis=0, tiled=True
            ).reshape(4, MAIN, PCH)
            result = post(tgt[at], cur, home)
        else:
            if step == 1:
                hidden_all = lax.all_gather(tie(hidden, buf), "dp", axis=0)
                wg_full = (gather(tie(wg_own, buf)),)
            if step == 3:
                wg = wg_full
            rows, packed = expert_pass(at, me, buf, fup, fgate, wd, wg, wu_full)
            result = post(tgt[at], cur, exchange(packed))
        held_rows.append(rows)
        results.append(result)
        if step < 3:
            cur = lax.ppermute(result, "pipe", moves[step])

    edge = jnp.logical_or(section == 0, section == 3)
    res_first = jnp.where(edge, results[0], results[1])
    res_second = jnp.where(edge, results[3], results[2])
    input_grads = jnp.where(
        first_up, jnp.stack([res_second, res_first]), jnp.stack([res_first, res_second])
    )[:, None]

    hidden_mine = lax.dynamic_slice_in_dim(hidden_all, dp * 256, 256, axis=3)
    rows_first = jnp.where(edge, held_rows[0], held_rows[1])
    rows_second = jnp.where(edge, held_rows[3], held_rows[2])
    contract = (((0,), (0,)), ((), ()))
    total = dot(hidden_mine[:, 0].reshape(4 * SLOTS, 256), gather(rows_first), contract)
    total = total + dot(hidden_mine[:, 1].reshape(4 * SLOTS, 256), gather(rows_second), contract)
    return input_grads, total.astype(BF)[None, None]


def solution(mesh):
    return jax.shard_map(
        per_device,
        mesh=mesh,
        in_specs=(
            P(None, ("expert", "dp"), None),
            P(None, "pipe", ("expert", "dp"), None),
            P(None, "pipe", ("expert", "dp"), None),
            P(None, "pipe", "dp", "expert", None, None),
            P(None, "pipe", "dp", "expert", None, None),
            P("pipe", "expert", "dp", None),
            P("pipe", "expert", "dp", None),
            P("pipe", "expert", "dp", None),
        ),
        out_specs=(P(None, "pipe", ("expert", "dp"), None), P("pipe", "expert", "dp", None)),
        check_vma=False,
    )
```

```python
import functools
import jax
import jax.numpy as jnp
from jax import lax
from jax.experimental import pallas as pl
from jax.experimental.pallas import tpu as pltpu
from jax.sharding import PartitionSpec as P

BF = jnp.bfloat16
F32 = jnp.float32
I32 = jnp.int32
D = 3584
FF = 1024
TOK = 64
EXP = 16
CAP = 9
SLOTS = 144
MAIN = 128
CH = 896
PCH = 1024
NCH = 4
PIECES = 7
NT = (((1,), (1,)), ((), ()))
NN = (((1,), (0,)), ((), ()))


def dot(a, b, dims=NN):
    return lax.dot_general(a, b, dims, preferred_element_type=F32)


def ones_where(mask):
    return jnp.where(mask, 1.0, 0.0).astype(BF)


def prep_kernel(order_ref, gate_ref, up_ref, fup_ref, fgate_ref, hidden_ref):
    row = lax.broadcasted_iota(I32, (SLOTS, SLOTS), 0)
    col = lax.broadcasted_iota(I32, (SLOTS, SLOTS), 1)
    slot = jnp.where(row < MAIN, (row >> 3) * CAP + (row & 7), (row - MAIN) * CAP + 8)
    perm = ones_where(col == slot)
    gate = dot(perm, gate_ref[0])
    up = dot(perm, up_ref[0])
    sig = 1.0 / (1.0 + jnp.exp(-gate))
    act = gate * sig
    fup_ref[0] = act
    fgate_ref[0] = up * sig * (1.0 + gate * (1.0 - sig))
    hidden_ref[0] = (act * up).astype(BF)


def prep(order, gate, up):
    spec_in = pl.BlockSpec((1, SLOTS, FF), lambda i, o: (o[i], 0, 0))
    spec_out = pl.BlockSpec((1, SLOTS, FF), lambda i, o: (i, 0, 0))
    return pl.pallas_call(
        prep_kernel,
        out_shape=(
            jax.ShapeDtypeStruct((2, SLOTS, FF), F32),
            jax.ShapeDtypeStruct((2, SLOTS, FF), F32),
            jax.ShapeDtypeStruct((2, SLOTS, FF), BF),
        ),
        grid_spec=pltpu.PrefetchScalarGridSpec(
            num_scalar_prefetch=1,
            grid=(2,),
            in_specs=[spec_in, spec_in],
            out_specs=[spec_out, spec_out, spec_out],
        ),
        compiler_params=pltpu.CompilerParams(vmem_limit_bytes=24 << 20),
        cost_estimate=pl.CostEstimate(flops=170_000_000, bytes_accessed=4_700_000, transcendentals=300_000),
        name="prep",
    )(order, gate, up)


def pre_kernel(t_ref, w_ref, cur_ref, out_ref):
    c = lax.broadcasted_iota(I32, (MAIN, TOK), 0)
    e9 = (c >> 3) * CAP
    t0 = t_ref[0:1, :]
    t1 = t_ref[1:2, :]
    w0 = w_ref[0:1, :]
    w1 = w_ref[1:2, :]

    def pick(slot):
        m0 = t0 == slot
        m1 = t1 == slot
        scale = jnp.sum(jnp.where(m0, w0, 0.0) + jnp.where(m1, w1, 0.0), axis=1, keepdims=True)
        return ones_where(jnp.logical_or(m0, m1)), scale

    main, scale_main = pick(e9 + (c & 7))
    last, scale_last = pick(e9 + 8)
    piece = lax.broadcasted_iota(I32, (MAIN, 128), 0) & 7
    for j in range(NCH):
        x = cur_ref[:, j * CH : (j + 1) * CH]
        out_ref[:, j * PCH : j * PCH + CH] = (dot(main, x) * scale_main).astype(BF)
        full = dot(last, x)
        part = jnp.zeros((MAIN, 128), F32)
        for k in range(PIECES):
            part = jnp.where(piece == k, full[:, k * 128 : (k + 1) * 128], part)
        out_ref[:, j * PCH + CH : (j + 1) * PCH] = (part * scale_last).astype(BF)


def pre(targets_t, weights_t, cur):
    return pl.pallas_call(
        pre_kernel,
        out_shape=jax.ShapeDtypeStruct((MAIN, NCH * PCH), BF),
        compiler_params=pltpu.CompilerParams(vmem_limit_bytes=16 << 20),
        cost_estimate=pl.CostEstimate(flops=120_000_000, bytes_accessed=1_600_000, transcendentals=0),
        name="pre",
    )(targets_t, weights_t, cur)


def post_kernel(t_ref, cur_ref, buf_ref, out_ref):
    c = lax.broadcasted_iota(I32, (TOK, MAIN), 1)
    e9 = (c >> 3) * CAP
    s = c & 7
    t0 = t_ref[:, 0:1]
    t1 = t_ref[:, 1:2]

    def pick(slot):
        return jnp.logical_or(t0 == slot, t1 == slot)

    main = ones_where(pick(e9 + s))
    last = pick(e9 + 8)
    tail = jnp.concatenate(
        [ones_where(jnp.logical_and(last, s == k)) for k in range(PIECES)], axis=0
    )
    for j in range(NCH):
        if len(buf_ref.shape) == 3:
            packed = buf_ref[j]
        else:
            packed = buf_ref[:, j * PCH : (j + 1) * PCH]
        acc = dot(main, packed[:, :CH])
        nin = dot(tail, packed[:, CH:])
        for k in range(PIECES):
            lo = j * CH + k * 128
            out_ref[:, lo : lo + 128] = (
                cur_ref[:, lo : lo + 128].astype(F32)
                + (acc[:, k * 128 : (k + 1) * 128] + nin[k * TOK : (k + 1) * TOK, :])
            ).astype(BF)


def post(targets, cur, buf):
    return pl.pallas_call(
        post_kernel,
        out_shape=jax.ShapeDtypeStruct((TOK, D), BF),
        compiler_params=pltpu.CompilerParams(vmem_limit_bytes=16 << 20),
        cost_estimate=pl.CostEstimate(flops=120_000_000, bytes_accessed=2_000_000, transcendentals=0),
        name="post",
    )(targets, cur, buf)


def unpack_rows(buf_ref, rows_ref):
    r = lax.broadcasted_iota(I32, (128, MAIN), 0)
    c = lax.broadcasted_iota(I32, (128, MAIN), 1)
    spread = ones_where(c == (r & 15) * 8 + (r >> 4))
    for j in range(NCH):
        rows_ref[0:MAIN, j * CH : (j + 1) * CH] = buf_ref[:, j * PCH : j * PCH + CH]
        nin = dot(spread, buf_ref[:, j * PCH + CH : (j + 1) * PCH]).astype(BF)
        for k in range(PIECES):
            lo = j * CH + k * 128
            rows_ref[MAIN:SLOTS, lo : lo + 128] = nin[k * 16 : (k + 1) * 16, :]


def put_chunk(grads, out_ref, lead, base):
    c = lax.broadcasted_iota(I32, (MAIN, 128), 0)
    r = lax.broadcasted_iota(I32, (MAIN, 128), 1)
    fold = ones_where(r == (c & 7) * 16 + (c >> 3))
    pieces = [grads[MAIN:SLOTS, k * 128 : (k + 1) * 128] for k in range(PIECES)]
    pieces.append(jnp.zeros((16, 128), BF))
    tail = dot(fold, jnp.concatenate(pieces, axis=0)).astype(BF)
    if lead is None:
        out_ref[:, pl.ds(base, CH)] = grads[0:MAIN]
        out_ref[:, pl.ds(base + CH, 128)] = tail
    else:
        out_ref[lead, :, 0:CH] = grads[0:MAIN]
        out_ref[lead, :, CH:PCH] = tail


def hidden_part(rows_ref, wd, fup_ref, fgate_ref, lo, width):
    d_hidden = dot(rows_ref[...], wd, NT)
    cols = pl.ds(lo, width)
    return (d_hidden * fgate_ref[:, cols]).astype(BF), (d_hidden * fup_ref[:, cols]).astype(BF)


def halves_plan(shard):
    half = shard // 2
    pieces = [(0, 0, shard)]
    groups = [(0, [0])]
    for shift, parts in ((3, False), (1, False), (2, True)):
        mine = []
        for row, width in ((0, half), (half, half)) if parts else ((0, shard),):
            mine.append(len(pieces))
            pieces.append((shift, row, width))
        groups.append((shift, mine))
    return pieces, groups


class Stream:
    def __init__(self, sems, ahead):
        self.sems, self.ahead, self.todo, self.flying, self.done = sems, ahead, [], [], 0

    def add(self, src, dst):
        self.todo.append((src, dst))
        return len(self.todo) - 1

    def start(self, upto):
        while len(self.flying) < min(upto, len(self.todo)):
            n = len(self.flying)
            copy = pltpu.make_async_copy(*self.todo[n], self.sems.at[n])
            copy.start()
            self.flying.append(copy)

    def wait(self, n):
        self.start(n + 1 + self.ahead)
        while self.done <= n:
            self.flying[self.done].wait()
            self.done += 1


def hidden_stage(stream, groups, ids, me, rows_ref, wd_ref, fup_ref, fgate_ref, store):
    for n, (shift, members) in enumerate(groups):
        for m in members:
            stream.wait(ids[m])
        lo = pl.multiple_of(((me + shift) & 3) * 256, 128)
        dg, du = hidden_part(rows_ref, wd_ref[n * 256 : (n + 1) * 256], fup_ref, fgate_ref, lo, 256)
        store(lo, dg, du)


IN_HBM = pl.BlockSpec(memory_space=pl.ANY)
IN_SMEM = pl.BlockSpec(memory_space=pltpu.SMEM)
IN_VMEM = pl.BlockSpec(memory_space=pltpu.VMEM)


def add_shards(stream, srcs, pieces, dst_ref):
    at = 0
    ids = []
    for src, (_, _, width) in zip(srcs, pieces):
        ids.append(stream.add(src, dst_ref.at[pl.ds(at, width)]))
        at += width
    return ids


def hidden_kernel(at_dir, me_ref, buf_hbm, fup_hbm, fgate_hbm, *rest):
    pieces, groups = halves_plan(256)
    wd_refs, rest = rest[: len(pieces)], rest[len(pieces) :]
    dgu_ref, buf_ref, rows_ref, wd_ref, fup_ref, fgate_ref, sems = rest
    stream = Stream(sems, 4)
    first = stream.add(buf_hbm, buf_ref)
    ids = add_shards(stream, wd_refs[:1], pieces[:1], wd_ref)
    stream.add(fup_hbm.at[at_dir], fup_ref)
    act = stream.add(fgate_hbm.at[at_dir], fgate_ref)
    ids += add_shards(stream, wd_refs[1:], pieces[1:], wd_ref.at[pl.ds(256, FF - 256)])
    stream.wait(first)
    unpack_rows(buf_ref, rows_ref)
    stream.wait(act)

    def store(lo, dg, du):
        dgu_ref[0, :, pl.ds(lo, 256)] = dg
        dgu_ref[1, :, pl.ds(lo, 256)] = du

    hidden_stage(stream, groups, ids, me_ref[0], rows_ref, wd_ref, fup_ref, fgate_ref, store)


def hidden_pass(at_dir, me, buf, fup, fgate, wd):
    return pl.pallas_call(
        functools.partial(hidden_kernel, at_dir),
        in_specs=[IN_SMEM] + [IN_HBM] * (3 + len(wd)),
        out_specs=IN_VMEM,
        out_shape=jax.ShapeDtypeStruct((2, SLOTS, FF), BF),
        scratch_shapes=[
            pltpu.VMEM((MAIN, NCH * PCH), BF),
            pltpu.VMEM((SLOTS, D), BF),
            pltpu.VMEM((FF, D), BF),
            pltpu.VMEM((SLOTS, FF), F32),
            pltpu.VMEM((SLOTS, FF), F32),
            pltpu.SemaphoreType.DMA((3 + len(wd),)),
        ],
        compiler_params=pltpu.CompilerParams(vmem_limit_bytes=60 << 20),
        cost_estimate=pl.CostEstimate(flops=1_060_000_000, bytes_accessed=11_000_000, transcendentals=0),
        name="hidden_pass",
    )(me, buf, fup, fgate, *wd)


def own_grads_kernel(me_ref, own, left, right, far_g, far_u, wg_hbm, wu_hbm, out_ref, d_ref, wg_ref, wu_ref, sems):
    srcs = [own.at[0], left.at[0], right.at[0], far_g.at[0], own.at[1], left.at[1], right.at[1], far_u.at[0]]
    stream = Stream(sems, 10)
    stream.add(wg_hbm, wg_ref)
    for n in range(4):
        stream.add(srcs[n], d_ref.at[0, pl.ds(n * SLOTS, SLOTS)])
    stream.add(wu_hbm, wu_ref)
    for n in range(4):
        stream.add(srcs[4 + n], d_ref.at[1, pl.ds(n * SLOTS, SLOTS)])
    stream.wait(4)
    total = dot(d_ref[0], wg_ref[...], NT)
    stream.wait(9)
    total = (total + dot(d_ref[1], wu_ref[...], NT)).astype(BF)
    for n, shift in enumerate((0, 3, 1, 2)):
        put_chunk(total[n * SLOTS : (n + 1) * SLOTS], out_ref, (me_ref[0] + shift) & 3, None)


def own_grads(me, own, left, right, far_g, far_u, wg, wu):
    return pl.pallas_call(
        own_grads_kernel,
        in_specs=[IN_SMEM] + [IN_HBM] * 7,
        out_specs=IN_VMEM,
        out_shape=jax.ShapeDtypeStruct((4, MAIN, PCH), BF),
        scratch_shapes=[
            pltpu.VMEM((2, 4 * SLOTS, FF), BF),
            pltpu.VMEM((CH, FF), BF),
            pltpu.VMEM((CH, FF), BF),
            pltpu.SemaphoreType.DMA((10,)),
        ],
        compiler_params=pltpu.CompilerParams(vmem_limit_bytes=60 << 20),
        cost_estimate=pl.CostEstimate(flops=2_120_000_000, bytes_accessed=8_000_000, transcendentals=0),
        name="own_grads",
    )(me, own, left, right, far_g, far_u, wg, wu)


def expert_kernel(at_dir, whole, me_ref, buf_hbm, fup_hbm, fgate_hbm, *rest):
    pieces, groups = halves_plan(256)
    wd_refs, rest = rest[: len(pieces)], rest[len(pieces) :]
    me = me_ref[0]
    gpieces, ggroups = halves_plan(CH)
    count = 1 if whole else len(gpieces)
    g_src, wu_full, rest = rest[:count], rest[count], rest[count + 1 :]
    if whole:
        gpieces, ggroups = [(k, 0, CH) for k in range(4)], [(k, [k]) for k in range(4)]
        starts = [k * CH for k in range(4)]
        g_src = [g_src[0].at[pl.ds(row, CH)] for row in starts]
    else:
        starts = [pl.multiple_of(((me + shift) & 3) * CH + row, 64) for shift, row, _ in gpieces]
    u_src = [wu_full.at[pl.ds(row, width)] for row, (_, _, width) in zip(starts, gpieces)]
    out_ref, buf_ref, rows_ref, wd_ref, wg_ref, wu_ref, fup_ref, fgate_ref, dg_ref, du_ref, sems = rest
    stream = Stream(sems, 4)
    first = stream.add(buf_hbm, buf_ref)
    ids = add_shards(stream, wd_refs[:1], pieces[:1], wd_ref)
    stream.add(fup_hbm.at[at_dir], fup_ref)
    act = stream.add(fgate_hbm.at[at_dir], fgate_ref)
    ids += add_shards(stream, wd_refs[1:], pieces[1:], wd_ref.at[pl.ds(256, FF - 256)])
    grad_ids = []
    at = 0
    for n, (_, _, width) in enumerate(gpieces):
        place = pl.ds(at, width)
        grad_ids.append((stream.add(g_src[n], wg_ref.at[place]), stream.add(u_src[n], wu_ref.at[place])))
        at += width
    stream.wait(first)
    unpack_rows(buf_ref, rows_ref)
    stream.wait(act)

    def store(lo, dg, du):
        dg_ref[:, pl.ds(lo, 256)] = dg
        du_ref[:, pl.ds(lo, 256)] = du

    hidden_stage(stream, groups, ids, me, rows_ref, wd_ref, fup_ref, fgate_ref, store)
    for n, (shift, members) in enumerate(ggroups):
        for m in members:
            stream.wait(grad_ids[m][1])
        at = slice(n * CH, (n + 1) * CH)
        total = dot(dg_ref[...], wg_ref[at], NT) + dot(du_ref[...], wu_ref[at], NT)
        base = shift * PCH if whole else pl.multiple_of(((me + shift) & 3) * PCH, 128)
        put_chunk(total.astype(BF), out_ref, None, base)


def expert_pass(at_dir, me, buf, fup, fgate, wd, wg, wu):
    whole = len(wg) == 1
    copies = 3 + len(wd) + 2 * (4 if whole else len(wg))
    return pl.pallas_call(
        functools.partial(expert_kernel, at_dir, whole),
        in_specs=[IN_SMEM] + [IN_HBM] * (4 + len(wd) + len(wg)),
        out_specs=IN_VMEM,
        out_shape=jax.ShapeDtypeStruct((MAIN, NCH * PCH), BF),
        scratch_shapes=[
            pltpu.VMEM((MAIN, NCH * PCH), BF),
            pltpu.VMEM((SLOTS, D), BF),
            pltpu.VMEM((FF, D), BF),
            pltpu.VMEM((D, FF), BF),
            pltpu.VMEM((D, FF), BF),
            pltpu.VMEM((SLOTS, FF), F32),
            pltpu.VMEM((SLOTS, FF), F32),
            pltpu.VMEM((SLOTS, FF), BF),
            pltpu.VMEM((SLOTS, FF), BF),
            pltpu.SemaphoreType.DMA((copies,)),
        ],
        compiler_params=pltpu.CompilerParams(vmem_limit_bytes=60 << 20),
        cost_estimate=pl.CostEstimate(flops=3_200_000_000, bytes_accessed=28_000_000, transcendentals=0),
        name="expert_pass",
    )(me, buf, fup, fgate, *wd, *wg, wu)


def down_kernel(ha_ref, hb_ref, bufa_ref, bufb_ref, out_ref, rows_ref):
    r = lax.broadcasted_iota(I32, (128, MAIN), 0)
    c = lax.broadcasted_iota(I32, (128, MAIN), 1)
    spread = ones_where(c == (r & 15) * 8 + (r >> 4))
    total = None
    for h_ref, buf_ref in ((ha_ref, bufa_ref), (hb_ref, bufb_ref)):
        for rep in range(4):
            lo = rep * SLOTS
            block = slice(rep * MAIN, (rep + 1) * MAIN)
            rows_ref[lo : lo + MAIN, :] = buf_ref[block, 0:CH]
            nin = dot(spread, buf_ref[block, CH:PCH]).astype(BF)
            for k in range(PIECES):
                rows_ref[lo + MAIN : lo + SLOTS, k * 128 : (k + 1) * 128] = nin[k * 16 : (k + 1) * 16, :]
        term = dot(h_ref[...], rows_ref[...])
        total = term if total is None else total + term
    out_ref[...] = total.astype(BF)


def down_pass(ha, hb, bufa, bufb):
    packed = pl.BlockSpec((4 * MAIN, PCH), lambda j: (0, j))
    whole = pl.BlockSpec((256, 4 * SLOTS), lambda j: (0, 0))
    return pl.pallas_call(
        down_kernel,
        grid=(NCH,),
        in_specs=[whole, whole, packed, packed],
        out_specs=pl.BlockSpec((256, CH), lambda j: (0, j)),
        out_shape=jax.ShapeDtypeStruct((256, D), BF),
        scratch_shapes=[pltpu.VMEM((4 * SLOTS, CH), BF)],
        compiler_params=pltpu.CompilerParams(vmem_limit_bytes=60 << 20),
        cost_estimate=pl.CostEstimate(flops=2_120_000_000, bytes_accessed=11_000_000, transcendentals=0),
        name="down_pass",
    )(ha, hb, bufa, bufb)


def exchange(buf):
    return lax.all_to_all(
        buf.reshape(EXP, 8, NCH * PCH), "expert", split_axis=0, concat_axis=0, tiled=True
    ).reshape(MAIN, NCH * PCH)


def slot_targets(routes):
    flat = routes.reshape(2, TOK * 2)
    n = TOK * 2
    row = lax.broadcasted_iota(I32, (n, n), 0)
    col = lax.broadcasted_iota(I32, (n, n), 1)
    same = jnp.logical_and(flat[:, :, None] == flat[:, None, :], (col < row)[None])
    return (flat * CAP + jnp.sum(same.astype(I32), axis=2)).reshape(2, TOK, 2)


def shift_dp(value, step, sections):
    pairs = [(s * 4 + i, s * 4 + (i + step) % 4) for s in sections for i in range(4)]
    return lax.ppermute(value, ("pipe", "dp"), pairs)


def tie(value, *others):
    return lax.optimization_barrier((value,) + others)[0]


def per_device(
    seed_grads, expert_routes, route_weights, saved_gate, saved_up, w_gate, w_up, w_down
):
    section = lax.axis_index("pipe")
    dp = lax.axis_index("dp").astype(I32)
    me = dp.reshape(1)
    first_up = section < 2
    first = jnp.where(first_up, 1, 0).astype(I32)
    order = jnp.stack([first, 1 - first])
    every, outer, inner = (0, 1, 2, 3), (0, 3), (1, 2)

    def gather(x):
        return lax.all_gather(x, "dp", axis=0, tiled=True)

    def near(x, sections):
        return shift_dp(x, 1, sections), shift_dp(x, -1, sections)

    def far(left, right, sections):
        half = left.shape[0] // 2
        return shift_dp(left[:half], 1, sections), shift_dp(right[half:], -1, sections)

    wd_own, wg_own, wu_own = w_down[0, 0], w_gate[0, 0], w_up[0, 0]
    wd_near = near(wd_own, every)

    def ordered(x):
        return jnp.where(first_up, x[1], x[0]), jnp.where(first_up, x[0], x[1])

    targets = slot_targets(expert_routes[:, 0])
    tgt = ordered(targets)
    wts = ordered(route_weights[:, 0])
    tgt_t = [t.T for t in tgt]
    wts_t = [w.T for w in wts]
    cur = jnp.where(first_up, seed_grads[1], seed_grads[0])
    fup, fgate, hidden = prep(order, saved_gate[:, 0, 0, 0], saved_up[:, 0, 0, 0])
    wg_near = near(tie(wg_own, hidden, *wd_near), inner)

    edge = jnp.logical_or(section == 0, section == 3)
    moves = [[(0, 1), (3, 2)], [(1, 2), (2, 1)], [(2, 3), (1, 0)]]
    results = []
    bufs = []
    for step in range(4):
        at = step // 2
        outgoing = pre(tgt_t[at], wts_t[at], cur)
        if step == 1:
            outgoing = tie(outgoing, *wg)
        if step == 2:
            outgoing = tie(outgoing, buf_first)
        buf = exchange(outgoing)
        bufs.append(buf)
        if step == 0:
            wd = (wd_own,) + wd_near + far(*[tie(w, buf) for w in wd_near], every)
            dgu = hidden_pass(at, me, buf, fup, fgate, wd)
            dgu_near = near(tie(dgu, *wg_near), outer)
            dgu_far = far(*dgu_near, outer)
            sent = own_grads(me, dgu, *dgu_near, *dgu_far, wg_own, wu_own)
            wu_full = gather(tie(wu_own, *dgu_far))
            wg = (wg_own,) + wg_near + far(*[tie(w, sent) for w in wg_near], inner)
            home = lax.all_to_all(
                sent.reshape(4 * EXP, 8, PCH), ("dp", "expert"), split_axis=0, concat_axis=0, tiled=True
            ).reshape(4, MAIN, PCH)
            result = post(tgt[at], cur, home)
        else:
            if step == 1:
                wg_full = (gather(tie(wg_own, buf)),)
                buf_first = jnp.where(edge, bufs[0], bufs[1])
                all_first = gather(buf_first)
                hidden_all = lax.all_gather(tie(hidden, buf_first), "dp", axis=0)
            if step == 3:
                wg = wg_full
                all_second = gather(jnp.where(edge, bufs[3], bufs[2]))
            packed = expert_pass(at, me, buf, fup, fgate, wd, wg, wu_full)
            result = post(tgt[at], cur, exchange(packed))
        results.append(result)
        if step < 3:
            cur = lax.ppermute(result, "pipe", moves[step])

    res_first = jnp.where(edge, results[0], results[1])
    res_second = jnp.where(edge, results[3], results[2])
    input_grads = jnp.where(
        first_up, jnp.stack([res_second, res_first]), jnp.stack([res_first, res_second])
    )[:, None]

    hidden_mine = lax.dynamic_slice_in_dim(hidden_all, dp * 256, 256, axis=3)
    hidden_t = hidden_mine.transpose(1, 3, 0, 2).reshape(2, 256, 4 * SLOTS)
    down_grads = down_pass(hidden_t[0], hidden_t[1], all_first, all_second)
    return input_grads, down_grads[None, None]


def solution(mesh):
    return jax.shard_map(
        per_device,
        mesh=mesh,
        in_specs=(
            P(None, ("expert", "dp"), None),
            P(None, "pipe", ("expert", "dp"), None),
            P(None, "pipe", ("expert", "dp"), None),
            P(None, "pipe", "dp", "expert", None, None),
            P(None, "pipe", "dp", "expert", None, None),
            P("pipe", "expert", "dp", None),
            P("pipe", "expert", "dp", None),
            P("pipe", "expert", "dp", None),
        ),
        out_specs=(P(None, "pipe", ("expert", "dp"), None), P("pipe", "expert", "dp", None)),
        check_vma=False,
    )
```

```python
import functools
import jax
import jax.numpy as jnp
from jax import lax
from jax.experimental import pallas as pl
from jax.experimental.pallas import tpu as pltpu
from jax.sharding import PartitionSpec as P

BF = jnp.bfloat16
F32 = jnp.float32
I32 = jnp.int32
D = 3584
FF = 1024
TOK = 64
EXP = 16
CAP = 9
SLOTS = 144
MAIN = 128
CH = 896
PCH = 1024
NCH = 4
PIECES = 7
NT = (((1,), (1,)), ((), ()))
NN = (((1,), (0,)), ((), ()))


IN_HBM = pl.BlockSpec(memory_space=pl.ANY)
IN_SMEM = pl.BlockSpec(memory_space=pltpu.SMEM)
IN_VMEM = pl.BlockSpec(memory_space=pltpu.VMEM)


def dot(a, b, dims=NN):
    return lax.dot_general(a, b, dims, preferred_element_type=F32)


def ones_where(mask):
    return jnp.where(mask, 1.0, 0.0).astype(BF)


def prep_kernel(order_ref, gate_ref, up_ref, fup_ref, fgate_ref, hidden_ref):
    row = lax.broadcasted_iota(I32, (SLOTS, SLOTS), 0)
    col = lax.broadcasted_iota(I32, (SLOTS, SLOTS), 1)
    slot = jnp.where(row < MAIN, (row >> 3) * CAP + (row & 7), (row - MAIN) * CAP + 8)
    perm = ones_where(col == slot)
    gate = dot(perm, gate_ref[0])
    up = dot(perm, up_ref[0])
    sig = 1.0 / (1.0 + jnp.exp(-gate))
    act = gate * sig
    fup_ref[0] = act
    fgate_ref[0] = up * sig * (1.0 + gate * (1.0 - sig))
    hidden_ref[0] = (act * up).astype(BF)


def prep(order, gate, up):
    spec_in = pl.BlockSpec((1, SLOTS, FF), lambda i, o: (o[i], 0, 0))
    spec_out = pl.BlockSpec((1, SLOTS, FF), lambda i, o: (i, 0, 0))
    return pl.pallas_call(
        prep_kernel,
        out_shape=(
            jax.ShapeDtypeStruct((2, SLOTS, FF), F32),
            jax.ShapeDtypeStruct((2, SLOTS, FF), F32),
            jax.ShapeDtypeStruct((2, SLOTS, FF), BF),
        ),
        grid_spec=pltpu.PrefetchScalarGridSpec(
            num_scalar_prefetch=1,
            grid=(2,),
            in_specs=[spec_in, spec_in],
            out_specs=[spec_out, spec_out, spec_out],
        ),
        compiler_params=pltpu.CompilerParams(vmem_limit_bytes=24 << 20),
        cost_estimate=pl.CostEstimate(flops=170_000_000, bytes_accessed=4_700_000, transcendentals=300_000),
        name="prep",
    )(order, gate, up)


def pre_kernel(pick_ref, t_ref, w_ref, old_ref, new_ref, out_ref):
    keep = pick_ref[0] > 0
    c = lax.broadcasted_iota(I32, (MAIN, TOK), 0)
    e9 = (c >> 3) * CAP
    t0 = t_ref[0:1, :]
    t1 = t_ref[1:2, :]
    w0 = w_ref[0:1, :]
    w1 = w_ref[1:2, :]

    def pick(slot):
        m0 = t0 == slot
        m1 = t1 == slot
        scale = jnp.sum(jnp.where(m0, w0, 0.0) + jnp.where(m1, w1, 0.0), axis=1, keepdims=True)
        return ones_where(jnp.logical_or(m0, m1)), scale

    main, scale_main = pick(e9 + (c & 7))
    last, scale_last = pick(e9 + 8)
    piece = lax.broadcasted_iota(I32, (MAIN, 128), 0) & 7
    for j in range(NCH):
        cols = slice(j * CH, (j + 1) * CH)
        x = jnp.where(keep, old_ref[:, cols], new_ref[:, cols])
        out_ref[:, j * PCH : j * PCH + CH] = (dot(main, x) * scale_main).astype(BF)
        full = dot(last, x)
        part = jnp.zeros((MAIN, 128), F32)
        for k in range(PIECES):
            part = jnp.where(piece == k, full[:, k * 128 : (k + 1) * 128], part)
        out_ref[:, j * PCH + CH : (j + 1) * PCH] = (part * scale_last).astype(BF)


def pre(keep, targets_t, weights_t, old, new):
    return pl.pallas_call(
        pre_kernel,
        in_specs=[IN_SMEM] + [IN_VMEM] * 4,
        out_shape=jax.ShapeDtypeStruct((MAIN, NCH * PCH), BF),
        compiler_params=pltpu.CompilerParams(vmem_limit_bytes=16 << 20),
        cost_estimate=pl.CostEstimate(flops=120_000_000, bytes_accessed=1_600_000, transcendentals=0),
        name="pre",
    )(keep, targets_t, weights_t, old, new)


def post_kernel(t_ref, cur_ref, buf_ref, out_ref):
    c = lax.broadcasted_iota(I32, (TOK, MAIN), 1)
    e9 = (c >> 3) * CAP
    s = c & 7
    t0 = t_ref[:, 0:1]
    t1 = t_ref[:, 1:2]

    def pick(slot):
        return jnp.logical_or(t0 == slot, t1 == slot)

    main = ones_where(pick(e9 + s))
    last = pick(e9 + 8)
    tail = jnp.concatenate(
        [ones_where(jnp.logical_and(last, s == k)) for k in range(PIECES)], axis=0
    )
    for j in range(NCH):
        if len(buf_ref.shape) == 3:
            packed = buf_ref[j]
        else:
            packed = buf_ref[:, j * PCH : (j + 1) * PCH]
        acc = dot(main, packed[:, :CH])
        nin = dot(tail, packed[:, CH:])
        for k in range(PIECES):
            lo = j * CH + k * 128
            out_ref[:, lo : lo + 128] = (
                cur_ref[:, lo : lo + 128].astype(F32)
                + (acc[:, k * 128 : (k + 1) * 128] + nin[k * TOK : (k + 1) * TOK, :])
            ).astype(BF)


def post(targets, cur, buf):
    return pl.pallas_call(
        post_kernel,
        out_shape=jax.ShapeDtypeStruct((TOK, D), BF),
        compiler_params=pltpu.CompilerParams(vmem_limit_bytes=16 << 20),
        cost_estimate=pl.CostEstimate(flops=120_000_000, bytes_accessed=2_000_000, transcendentals=0),
        name="post",
    )(targets, cur, buf)


def unpack_rows(buf_ref, rows_ref):
    r = lax.broadcasted_iota(I32, (128, MAIN), 0)
    c = lax.broadcasted_iota(I32, (128, MAIN), 1)
    spread = ones_where(c == (r & 15) * 8 + (r >> 4))
    for j in range(NCH):
        rows_ref[0:MAIN, j * CH : (j + 1) * CH] = buf_ref[:, j * PCH : j * PCH + CH]
        nin = dot(spread, buf_ref[:, j * PCH + CH : (j + 1) * PCH]).astype(BF)
        for k in range(PIECES):
            lo = j * CH + k * 128
            rows_ref[MAIN:SLOTS, lo : lo + 128] = nin[k * 16 : (k + 1) * 16, :]


def put_chunk(grads, out_ref, lead, base):
    c = lax.broadcasted_iota(I32, (MAIN, 128), 0)
    r = lax.broadcasted_iota(I32, (MAIN, 128), 1)
    fold = ones_where(r == (c & 7) * 16 + (c >> 3))
    pieces = [grads[MAIN:SLOTS, k * 128 : (k + 1) * 128] for k in range(PIECES)]
    pieces.append(jnp.zeros((16, 128), BF))
    tail = dot(fold, jnp.concatenate(pieces, axis=0)).astype(BF)
    if lead is None:
        out_ref[:, pl.ds(base, CH)] = grads[0:MAIN]
        out_ref[:, pl.ds(base + CH, 128)] = tail
    else:
        out_ref[lead, :, 0:CH] = grads[0:MAIN]
        out_ref[lead, :, CH:PCH] = tail


def hidden_part(rows_ref, wd, fup_ref, fgate_ref, lo, width):
    d_hidden = dot(rows_ref[...], wd, NT)
    cols = pl.ds(lo, width)
    return (d_hidden * fgate_ref[:, cols]).astype(BF), (d_hidden * fup_ref[:, cols]).astype(BF)


def halves_plan(shard):
    half = shard // 2
    pieces = [(0, 0, shard)]
    groups = [(0, [0])]
    for shift, parts in ((3, False), (1, False), (2, True)):
        mine = []
        for row, width in ((0, half), (half, half)) if parts else ((0, shard),):
            mine.append(len(pieces))
            pieces.append((shift, row, width))
        groups.append((shift, mine))
    return pieces, groups


class Stream:
    def __init__(self, sems, ahead):
        self.sems, self.ahead, self.todo, self.flying, self.done = sems, ahead, [], [], 0

    def add(self, src, dst):
        self.todo.append((src, dst))
        return len(self.todo) - 1

    def start(self, upto):
        while len(self.flying) < min(upto, len(self.todo)):
            n = len(self.flying)
            copy = pltpu.make_async_copy(*self.todo[n], self.sems.at[n])
            copy.start()
            self.flying.append(copy)

    def wait(self, n):
        self.start(n + 1 + self.ahead)
        while self.done <= n:
            self.flying[self.done].wait()
            self.done += 1


def hidden_stage(stream, groups, ids, me, rows_ref, wd_ref, fup_ref, fgate_ref, store):
    for n, (shift, members) in enumerate(groups):
        for m in members:
            stream.wait(ids[m])
        lo = pl.multiple_of(((me + shift) & 3) * 256, 128)
        dg, du = hidden_part(rows_ref, wd_ref[n * 256 : (n + 1) * 256], fup_ref, fgate_ref, lo, 256)
        store(lo, dg, du)


def add_shards(stream, srcs, pieces, dst_ref):
    at = 0
    ids = []
    for src, (_, _, width) in zip(srcs, pieces):
        ids.append(stream.add(src, dst_ref.at[pl.ds(at, width)]))
        at += width
    return ids


def hidden_kernel(at_dir, me_ref, buf_hbm, fup_hbm, fgate_hbm, *rest):
    pieces, groups = halves_plan(256)
    wd_refs, rest = rest[: len(pieces)], rest[len(pieces) :]
    dgu_ref, buf_ref, rows_ref, wd_ref, fup_ref, fgate_ref, sems = rest
    stream = Stream(sems, 4)
    first = stream.add(buf_hbm, buf_ref)
    ids = add_shards(stream, wd_refs[:1], pieces[:1], wd_ref)
    stream.add(fup_hbm.at[at_dir], fup_ref)
    act = stream.add(fgate_hbm.at[at_dir], fgate_ref)
    ids += add_shards(stream, wd_refs[1:], pieces[1:], wd_ref.at[pl.ds(256, FF - 256)])
    stream.wait(first)
    unpack_rows(buf_ref, rows_ref)
    stream.wait(act)

    def store(lo, dg, du):
        dgu_ref[0, :, pl.ds(lo, 256)] = dg
        dgu_ref[1, :, pl.ds(lo, 256)] = du

    hidden_stage(stream, groups, ids, me_ref[0], rows_ref, wd_ref, fup_ref, fgate_ref, store)


def hidden_pass(at_dir, me, buf, fup, fgate, wd):
    return pl.pallas_call(
        functools.partial(hidden_kernel, at_dir),
        in_specs=[IN_SMEM] + [IN_HBM] * (3 + len(wd)),
        out_specs=IN_VMEM,
        out_shape=jax.ShapeDtypeStruct((2, SLOTS, FF), BF),
        scratch_shapes=[
            pltpu.VMEM((MAIN, NCH * PCH), BF),
            pltpu.VMEM((SLOTS, D), BF),
            pltpu.VMEM((FF, D), BF),
            pltpu.VMEM((SLOTS, FF), F32),
            pltpu.VMEM((SLOTS, FF), F32),
            pltpu.SemaphoreType.DMA((3 + len(wd),)),
        ],
        compiler_params=pltpu.CompilerParams(vmem_limit_bytes=60 << 20),
        cost_estimate=pl.CostEstimate(flops=1_060_000_000, bytes_accessed=11_000_000, transcendentals=0),
        name="hidden_pass",
    )(me, buf, fup, fgate, *wd)


def own_grads_kernel(me_ref, own, left, right, far_g, far_u, wg_hbm, wu_hbm, out_ref, d_ref, wg_ref, wu_ref, sems):
    srcs = [own.at[0], left.at[0], right.at[0], far_g.at[0], own.at[1], left.at[1], right.at[1], far_u.at[0]]
    stream = Stream(sems, 10)
    stream.add(wg_hbm, wg_ref)
    for n in range(4):
        stream.add(srcs[n], d_ref.at[0, pl.ds(n * SLOTS, SLOTS)])
    stream.add(wu_hbm, wu_ref)
    for n in range(4):
        stream.add(srcs[4 + n], d_ref.at[1, pl.ds(n * SLOTS, SLOTS)])
    stream.wait(4)
    total = dot(d_ref[0], wg_ref[...], NT)
    stream.wait(9)
    total = (total + dot(d_ref[1], wu_ref[...], NT)).astype(BF)
    for n, shift in enumerate((0, 3, 1, 2)):
        put_chunk(total[n * SLOTS : (n + 1) * SLOTS], out_ref, (me_ref[0] + shift) & 3, None)


def own_grads(me, own, left, right, far_g, far_u, wg, wu):
    return pl.pallas_call(
        own_grads_kernel,
        in_specs=[IN_SMEM] + [IN_HBM] * 7,
        out_specs=IN_VMEM,
        out_shape=jax.ShapeDtypeStruct((4, MAIN, PCH), BF),
        scratch_shapes=[
            pltpu.VMEM((2, 4 * SLOTS, FF), BF),
            pltpu.VMEM((CH, FF), BF),
            pltpu.VMEM((CH, FF), BF),
            pltpu.SemaphoreType.DMA((10,)),
        ],
        compiler_params=pltpu.CompilerParams(vmem_limit_bytes=60 << 20),
        cost_estimate=pl.CostEstimate(flops=2_120_000_000, bytes_accessed=8_000_000, transcendentals=0),
        name="own_grads",
    )(me, own, left, right, far_g, far_u, wg, wu)


def expert_kernel(at_dir, whole, me_ref, buf_hbm, fup_hbm, fgate_hbm, *rest):
    pieces, groups = halves_plan(256)
    wd_refs, rest = rest[: len(pieces)], rest[len(pieces) :]
    me = me_ref[0]
    gpieces, ggroups = halves_plan(CH)
    count = 1 if whole else len(gpieces)
    g_src, wu_full, rest = rest[:count], rest[count], rest[count + 1 :]
    if whole:
        gpieces, ggroups = [(k, 0, CH) for k in range(4)], [(k, [k]) for k in range(4)]
        starts = [k * CH for k in range(4)]
        g_src = [g_src[0].at[pl.ds(row, CH)] for row in starts]
    else:
        starts = [pl.multiple_of(((me + shift) & 3) * CH + row, 64) for shift, row, _ in gpieces]
    u_src = [wu_full.at[pl.ds(row, width)] for row, (_, _, width) in zip(starts, gpieces)]
    out_ref, buf_ref, rows_ref, wd_ref, wg_ref, wu_ref, fup_ref, fgate_ref, dg_ref, du_ref, sems = rest
    stream = Stream(sems, 4)
    first = stream.add(buf_hbm, buf_ref)
    ids = add_shards(stream, wd_refs[:1], pieces[:1], wd_ref)
    stream.add(fup_hbm.at[at_dir], fup_ref)
    act = stream.add(fgate_hbm.at[at_dir], fgate_ref)
    ids += add_shards(stream, wd_refs[1:], pieces[1:], wd_ref.at[pl.ds(256, FF - 256)])
    grad_ids = []
    at = 0
    for n, (_, _, width) in enumerate(gpieces):
        place = pl.ds(at, width)
        grad_ids.append((stream.add(g_src[n], wg_ref.at[place]), stream.add(u_src[n], wu_ref.at[place])))
        at += width
    stream.wait(first)
    unpack_rows(buf_ref, rows_ref)
    stream.wait(act)

    def store(lo, dg, du):
        dg_ref[:, pl.ds(lo, 256)] = dg
        du_ref[:, pl.ds(lo, 256)] = du

    hidden_stage(stream, groups, ids, me, rows_ref, wd_ref, fup_ref, fgate_ref, store)
    for n, (shift, members) in enumerate(ggroups):
        for m in members:
            stream.wait(grad_ids[m][1])
        at = slice(n * CH, (n + 1) * CH)
        total = dot(dg_ref[...], wg_ref[at], NT) + dot(du_ref[...], wu_ref[at], NT)
        base = shift * PCH if whole else pl.multiple_of(((me + shift) & 3) * PCH, 128)
        put_chunk(total.astype(BF), out_ref, None, base)


def expert_pass(at_dir, me, buf, fup, fgate, wd, wg, wu):
    whole = len(wg) == 1
    copies = 3 + len(wd) + 2 * (4 if whole else len(wg))
    return pl.pallas_call(
        functools.partial(expert_kernel, at_dir, whole),
        in_specs=[IN_SMEM] + [IN_HBM] * (4 + len(wd) + len(wg)),
        out_specs=IN_VMEM,
        out_shape=jax.ShapeDtypeStruct((MAIN, NCH * PCH), BF),
        scratch_shapes=[
            pltpu.VMEM((MAIN, NCH * PCH), BF),
            pltpu.VMEM((SLOTS, D), BF),
            pltpu.VMEM((FF, D), BF),
            pltpu.VMEM((D, FF), BF),
            pltpu.VMEM((D, FF), BF),
            pltpu.VMEM((SLOTS, FF), F32),
            pltpu.VMEM((SLOTS, FF), F32),
            pltpu.VMEM((SLOTS, FF), BF),
            pltpu.VMEM((SLOTS, FF), BF),
            pltpu.SemaphoreType.DMA((copies,)),
        ],
        compiler_params=pltpu.CompilerParams(vmem_limit_bytes=60 << 20),
        cost_estimate=pl.CostEstimate(flops=3_200_000_000, bytes_accessed=28_000_000, transcendentals=0),
        name="expert_pass",
    )(me, buf, fup, fgate, *wd, *wg, wu)


def down_term(h_ref, buf_ref, rows_ref):
    r = lax.broadcasted_iota(I32, (128, MAIN), 0)
    c = lax.broadcasted_iota(I32, (128, MAIN), 1)
    spread = ones_where(c == (r & 15) * 8 + (r >> 4))
    for rep in range(4):
        lo = rep * SLOTS
        block = slice(rep * MAIN, (rep + 1) * MAIN)
        rows_ref[lo : lo + MAIN, :] = buf_ref[block, 0:CH]
        nin = dot(spread, buf_ref[block, CH:PCH]).astype(BF)
        for k in range(PIECES):
            rows_ref[lo + MAIN : lo + SLOTS, k * 128 : (k + 1) * 128] = nin[k * 16 : (k + 1) * 16, :]
    return dot(h_ref[...], rows_ref[...])


def down_first_kernel(h_ref, buf_ref, out_ref, rows_ref):
    out_ref[...] = down_term(h_ref, buf_ref, rows_ref)


def down_last_kernel(h_ref, buf_ref, sum_ref, out_ref, rows_ref):
    out_ref[...] = (sum_ref[...] + down_term(h_ref, buf_ref, rows_ref)).astype(BF)


def down_pass(h, buf, total=None):
    block = pl.BlockSpec((256, CH), lambda j: (0, j))
    specs = [
        pl.BlockSpec((256, 4 * SLOTS), lambda j: (0, 0)),
        pl.BlockSpec((4 * MAIN, PCH), lambda j: (0, j)),
    ]
    args = [h, buf]
    if total is not None:
        specs.append(block)
        args.append(total)
    return pl.pallas_call(
        down_first_kernel if total is None else down_last_kernel,
        grid=(NCH,),
        in_specs=specs,
        out_specs=block,
        out_shape=jax.ShapeDtypeStruct((256, D), F32 if total is None else BF),
        scratch_shapes=[pltpu.VMEM((4 * SLOTS, CH), BF)],
        compiler_params=pltpu.CompilerParams(vmem_limit_bytes=60 << 20),
        cost_estimate=pl.CostEstimate(flops=1_060_000_000, bytes_accessed=8_000_000, transcendentals=0),
        name="down_pass",
    )(*args)


def exchange(buf):
    return lax.all_to_all(
        buf.reshape(EXP, 8, NCH * PCH), "expert", split_axis=0, concat_axis=0, tiled=True
    ).reshape(MAIN, NCH * PCH)


def slot_targets(routes):
    flat = routes.reshape(2, TOK * 2)
    n = TOK * 2
    row = lax.broadcasted_iota(I32, (n, n), 0)
    col = lax.broadcasted_iota(I32, (n, n), 1)
    same = jnp.logical_and(flat[:, :, None] == flat[:, None, :], (col < row)[None])
    return (flat * CAP + jnp.sum(same.astype(I32), axis=2)).reshape(2, TOK, 2)


def shift_dp(value, step, sections):
    pairs = [(s * 4 + i, s * 4 + (i + step) % 4) for s in sections for i in range(4)]
    return lax.ppermute(value, ("pipe", "dp"), pairs)


def tie(value, *others):
    return lax.optimization_barrier((value,) + others)[0]


def per_device(
    seed_grads, expert_routes, route_weights, saved_gate, saved_up, w_gate, w_up, w_down
):
    section = lax.axis_index("pipe")
    dp = lax.axis_index("dp").astype(I32)
    me = dp.reshape(1)
    first_up = section < 2
    first = jnp.where(first_up, 1, 0).astype(I32)
    order = jnp.stack([first, 1 - first])
    every, outer, inner = (0, 1, 2, 3), (0, 3), (1, 2)

    def gather(x):
        return lax.all_gather(x, "dp", axis=0, tiled=True)

    def near(x, sections):
        return shift_dp(x, 1, sections), shift_dp(x, -1, sections)

    def far(left, right, sections):
        half = left.shape[0] // 2
        return shift_dp(left[:half], 1, sections), shift_dp(right[half:], -1, sections)

    wd_own, wg_own, wu_own = w_down[0, 0], w_gate[0, 0], w_up[0, 0]
    wd_near = near(wd_own, every)

    def ordered(x):
        return jnp.where(first_up, x[1], x[0]), jnp.where(first_up, x[0], x[1])

    targets = slot_targets(expert_routes[:, 0])
    tgt = ordered(targets)
    wts = ordered(route_weights[:, 0])
    tgt_t = [t.T for t in tgt]
    wts_t = [w.T for w in wts]
    cur = jnp.where(first_up, seed_grads[1], seed_grads[0])
    fup, fgate, hidden = prep(order, saved_gate[:, 0, 0, 0], saved_up[:, 0, 0, 0])

    wg_near = near(tie(wg_own, hidden, *wd_near), inner)

    edge = jnp.logical_or(section == 0, section == 3)
    keep_edge = edge.astype(I32).reshape(1)
    old = cur
    moves = [[(0, 1), (3, 2)], [(1, 2), (2, 1)], [(2, 3), (1, 0)]]
    results = []
    for step in range(4):
        at = step // 2
        keep = keep_edge if step == 1 else 1 - keep_edge if step == 3 else 0 * keep_edge
        outgoing = pre(keep, tgt_t[at], wts_t[at], old, cur)
        old = cur
        if step == 1:
            outgoing = tie(outgoing, *wg)
        buf = exchange(outgoing)
        if step == 0:
            wd = (wd_own,) + wd_near + far(*[tie(w, buf) for w in wd_near], every)
            dgu = hidden_pass(at, me, buf, fup, fgate, wd)
            dgu_near = near(tie(dgu, *wg_near), outer)
            dgu_far = far(*dgu_near, outer)
            sent = own_grads(me, dgu, *dgu_near, *dgu_far, wg_own, wu_own)
            wu_full = gather(tie(wu_own, *dgu_far))
            wg = (wg_own,) + wg_near + far(*[tie(w, sent) for w in wg_near], inner)
            home = lax.all_to_all(
                sent.reshape(4 * EXP, 8, PCH), ("dp", "expert"), split_axis=0, concat_axis=0, tiled=True
            ).reshape(4, MAIN, PCH)
            result = post(tgt[at], cur, home)
        else:
            if step == 1:
                wg_full = (gather(tie(wg_own, buf)),)
                all_first = gather(buf)
                hidden_all = lax.all_gather(tie(hidden, buf), "dp", axis=0)
            if step == 3:
                wg = wg_full
                all_second = gather(buf)
            packed = expert_pass(at, me, buf, fup, fgate, wd, wg, wu_full)
            result = post(tgt[at], cur, exchange(packed))
        results.append(result)
        if step < 3:
            cur = lax.ppermute(result, "pipe", moves[step])

    res_first = jnp.where(edge, results[0], results[1])
    res_second = jnp.where(edge, results[3], results[2])
    input_grads = jnp.where(
        first_up, jnp.stack([res_second, res_first]), jnp.stack([res_first, res_second])
    )[:, None]

    hidden_mine = lax.dynamic_slice_in_dim(hidden_all, dp * 256, 256, axis=3)
    hidden_t = hidden_mine.transpose(1, 3, 0, 2).reshape(2, 256, 4 * SLOTS)
    down_grads = down_pass(hidden_t[1], all_second, down_pass(hidden_t[0], all_first))
    return input_grads, down_grads[None, None]


def solution(mesh):
    return jax.shard_map(
        per_device,
        mesh=mesh,
        in_specs=(
            P(None, ("expert", "dp"), None),
            P(None, "pipe", ("expert", "dp"), None),
            P(None, "pipe", ("expert", "dp"), None),
            P(None, "pipe", "dp", "expert", None, None),
            P(None, "pipe", "dp", "expert", None, None),
            P("pipe", "expert", "dp", None),
            P("pipe", "expert", "dp", None),
            P("pipe", "expert", "dp", None),
        ),
        out_specs=(P(None, "pipe", ("expert", "dp"), None), P("pipe", "expert", "dp", None)),
        check_vma=False,
    )
```

```python
import functools
import jax
import jax.numpy as jnp
from jax import lax
from jax.experimental import pallas as pl
from jax.experimental.pallas import tpu as pltpu
from jax.sharding import PartitionSpec as P

BF = jnp.bfloat16
F32 = jnp.float32
I32 = jnp.int32
D = 3584
FF = 1024
TOK = 64
EXP = 16
CAP = 9
SLOTS = 144
MAIN = 128
CH = 896
PCH = 1024
NCH = 4
PIECES = 7
NT = (((1,), (1,)), ((), ()))
NN = (((1,), (0,)), ((), ()))


IN_HBM = pl.BlockSpec(memory_space=pl.ANY)
IN_SMEM = pl.BlockSpec(memory_space=pltpu.SMEM)
IN_VMEM = pl.BlockSpec(memory_space=pltpu.VMEM)


def dot(a, b, dims=NN):
    return lax.dot_general(a, b, dims, preferred_element_type=F32)


def ones_where(mask):
    return jnp.where(mask, 1.0, 0.0).astype(BF)


def prep_kernel(order_ref, gate_ref, up_ref, fup_ref, fgate_ref, hidden_ref):
    row = lax.broadcasted_iota(I32, (SLOTS, SLOTS), 0)
    col = lax.broadcasted_iota(I32, (SLOTS, SLOTS), 1)
    slot = jnp.where(row < MAIN, (row >> 3) * CAP + (row & 7), (row - MAIN) * CAP + 8)
    perm = ones_where(col == slot)
    gate = dot(perm, gate_ref[0])
    up = dot(perm, up_ref[0])
    sig = 1.0 / (1.0 + jnp.exp(-gate))
    act = gate * sig
    fup_ref[0] = act
    fgate_ref[0] = up * sig * (1.0 + gate * (1.0 - sig))
    hidden_ref[0] = (act * up).astype(BF)


def prep(order, gate, up):
    spec_in = pl.BlockSpec((1, SLOTS, FF), lambda i, o: (o[i], 0, 0))
    spec_out = pl.BlockSpec((1, SLOTS, FF), lambda i, o: (i, 0, 0))
    return pl.pallas_call(
        prep_kernel,
        out_shape=(
            jax.ShapeDtypeStruct((2, SLOTS, FF), F32),
            jax.ShapeDtypeStruct((2, SLOTS, FF), F32),
            jax.ShapeDtypeStruct((2, SLOTS, FF), BF),
        ),
        grid_spec=pltpu.PrefetchScalarGridSpec(
            num_scalar_prefetch=1,
            grid=(2,),
            in_specs=[spec_in, spec_in],
            out_specs=[spec_out, spec_out, spec_out],
        ),
        compiler_params=pltpu.CompilerParams(vmem_limit_bytes=24 << 20),
        cost_estimate=pl.CostEstimate(flops=170_000_000, bytes_accessed=4_700_000, transcendentals=300_000),
        name="prep",
    )(order, gate, up)


def pre_kernel(pick_ref, t_ref, w_ref, old_ref, new_ref, out_ref):
    keep = pick_ref[0] > 0
    c = lax.broadcasted_iota(I32, (MAIN, TOK), 0)
    e9 = (c >> 3) * CAP
    t0 = t_ref[0:1, :]
    t1 = t_ref[1:2, :]
    w0 = w_ref[0:1, :]
    w1 = w_ref[1:2, :]

    def pick(slot):
        m0 = t0 == slot
        m1 = t1 == slot
        scale = jnp.sum(jnp.where(m0, w0, 0.0) + jnp.where(m1, w1, 0.0), axis=1, keepdims=True)
        return ones_where(jnp.logical_or(m0, m1)), scale

    main, scale_main = pick(e9 + (c & 7))
    last, scale_last = pick(e9 + 8)
    piece = lax.broadcasted_iota(I32, (MAIN, 128), 0) & 7
    for j in range(NCH):
        cols = slice(j * CH, (j + 1) * CH)
        x = jnp.where(keep, old_ref[:, cols], new_ref[:, cols])
        out_ref[:, j * PCH : j * PCH + CH] = (dot(main, x) * scale_main).astype(BF)
        full = dot(last, x)
        part = jnp.zeros((MAIN, 128), F32)
        for k in range(PIECES):
            part = jnp.where(piece == k, full[:, k * 128 : (k + 1) * 128], part)
        out_ref[:, j * PCH + CH : (j + 1) * PCH] = (part * scale_last).astype(BF)


def pre(keep, targets_t, weights_t, old, new):
    return pl.pallas_call(
        pre_kernel,
        in_specs=[IN_SMEM] + [IN_VMEM] * 4,
        out_shape=jax.ShapeDtypeStruct((MAIN, NCH * PCH), BF),
        compiler_params=pltpu.CompilerParams(vmem_limit_bytes=16 << 20),
        cost_estimate=pl.CostEstimate(flops=120_000_000, bytes_accessed=1_600_000, transcendentals=0),
        name="pre",
    )(keep, targets_t, weights_t, old, new)


def post_kernel(t_ref, cur_ref, buf_ref, out_ref):
    c = lax.broadcasted_iota(I32, (TOK, MAIN), 1)
    e9 = (c >> 3) * CAP
    s = c & 7
    t0 = t_ref[:, 0:1]
    t1 = t_ref[:, 1:2]

    def pick(slot):
        return jnp.logical_or(t0 == slot, t1 == slot)

    main = ones_where(pick(e9 + s))
    last = pick(e9 + 8)
    tail = jnp.concatenate(
        [ones_where(jnp.logical_and(last, s == k)) for k in range(PIECES)], axis=0
    )
    for j in range(NCH):
        if len(buf_ref.shape) == 3:
            packed = buf_ref[j]
        else:
            packed = buf_ref[:, j * PCH : (j + 1) * PCH]
        acc = dot(main, packed[:, :CH])
        nin = dot(tail, packed[:, CH:])
        for k in range(PIECES):
            lo = j * CH + k * 128
            out_ref[:, lo : lo + 128] = (
                cur_ref[:, lo : lo + 128].astype(F32)
                + (acc[:, k * 128 : (k + 1) * 128] + nin[k * TOK : (k + 1) * TOK, :])
            ).astype(BF)


def post(targets, cur, buf):
    return pl.pallas_call(
        post_kernel,
        out_shape=jax.ShapeDtypeStruct((TOK, D), BF),
        compiler_params=pltpu.CompilerParams(vmem_limit_bytes=16 << 20),
        cost_estimate=pl.CostEstimate(flops=120_000_000, bytes_accessed=2_000_000, transcendentals=0),
        name="post",
    )(targets, cur, buf)


def unpack_rows(buf_ref, rows_ref):
    r = lax.broadcasted_iota(I32, (128, MAIN), 0)
    c = lax.broadcasted_iota(I32, (128, MAIN), 1)
    spread = ones_where(c == (r & 15) * 8 + (r >> 4))
    for j in range(NCH):
        rows_ref[0:MAIN, j * CH : (j + 1) * CH] = buf_ref[:, j * PCH : j * PCH + CH]
        nin = dot(spread, buf_ref[:, j * PCH + CH : (j + 1) * PCH]).astype(BF)
        for k in range(PIECES):
            lo = j * CH + k * 128
            rows_ref[MAIN:SLOTS, lo : lo + 128] = nin[k * 16 : (k + 1) * 16, :]


def put_chunk(grads, out_ref, lead, base):
    c = lax.broadcasted_iota(I32, (MAIN, 128), 0)
    r = lax.broadcasted_iota(I32, (MAIN, 128), 1)
    fold = ones_where(r == (c & 7) * 16 + (c >> 3))
    pieces = [grads[MAIN:SLOTS, k * 128 : (k + 1) * 128] for k in range(PIECES)]
    pieces.append(jnp.zeros((16, 128), BF))
    tail = dot(fold, jnp.concatenate(pieces, axis=0)).astype(BF)
    if lead is None:
        out_ref[:, pl.ds(base, CH)] = grads[0:MAIN]
        out_ref[:, pl.ds(base + CH, 128)] = tail
    else:
        out_ref[lead, :, 0:CH] = grads[0:MAIN]
        out_ref[lead, :, CH:PCH] = tail


def hidden_part(rows_ref, wd, fup_ref, fgate_ref, lo, width):
    d_hidden = dot(rows_ref[...], wd, NT)
    cols = pl.ds(lo, width)
    return (d_hidden * fgate_ref[:, cols]).astype(BF), (d_hidden * fup_ref[:, cols]).astype(BF)


def halves_plan(shard):
    half = shard // 2
    pieces = [(0, 0, shard)]
    groups = [(0, [0])]
    for shift, parts in ((3, False), (1, False), (2, True)):
        mine = []
        for row, width in ((0, half), (half, half)) if parts else ((0, shard),):
            mine.append(len(pieces))
            pieces.append((shift, row, width))
        groups.append((shift, mine))
    return pieces, groups


class Stream:
    def __init__(self, sems, ahead):
        self.sems, self.ahead, self.todo, self.flying, self.done = sems, ahead, [], [], 0

    def add(self, src, dst):
        self.todo.append((src, dst))
        return len(self.todo) - 1

    def start(self, upto):
        while len(self.flying) < min(upto, len(self.todo)):
            n = len(self.flying)
            copy = pltpu.make_async_copy(*self.todo[n], self.sems.at[n])
            copy.start()
            self.flying.append(copy)

    def wait(self, n):
        self.start(n + 1 + self.ahead)
        while self.done <= n:
            self.flying[self.done].wait()
            self.done += 1


def hidden_stage(stream, groups, ids, me, rows_ref, wd_ref, fup_ref, fgate_ref, store):
    for n, (shift, members) in enumerate(groups):
        for m in members:
            stream.wait(ids[m])
        lo = pl.multiple_of(((me + shift) & 3) * 256, 128)
        dg, du = hidden_part(rows_ref, wd_ref[n * 256 : (n + 1) * 256], fup_ref, fgate_ref, lo, 256)
        store(lo, dg, du)


def add_shards(stream, srcs, pieces, dst_ref):
    at = 0
    ids = []
    for src, (_, _, width) in zip(srcs, pieces):
        ids.append(stream.add(src, dst_ref.at[pl.ds(at, width)]))
        at += width
    return ids


def hidden_kernel(at_dir, me_ref, buf_hbm, fup_hbm, fgate_hbm, *rest):
    pieces, groups = halves_plan(256)
    wd_refs, rest = rest[: len(pieces)], rest[len(pieces) :]
    dgu_ref, buf_ref, rows_ref, wd_ref, fup_ref, fgate_ref, sems = rest
    stream = Stream(sems, 4)
    first = stream.add(buf_hbm, buf_ref)
    ids = add_shards(stream, wd_refs[:1], pieces[:1], wd_ref)
    stream.add(fup_hbm.at[at_dir], fup_ref)
    act = stream.add(fgate_hbm.at[at_dir], fgate_ref)
    ids += add_shards(stream, wd_refs[1:], pieces[1:], wd_ref.at[pl.ds(256, FF - 256)])
    stream.wait(first)
    unpack_rows(buf_ref, rows_ref)
    stream.wait(act)

    def store(lo, dg, du):
        dgu_ref[0, :, pl.ds(lo, 256)] = dg
        dgu_ref[1, :, pl.ds(lo, 256)] = du

    hidden_stage(stream, groups, ids, me_ref[0], rows_ref, wd_ref, fup_ref, fgate_ref, store)


def hidden_pass(at_dir, me, buf, fup, fgate, wd):
    return pl.pallas_call(
        functools.partial(hidden_kernel, at_dir),
        in_specs=[IN_SMEM] + [IN_HBM] * (3 + len(wd)),
        out_specs=IN_VMEM,
        out_shape=jax.ShapeDtypeStruct((2, SLOTS, FF), BF),
        scratch_shapes=[
            pltpu.VMEM((MAIN, NCH * PCH), BF),
            pltpu.VMEM((SLOTS, D), BF),
            pltpu.VMEM((FF, D), BF),
            pltpu.VMEM((SLOTS, FF), F32),
            pltpu.VMEM((SLOTS, FF), F32),
            pltpu.SemaphoreType.DMA((3 + len(wd),)),
        ],
        compiler_params=pltpu.CompilerParams(vmem_limit_bytes=60 << 20),
        cost_estimate=pl.CostEstimate(flops=1_060_000_000, bytes_accessed=11_000_000, transcendentals=0),
        name="hidden_pass",
    )(me, buf, fup, fgate, *wd)


def own_grads_kernel(me_ref, own, left, right, far_g, far_u, wg_hbm, wu_hbm, out_ref, d_ref, wg_ref, wu_ref, sems):
    srcs = [own.at[0], left.at[0], right.at[0], far_g.at[0], own.at[1], left.at[1], right.at[1], far_u.at[0]]
    stream = Stream(sems, 10)
    stream.add(wg_hbm, wg_ref)
    for n in range(4):
        stream.add(srcs[n], d_ref.at[0, pl.ds(n * SLOTS, SLOTS)])
    stream.add(wu_hbm, wu_ref)
    for n in range(4):
        stream.add(srcs[4 + n], d_ref.at[1, pl.ds(n * SLOTS, SLOTS)])
    stream.wait(4)
    total = dot(d_ref[0], wg_ref[...], NT)
    stream.wait(9)
    total = (total + dot(d_ref[1], wu_ref[...], NT)).astype(BF)
    for n, shift in enumerate((0, 3, 1, 2)):
        put_chunk(total[n * SLOTS : (n + 1) * SLOTS], out_ref, (me_ref[0] + shift) & 3, None)


def own_grads(me, own, left, right, far_g, far_u, wg, wu):
    return pl.pallas_call(
        own_grads_kernel,
        in_specs=[IN_SMEM] + [IN_HBM] * 7,
        out_specs=IN_VMEM,
        out_shape=jax.ShapeDtypeStruct((4, MAIN, PCH), BF),
        scratch_shapes=[
            pltpu.VMEM((2, 4 * SLOTS, FF), BF),
            pltpu.VMEM((CH, FF), BF),
            pltpu.VMEM((CH, FF), BF),
            pltpu.SemaphoreType.DMA((10,)),
        ],
        compiler_params=pltpu.CompilerParams(vmem_limit_bytes=60 << 20),
        cost_estimate=pl.CostEstimate(flops=2_120_000_000, bytes_accessed=8_000_000, transcendentals=0),
        name="own_grads",
    )(me, own, left, right, far_g, far_u, wg, wu)


def expert_kernel(at_dir, whole, me_ref, buf_hbm, fup_hbm, fgate_hbm, *rest):
    pieces, groups = halves_plan(256)
    wd_refs, rest = rest[: len(pieces)], rest[len(pieces) :]
    me = me_ref[0]
    gpieces, ggroups = halves_plan(CH)
    count = 1 if whole else len(gpieces)
    g_src, wu_full, rest = rest[:count], rest[count], rest[count + 1 :]
    if whole:
        gpieces, ggroups = [(k, 0, CH) for k in range(4)], [(k, [k]) for k in range(4)]
        starts = [k * CH for k in range(4)]
        g_src = [g_src[0].at[pl.ds(row, CH)] for row in starts]
    else:
        starts = [pl.multiple_of(((me + shift) & 3) * CH + row, 64) for shift, row, _ in gpieces]
    u_src = [wu_full.at[pl.ds(row, width)] for row, (_, _, width) in zip(starts, gpieces)]
    out_ref, buf_ref, rows_ref, wd_ref, wg_ref, wu_ref, fup_ref, fgate_ref, dg_ref, du_ref, sems = rest
    stream = Stream(sems, 4)
    first = stream.add(buf_hbm, buf_ref)
    ids = add_shards(stream, wd_refs[:1], pieces[:1], wd_ref)
    stream.add(fup_hbm.at[at_dir], fup_ref)
    act = stream.add(fgate_hbm.at[at_dir], fgate_ref)
    ids += add_shards(stream, wd_refs[1:], pieces[1:], wd_ref.at[pl.ds(256, FF - 256)])
    grad_ids = []
    at = 0
    for n, (_, _, width) in enumerate(gpieces):
        place = pl.ds(at, width)
        grad_ids.append((stream.add(g_src[n], wg_ref.at[place]), stream.add(u_src[n], wu_ref.at[place])))
        at += width
    stream.wait(first)
    unpack_rows(buf_ref, rows_ref)
    stream.wait(act)

    def store(lo, dg, du):
        dg_ref[:, pl.ds(lo, 256)] = dg
        du_ref[:, pl.ds(lo, 256)] = du

    hidden_stage(stream, groups, ids, me, rows_ref, wd_ref, fup_ref, fgate_ref, store)
    for n, (shift, members) in enumerate(ggroups):
        for m in members:
            stream.wait(grad_ids[m][1])
        at = slice(n * CH, (n + 1) * CH)
        total = dot(dg_ref[...], wg_ref[at], NT) + dot(du_ref[...], wu_ref[at], NT)
        base = shift * PCH if whole else pl.multiple_of(((me + shift) & 3) * PCH, 128)
        put_chunk(total.astype(BF), out_ref, None, base)


def expert_pass(at_dir, me, buf, fup, fgate, wd, wg, wu):
    whole = len(wg) == 1
    copies = 3 + len(wd) + 2 * (4 if whole else len(wg))
    return pl.pallas_call(
        functools.partial(expert_kernel, at_dir, whole),
        in_specs=[IN_SMEM] + [IN_HBM] * (4 + len(wd) + len(wg)),
        out_specs=IN_VMEM,
        out_shape=jax.ShapeDtypeStruct((MAIN, NCH * PCH), BF),
        scratch_shapes=[
            pltpu.VMEM((MAIN, NCH * PCH), BF),
            pltpu.VMEM((SLOTS, D), BF),
            pltpu.VMEM((FF, D), BF),
            pltpu.VMEM((D, FF), BF),
            pltpu.VMEM((D, FF), BF),
            pltpu.VMEM((SLOTS, FF), F32),
            pltpu.VMEM((SLOTS, FF), F32),
            pltpu.VMEM((SLOTS, FF), BF),
            pltpu.VMEM((SLOTS, FF), BF),
            pltpu.SemaphoreType.DMA((copies,)),
        ],
        compiler_params=pltpu.CompilerParams(vmem_limit_bytes=60 << 20),
        cost_estimate=pl.CostEstimate(flops=3_200_000_000, bytes_accessed=28_000_000, transcendentals=0),
        name="expert_pass",
    )(me, buf, fup, fgate, *wd, *wg, wu)


def front_kernel(at_dir, me_ref, buf_hbm, fup_hbm, fgate_hbm, *rest):
    pieces, groups = halves_plan(256)
    gpieces, ggroups = halves_plan(CH)
    wd_refs, wg_refs, rest = rest[:5], rest[5:10], rest[10:]
    (
        part_hbm, du_ref, buf_ref, rows_ref, wd_ref, wg_ref, fup_ref, fgate_ref, dg_ref, part_ref,
        sems, out_sems,
    ) = rest
    me = me_ref[0]
    stream = Stream(sems, 4)
    first = stream.add(buf_hbm, buf_ref)
    ids = add_shards(stream, wd_refs[:1], pieces[:1], wd_ref)
    stream.add(fup_hbm.at[at_dir], fup_ref)
    act = stream.add(fgate_hbm.at[at_dir], fgate_ref)
    ids += add_shards(stream, wd_refs[1:], pieces[1:], wd_ref.at[pl.ds(256, FF - 256)])
    grad_ids = add_shards(stream, wg_refs, gpieces, wg_ref)
    stream.wait(first)
    unpack_rows(buf_ref, rows_ref)
    stream.wait(act)

    def store(lo, dg, du):
        dg_ref[:, pl.ds(lo, 256)] = dg
        du_ref[:, pl.ds(lo, 256)] = du

    hidden_stage(stream, groups, ids, me, rows_ref, wd_ref, fup_ref, fgate_ref, store)
    outs = []
    for n, (shift, members) in enumerate(ggroups):
        for m in members:
            stream.wait(grad_ids[m])
        part_ref[n] = dot(dg_ref[...], wg_ref[n * CH : (n + 1) * CH], NT)
        outs.append(pltpu.make_async_copy(part_ref.at[n], part_hbm.at[(me + shift) & 3], out_sems.at[n]))
        outs[-1].start()
    for copy in outs:
        copy.wait()


def front_pass(at_dir, me, buf, fup, fgate, wd, wg):
    return pl.pallas_call(
        functools.partial(front_kernel, at_dir),
        in_specs=[IN_SMEM] + [IN_HBM] * 13,
        out_specs=[IN_HBM, IN_VMEM],
        out_shape=(
            jax.ShapeDtypeStruct((NCH, SLOTS, CH), F32),
            jax.ShapeDtypeStruct((SLOTS, FF), BF),
        ),
        scratch_shapes=[
            pltpu.VMEM((MAIN, NCH * PCH), BF),
            pltpu.VMEM((SLOTS, D), BF),
            pltpu.VMEM((FF, D), BF),
            pltpu.VMEM((D, FF), BF),
            pltpu.VMEM((SLOTS, FF), F32),
            pltpu.VMEM((SLOTS, FF), F32),
            pltpu.VMEM((SLOTS, FF), BF),
            pltpu.VMEM((NCH, SLOTS, CH), F32),
            pltpu.SemaphoreType.DMA((13,)),
            pltpu.SemaphoreType.DMA((NCH,)),
        ],
        compiler_params=pltpu.CompilerParams(vmem_limit_bytes=60 << 20),
        cost_estimate=pl.CostEstimate(flops=2_100_000_000, bytes_accessed=20_000_000, transcendentals=0),
        name="front_pass",
    )(me, buf, fup, fgate, *wd, *wg)


def back_kernel(du_hbm, part_hbm, wu_hbm, out_ref, du_ref, part_ref, wu_ref, sems):
    stream = Stream(sems, 4)
    stream.add(du_hbm, du_ref)
    for k in range(NCH):
        stream.add(wu_hbm.at[pl.ds(k * CH, CH)], wu_ref.at[k])
        stream.add(part_hbm.at[k], part_ref.at[k])
    for k in range(NCH):
        stream.wait(2 * k + 2)
        total = part_ref[k] + dot(du_ref[...], wu_ref[k], NT)
        put_chunk(total.astype(BF), out_ref, None, k * PCH)


def back_pass(du, part, wu):
    return pl.pallas_call(
        back_kernel,
        in_specs=[IN_HBM] * 3,
        out_specs=IN_VMEM,
        out_shape=jax.ShapeDtypeStruct((MAIN, NCH * PCH), BF),
        scratch_shapes=[
            pltpu.VMEM((SLOTS, FF), BF),
            pltpu.VMEM((NCH, SLOTS, CH), F32),
            pltpu.VMEM((NCH, CH, FF), BF),
            pltpu.SemaphoreType.DMA((1 + 2 * NCH,)),
        ],
        compiler_params=pltpu.CompilerParams(vmem_limit_bytes=60 << 20),
        cost_estimate=pl.CostEstimate(flops=1_060_000_000, bytes_accessed=10_000_000, transcendentals=0),
        name="back_pass",
    )(du, part, wu)


def down_term(h_ref, buf_ref, rows_ref):
    r = lax.broadcasted_iota(I32, (128, MAIN), 0)
    c = lax.broadcasted_iota(I32, (128, MAIN), 1)
    spread = ones_where(c == (r & 15) * 8 + (r >> 4))
    for rep in range(4):
        lo = rep * SLOTS
        block = slice(rep * MAIN, (rep + 1) * MAIN)
        rows_ref[lo : lo + MAIN, :] = buf_ref[block, 0:CH]
        nin = dot(spread, buf_ref[block, CH:PCH]).astype(BF)
        for k in range(PIECES):
            rows_ref[lo + MAIN : lo + SLOTS, k * 128 : (k + 1) * 128] = nin[k * 16 : (k + 1) * 16, :]
    return dot(h_ref[...], rows_ref[...])


def down_first_kernel(h_ref, buf_ref, out_ref, rows_ref):
    out_ref[...] = down_term(h_ref, buf_ref, rows_ref)


def down_first(h, buf):
    return pl.pallas_call(
        down_first_kernel,
        grid=(NCH,),
        in_specs=[
            pl.BlockSpec((256, 4 * SLOTS), lambda j: (0, 0)),
            pl.BlockSpec((4 * MAIN, PCH), lambda j: (0, j)),
        ],
        out_specs=pl.BlockSpec((256, CH), lambda j: (0, j)),
        out_shape=jax.ShapeDtypeStruct((256, D), F32),
        scratch_shapes=[pltpu.VMEM((4 * SLOTS, CH), BF)],
        compiler_params=pltpu.CompilerParams(vmem_limit_bytes=60 << 20),
        cost_estimate=pl.CostEstimate(flops=1_060_000_000, bytes_accessed=8_000_000, transcendentals=0),
        name="down_first",
    )(h, buf)


def down_last_kernel(h_hbm, buf_hbm, sum_hbm, out_hbm, h_ref, buf_ref, sum_ref, out_ref, rows_ref, sems, out_sems):
    stream = Stream(sems, 9)
    stream.add(h_hbm, h_ref)
    for j in range(NCH):
        stream.add(buf_hbm.at[:, pl.ds(j * PCH, PCH)], buf_ref.at[j])
        stream.add(sum_hbm.at[:, pl.ds(j * CH, CH)], sum_ref.at[j])
    outs = []
    for j in range(NCH):
        stream.wait(2 + 2 * j)
        out_ref[j] = (sum_ref[j] + down_term(h_ref, buf_ref.at[j], rows_ref.at[j % 2])).astype(BF)
        outs.append(pltpu.make_async_copy(out_ref.at[j], out_hbm.at[:, pl.ds(j * CH, CH)], out_sems.at[j]))
        outs[-1].start()
    for copy in outs:
        copy.wait()


def down_last(h, buf, total):
    return pl.pallas_call(
        down_last_kernel,
        in_specs=[IN_HBM] * 3,
        out_specs=IN_HBM,
        out_shape=jax.ShapeDtypeStruct((256, D), BF),
        scratch_shapes=[
            pltpu.VMEM((256, 4 * SLOTS), BF),
            pltpu.VMEM((NCH, 4 * MAIN, PCH), BF),
            pltpu.VMEM((NCH, 256, CH), F32),
            pltpu.VMEM((NCH, 256, CH), BF),
            pltpu.VMEM((2, 4 * SLOTS, CH), BF),
            pltpu.SemaphoreType.DMA((9,)),
            pltpu.SemaphoreType.DMA((NCH,)),
        ],
        compiler_params=pltpu.CompilerParams(vmem_limit_bytes=60 << 20),
        cost_estimate=pl.CostEstimate(flops=1_060_000_000, bytes_accessed=10_000_000, transcendentals=0),
        name="down_last",
    )(h, buf, total)


def exchange(buf):
    return lax.all_to_all(
        buf.reshape(EXP, 8, NCH * PCH), "expert", split_axis=0, concat_axis=0, tiled=True
    ).reshape(MAIN, NCH * PCH)


def slot_targets(routes):
    flat = routes.reshape(2, TOK * 2)
    n = TOK * 2
    row = lax.broadcasted_iota(I32, (n, n), 0)
    col = lax.broadcasted_iota(I32, (n, n), 1)
    same = jnp.logical_and(flat[:, :, None] == flat[:, None, :], (col < row)[None])
    return (flat * CAP + jnp.sum(same.astype(I32), axis=2)).reshape(2, TOK, 2)


def shift_dp(value, step, sections):
    pairs = [(s * 4 + i, s * 4 + (i + step) % 4) for s in sections for i in range(4)]
    return lax.ppermute(value, ("pipe", "dp"), pairs)


def tie(value, *others):
    return lax.optimization_barrier((value,) + others)[0]


def per_device(
    seed_grads, expert_routes, route_weights, saved_gate, saved_up, w_gate, w_up, w_down
):
    section = lax.axis_index("pipe")
    dp = lax.axis_index("dp").astype(I32)
    me = dp.reshape(1)
    first_up = section < 2
    first = jnp.where(first_up, 1, 0).astype(I32)
    order = jnp.stack([first, 1 - first])
    every, outer, inner = (0, 1, 2, 3), (0, 3), (1, 2)

    def gather(x):
        return lax.all_gather(x, "dp", axis=0, tiled=True)

    def near(x, sections):
        return shift_dp(x, 1, sections), shift_dp(x, -1, sections)

    def hop(top, low, sections):
        return shift_dp(top, 1, sections), shift_dp(low, -1, sections)

    def far(left, right, sections):
        half = left.shape[0] // 2
        return hop(left[:half], right[half:], sections)

    wd_own, wg_own, wu_own = w_down[0, 0], w_gate[0, 0], w_up[0, 0]
    wd_near = near(wd_own, every)

    def ordered(x):
        return jnp.where(first_up, x[1], x[0]), jnp.where(first_up, x[0], x[1])

    targets = slot_targets(expert_routes[:, 0])
    tgt = ordered(targets)
    wts = ordered(route_weights[:, 0])
    tgt_t = [t.T for t in tgt]
    wts_t = [w.T for w in wts]
    cur = jnp.where(first_up, seed_grads[1], seed_grads[0])
    fup, fgate, hidden = prep(order, saved_gate[:, 0, 0, 0], saved_up[:, 0, 0, 0])

    wg_near = near(tie(wg_own, hidden, *wd_near), inner)

    edge = jnp.logical_or(section == 0, section == 3)
    keep_edge = edge.astype(I32).reshape(1)
    old = cur
    moves = [[(0, 1), (3, 2)], [(1, 2), (2, 1)], [(2, 3), (1, 0)]]
    results = []
    for step in range(4):
        at = step // 2
        keep = keep_edge if step == 1 else 1 - keep_edge if step == 3 else 0 * keep_edge
        outgoing = pre(keep, tgt_t[at], wts_t[at], old, cur)
        old = cur
        buf = exchange(outgoing)
        if step == 0:
            halves = tie(wd_near[0], buf)[:128], tie(wd_near[1], buf)[128:]
            wd_outer = (wd_own,) + wd_near + hop(*halves, outer)
            dgu = hidden_pass(at, me, buf, fup, fgate, wd_outer)
            dgu_near = near(tie(dgu, *wg_near), outer)
            dgu_far = far(*dgu_near, outer)
            sent = own_grads(me, dgu, *dgu_near, *dgu_far, wg_own, wu_own)
            wd = (wd_own,) + wd_near + hop(*[tie(h, dgu) for h in halves], inner)
            wg = (wg_own,) + wg_near + far(*wg_near, inner)
            sent = tie(sent, *wd, *wg)
            wu_full = gather(tie(wu_own, sent))
            home = lax.all_to_all(
                sent.reshape(4 * EXP, 8, PCH), ("dp", "expert"), split_axis=0, concat_axis=0, tiled=True
            ).reshape(4, MAIN, PCH)
            result = post(tgt[at], cur, home)
        else:
            if step == 1:
                wg_full = (gather(tie(wg_own, buf)),)
                all_first = gather(buf)
                hidden_all = lax.all_gather(tie(hidden, buf), "dp", axis=0)
                part, du = front_pass(at, me, buf, fup, fgate, wd, wg)
                packed = back_pass(du, part, wu_full)
            elif step == 2:
                packed = expert_pass(at, me, buf, fup, fgate, wd, wg, wu_full)
            else:
                all_second = gather(buf)
                packed = expert_pass(at, me, buf, fup, fgate, wd_outer, wg_full, wu_full)
            result = post(tgt[at], cur, exchange(packed))
        results.append(result)
        if step < 3:
            cur = lax.ppermute(result, "pipe", moves[step])

    res_first = jnp.where(edge, results[0], results[1])
    res_second = jnp.where(edge, results[3], results[2])
    input_grads = jnp.where(
        first_up, jnp.stack([res_second, res_first]), jnp.stack([res_first, res_second])
    )[:, None]

    hidden_mine = lax.dynamic_slice_in_dim(hidden_all, dp * 256, 256, axis=3)
    hidden_t = hidden_mine.transpose(1, 3, 0, 2).reshape(2, 256, 4 * SLOTS)
    down_grads = down_last(hidden_t[1], all_second, down_first(hidden_t[0], all_first))
    return input_grads, down_grads[None, None]


def solution(mesh):
    return jax.shard_map(
        per_device,
        mesh=mesh,
        in_specs=(
            P(None, ("expert", "dp"), None),
            P(None, "pipe", ("expert", "dp"), None),
            P(None, "pipe", ("expert", "dp"), None),
            P(None, "pipe", "dp", "expert", None, None),
            P(None, "pipe", "dp", "expert", None, None),
            P("pipe", "expert", "dp", None),
            P("pipe", "expert", "dp", None),
            P("pipe", "expert", "dp", None),
        ),
        out_specs=(P(None, "pipe", ("expert", "dp"), None), P("pipe", "expert", "dp", None)),
        check_vma=False,
    )
```

```python
import functools
import jax
import jax.numpy as jnp
from jax import lax
from jax.experimental import pallas as pl
from jax.experimental.pallas import tpu as pltpu
from jax.sharding import PartitionSpec as P

BF = jnp.bfloat16
F32 = jnp.float32
I32 = jnp.int32
D = 3584
FF = 1024
TOK = 64
EXP = 16
CAP = 9
SLOTS = 144
MAIN = 128
CH = 896
PCH = 1024
NCH = 4
PIECES = 7
NT = (((1,), (1,)), ((), ()))
NN = (((1,), (0,)), ((), ()))


IN_HBM = pl.BlockSpec(memory_space=pl.ANY)
IN_SMEM = pl.BlockSpec(memory_space=pltpu.SMEM)
IN_VMEM = pl.BlockSpec(memory_space=pltpu.VMEM)


def dot(a, b, dims=NN):
    return lax.dot_general(a, b, dims, preferred_element_type=F32)


def ones_where(mask):
    return jnp.where(mask, 1.0, 0.0).astype(BF)


def prep_kernel(order_ref, gate_ref, up_ref, fup_ref, fgate_ref, hidden_ref):
    row = lax.broadcasted_iota(I32, (SLOTS, SLOTS), 0)
    col = lax.broadcasted_iota(I32, (SLOTS, SLOTS), 1)
    slot = jnp.where(row < MAIN, (row >> 3) * CAP + (row & 7), (row - MAIN) * CAP + 8)
    perm = ones_where(col == slot)
    gate = dot(perm, gate_ref[0])
    up = dot(perm, up_ref[0])
    sig = 1.0 / (1.0 + jnp.exp(-gate))
    act = gate * sig
    fup_ref[0] = act
    fgate_ref[0] = up * sig * (1.0 + gate * (1.0 - sig))
    hidden_ref[0] = (act * up).astype(BF)


def prep(order, gate, up):
    spec_in = pl.BlockSpec((1, SLOTS, FF), lambda i, o: (o[i], 0, 0))
    spec_out = pl.BlockSpec((1, SLOTS, FF), lambda i, o: (i, 0, 0))
    return pl.pallas_call(
        prep_kernel,
        out_shape=(
            jax.ShapeDtypeStruct((2, SLOTS, FF), F32),
            jax.ShapeDtypeStruct((2, SLOTS, FF), F32),
            jax.ShapeDtypeStruct((2, SLOTS, FF), BF),
        ),
        grid_spec=pltpu.PrefetchScalarGridSpec(
            num_scalar_prefetch=1,
            grid=(2,),
            in_specs=[spec_in, spec_in],
            out_specs=[spec_out, spec_out, spec_out],
        ),
        compiler_params=pltpu.CompilerParams(vmem_limit_bytes=24 << 20),
        cost_estimate=pl.CostEstimate(flops=170_000_000, bytes_accessed=4_700_000, transcendentals=300_000),
        name="prep",
    )(order, gate, up)


def pre_kernel(pick_ref, t_ref, w_ref, old_ref, new_ref, out_ref):
    keep = pick_ref[0] > 0
    c = lax.broadcasted_iota(I32, (MAIN, TOK), 0)
    e9 = (c >> 3) * CAP
    t0 = t_ref[0:1, :]
    t1 = t_ref[1:2, :]
    w0 = w_ref[0:1, :]
    w1 = w_ref[1:2, :]

    def pick(slot):
        m0 = t0 == slot
        m1 = t1 == slot
        scale = jnp.sum(jnp.where(m0, w0, 0.0) + jnp.where(m1, w1, 0.0), axis=1, keepdims=True)
        return ones_where(jnp.logical_or(m0, m1)), scale

    main, scale_main = pick(e9 + (c & 7))
    last, scale_last = pick(e9 + 8)
    piece = lax.broadcasted_iota(I32, (MAIN, 128), 0) & 7
    for j in range(NCH):
        cols = slice(j * CH, (j + 1) * CH)
        x = jnp.where(keep, old_ref[:, cols], new_ref[:, cols])
        out_ref[:, j * PCH : j * PCH + CH] = (dot(main, x) * scale_main).astype(BF)
        full = dot(last, x)
        part = jnp.zeros((MAIN, 128), F32)
        for k in range(PIECES):
            part = jnp.where(piece == k, full[:, k * 128 : (k + 1) * 128], part)
        out_ref[:, j * PCH + CH : (j + 1) * PCH] = (part * scale_last).astype(BF)


def pre(keep, targets_t, weights_t, old, new):
    return pl.pallas_call(
        pre_kernel,
        in_specs=[IN_SMEM] + [IN_VMEM] * 4,
        out_shape=jax.ShapeDtypeStruct((MAIN, NCH * PCH), BF),
        compiler_params=pltpu.CompilerParams(vmem_limit_bytes=16 << 20),
        cost_estimate=pl.CostEstimate(flops=120_000_000, bytes_accessed=1_600_000, transcendentals=0),
        name="pre",
    )(keep, targets_t, weights_t, old, new)


def post_kernel(t_ref, cur_ref, buf_ref, out_ref):
    c = lax.broadcasted_iota(I32, (TOK, MAIN), 1)
    e9 = (c >> 3) * CAP
    s = c & 7
    t0 = t_ref[:, 0:1]
    t1 = t_ref[:, 1:2]

    def pick(slot):
        return jnp.logical_or(t0 == slot, t1 == slot)

    main = ones_where(pick(e9 + s))
    last = pick(e9 + 8)
    tail = jnp.concatenate(
        [ones_where(jnp.logical_and(last, s == k)) for k in range(PIECES)], axis=0
    )
    for j in range(NCH):
        if len(buf_ref.shape) == 3:
            packed = buf_ref[j]
        else:
            packed = buf_ref[:, j * PCH : (j + 1) * PCH]
        acc = dot(main, packed[:, :CH])
        nin = dot(tail, packed[:, CH:])
        for k in range(PIECES):
            lo = j * CH + k * 128
            out_ref[:, lo : lo + 128] = (
                cur_ref[:, lo : lo + 128].astype(F32)
                + (acc[:, k * 128 : (k + 1) * 128] + nin[k * TOK : (k + 1) * TOK, :])
            ).astype(BF)


def post(targets, cur, buf):
    return pl.pallas_call(
        post_kernel,
        out_shape=jax.ShapeDtypeStruct((TOK, D), BF),
        compiler_params=pltpu.CompilerParams(vmem_limit_bytes=16 << 20),
        cost_estimate=pl.CostEstimate(flops=120_000_000, bytes_accessed=2_000_000, transcendentals=0),
        name="post",
    )(targets, cur, buf)


def unpack_rows(buf_ref, rows_ref):
    r = lax.broadcasted_iota(I32, (128, MAIN), 0)
    c = lax.broadcasted_iota(I32, (128, MAIN), 1)
    spread = ones_where(c == (r & 15) * 8 + (r >> 4))
    for j in range(NCH):
        rows_ref[0:MAIN, j * CH : (j + 1) * CH] = buf_ref[:, j * PCH : j * PCH + CH]
        nin = dot(spread, buf_ref[:, j * PCH + CH : (j + 1) * PCH]).astype(BF)
        for k in range(PIECES):
            lo = j * CH + k * 128
            rows_ref[MAIN:SLOTS, lo : lo + 128] = nin[k * 16 : (k + 1) * 16, :]


def put_chunk(grads, out_ref, lead, base):
    c = lax.broadcasted_iota(I32, (MAIN, 128), 0)
    r = lax.broadcasted_iota(I32, (MAIN, 128), 1)
    fold = ones_where(r == (c & 7) * 16 + (c >> 3))
    pieces = [grads[MAIN:SLOTS, k * 128 : (k + 1) * 128] for k in range(PIECES)]
    pieces.append(jnp.zeros((16, 128), BF))
    tail = dot(fold, jnp.concatenate(pieces, axis=0)).astype(BF)
    if lead is None:
        out_ref[:, pl.ds(base, CH)] = grads[0:MAIN]
        out_ref[:, pl.ds(base + CH, 128)] = tail
    else:
        out_ref[lead, :, 0:CH] = grads[0:MAIN]
        out_ref[lead, :, CH:PCH] = tail


def hidden_part(rows_ref, wd, fup_ref, fgate_ref, lo, width):
    d_hidden = dot(rows_ref[...], wd, NT)
    cols = pl.ds(lo, width)
    return (d_hidden * fgate_ref[:, cols]).astype(BF), (d_hidden * fup_ref[:, cols]).astype(BF)


def halves_plan(shard):
    half = shard // 2
    pieces = [(0, 0, shard)]
    groups = [(0, [0])]
    for shift, parts in ((3, False), (1, False), (2, True)):
        mine = []
        for row, width in ((0, half), (half, half)) if parts else ((0, shard),):
            mine.append(len(pieces))
            pieces.append((shift, row, width))
        groups.append((shift, mine))
    return pieces, groups


class Stream:
    def __init__(self, sems, ahead):
        self.sems, self.ahead, self.todo, self.flying, self.done = sems, ahead, [], [], 0

    def add(self, src, dst):
        self.todo.append((src, dst))
        return len(self.todo) - 1

    def start(self, upto):
        while len(self.flying) < min(upto, len(self.todo)):
            n = len(self.flying)
            copy = pltpu.make_async_copy(*self.todo[n], self.sems.at[n])
            copy.start()
            self.flying.append(copy)

    def wait(self, n):
        self.start(n + 1 + self.ahead)
        while self.done <= n:
            self.flying[self.done].wait()
            self.done += 1


def hidden_stage(stream, groups, ids, me, rows_ref, wd_ref, fup_ref, fgate_ref, store):
    for n, (shift, members) in enumerate(groups):
        for m in members:
            stream.wait(ids[m])
        lo = pl.multiple_of(((me + shift) & 3) * 256, 128)
        dg, du = hidden_part(rows_ref, wd_ref[n * 256 : (n + 1) * 256], fup_ref, fgate_ref, lo, 256)
        store(lo, dg, du)


def add_shards(stream, srcs, pieces, dst_ref):
    at = 0
    ids = []
    for src, (_, _, width) in zip(srcs, pieces):
        ids.append(stream.add(src, dst_ref.at[pl.ds(at, width)]))
        at += width
    return ids


def hidden_kernel(at_dir, me_ref, buf_hbm, fup_hbm, fgate_hbm, *rest):
    pieces, groups = halves_plan(256)
    wd_refs, rest = rest[: len(pieces)], rest[len(pieces) :]
    dgu_ref, buf_ref, rows_ref, wd_ref, fup_ref, fgate_ref, sems = rest
    stream = Stream(sems, 4)
    first = stream.add(buf_hbm, buf_ref)
    ids = add_shards(stream, wd_refs[:1], pieces[:1], wd_ref)
    stream.add(fup_hbm.at[at_dir], fup_ref)
    act = stream.add(fgate_hbm.at[at_dir], fgate_ref)
    ids += add_shards(stream, wd_refs[1:], pieces[1:], wd_ref.at[pl.ds(256, FF - 256)])
    stream.wait(first)
    unpack_rows(buf_ref, rows_ref)
    stream.wait(act)

    def store(lo, dg, du):
        dgu_ref[0, :, pl.ds(lo, 256)] = dg
        dgu_ref[1, :, pl.ds(lo, 256)] = du

    hidden_stage(stream, groups, ids, me_ref[0], rows_ref, wd_ref, fup_ref, fgate_ref, store)


def hidden_pass(at_dir, me, buf, fup, fgate, wd):
    return pl.pallas_call(
        functools.partial(hidden_kernel, at_dir),
        in_specs=[IN_SMEM] + [IN_HBM] * (3 + len(wd)),
        out_specs=IN_VMEM,
        out_shape=jax.ShapeDtypeStruct((2, SLOTS, FF), BF),
        scratch_shapes=[
            pltpu.VMEM((MAIN, NCH * PCH), BF),
            pltpu.VMEM((SLOTS, D), BF),
            pltpu.VMEM((FF, D), BF),
            pltpu.VMEM((SLOTS, FF), F32),
            pltpu.VMEM((SLOTS, FF), F32),
            pltpu.SemaphoreType.DMA((3 + len(wd),)),
        ],
        compiler_params=pltpu.CompilerParams(vmem_limit_bytes=60 << 20),
        cost_estimate=pl.CostEstimate(flops=1_060_000_000, bytes_accessed=11_000_000, transcendentals=0),
        name="hidden_pass",
    )(me, buf, fup, fgate, *wd)


def own_grads_kernel(me_ref, own, left, right, far, wg_hbm, wu_hbm, out_hbm, out_ref, d_ref, wg_ref, wu_ref, sems, out_sems):
    srcs = [own, left, right, far]
    stream = Stream(sems, 10)
    stream.add(wg_hbm, wg_ref)
    for n in range(4):
        stream.add(srcs[n].at[0], d_ref.at[0, pl.ds(n * SLOTS, SLOTS)])
    stream.add(wu_hbm, wu_ref)
    for n in range(4):
        stream.add(srcs[n].at[1], d_ref.at[1, pl.ds(n * SLOTS, SLOTS)])
    stream.wait(4)
    total = dot(d_ref[0], wg_ref[...], NT)
    stream.wait(9)
    total = (total + dot(d_ref[1], wu_ref[...], NT)).astype(BF)
    outs = []
    for n, shift in enumerate((0, 3, 1, 2)):
        put_chunk(total[n * SLOTS : (n + 1) * SLOTS], out_ref, n, None)
        outs.append(pltpu.make_async_copy(out_ref.at[n], out_hbm.at[(me_ref[0] + shift) & 3], out_sems.at[n]))
        outs[-1].start()
    for copy in outs:
        copy.wait()


def own_grads(me, own, left, right, far, wg, wu):
    return pl.pallas_call(
        own_grads_kernel,
        in_specs=[IN_SMEM] + [IN_HBM] * 6,
        out_specs=IN_HBM,
        out_shape=jax.ShapeDtypeStruct((4, MAIN, PCH), BF),
        scratch_shapes=[
            pltpu.VMEM((4, MAIN, PCH), BF),
            pltpu.VMEM((2, 4 * SLOTS, FF), BF),
            pltpu.VMEM((CH, FF), BF),
            pltpu.VMEM((CH, FF), BF),
            pltpu.SemaphoreType.DMA((10,)),
            pltpu.SemaphoreType.DMA((4,)),
        ],
        compiler_params=pltpu.CompilerParams(vmem_limit_bytes=60 << 20),
        cost_estimate=pl.CostEstimate(flops=2_120_000_000, bytes_accessed=8_000_000, transcendentals=0),
        name="own_grads",
    )(me, own, left, right, far, wg, wu)


def expert_kernel(at_dir, whole, me_ref, buf_hbm, fup_hbm, fgate_hbm, *rest):
    pieces, groups = halves_plan(256)
    wd_refs, rest = rest[: len(pieces)], rest[len(pieces) :]
    me = me_ref[0]
    gpieces, ggroups = halves_plan(CH)
    count = 1 if whole else len(gpieces)
    g_src, wu_full, rest = rest[:count], rest[count], rest[count + 1 :]
    if whole:
        gpieces, ggroups = [(k, 0, CH) for k in range(4)], [(k, [k]) for k in range(4)]
        starts = [k * CH for k in range(4)]
        g_src = [g_src[0].at[pl.ds(row, CH)] for row in starts]
    else:
        starts = [pl.multiple_of(((me + shift) & 3) * CH + row, 64) for shift, row, _ in gpieces]
    u_src = [wu_full.at[pl.ds(row, width)] for row, (_, _, width) in zip(starts, gpieces)]
    out_ref, buf_ref, rows_ref, wd_ref, wg_ref, wu_ref, fup_ref, fgate_ref, dg_ref, du_ref, sems = rest
    stream = Stream(sems, 4)
    first = stream.add(buf_hbm, buf_ref)
    ids = add_shards(stream, wd_refs[:1], pieces[:1], wd_ref)
    stream.add(fup_hbm.at[at_dir], fup_ref)
    act = stream.add(fgate_hbm.at[at_dir], fgate_ref)
    ids += add_shards(stream, wd_refs[1:], pieces[1:], wd_ref.at[pl.ds(256, FF - 256)])
    grad_ids = []
    at = 0
    for n, (_, _, width) in enumerate(gpieces):
        place = pl.ds(at, width)
        grad_ids.append((stream.add(g_src[n], wg_ref.at[place]), stream.add(u_src[n], wu_ref.at[place])))
        at += width
    stream.wait(first)
    unpack_rows(buf_ref, rows_ref)
    stream.wait(act)

    def store(lo, dg, du):
        dg_ref[:, pl.ds(lo, 256)] = dg
        du_ref[:, pl.ds(lo, 256)] = du

    hidden_stage(stream, groups, ids, me, rows_ref, wd_ref, fup_ref, fgate_ref, store)
    for n, (shift, members) in enumerate(ggroups):
        for m in members:
            stream.wait(grad_ids[m][1])
        at = slice(n * CH, (n + 1) * CH)
        total = dot(dg_ref[...], wg_ref[at], NT) + dot(du_ref[...], wu_ref[at], NT)
        base = shift * PCH if whole else pl.multiple_of(((me + shift) & 3) * PCH, 128)
        put_chunk(total.astype(BF), out_ref, None, base)


def expert_pass(at_dir, me, buf, fup, fgate, wd, wg, wu):
    whole = len(wg) == 1
    copies = 3 + len(wd) + 2 * (4 if whole else len(wg))
    return pl.pallas_call(
        functools.partial(expert_kernel, at_dir, whole),
        in_specs=[IN_SMEM] + [IN_HBM] * (4 + len(wd) + len(wg)),
        out_specs=IN_VMEM,
        out_shape=jax.ShapeDtypeStruct((MAIN, NCH * PCH), BF),
        scratch_shapes=[
            pltpu.VMEM((MAIN, NCH * PCH), BF),
            pltpu.VMEM((SLOTS, D), BF),
            pltpu.VMEM((FF, D), BF),
            pltpu.VMEM((D, FF), BF),
            pltpu.VMEM((D, FF), BF),
            pltpu.VMEM((SLOTS, FF), F32),
            pltpu.VMEM((SLOTS, FF), F32),
            pltpu.VMEM((SLOTS, FF), BF),
            pltpu.VMEM((SLOTS, FF), BF),
            pltpu.SemaphoreType.DMA((copies,)),
        ],
        compiler_params=pltpu.CompilerParams(vmem_limit_bytes=60 << 20),
        cost_estimate=pl.CostEstimate(flops=3_200_000_000, bytes_accessed=28_000_000, transcendentals=0),
        name="expert_pass",
    )(me, buf, fup, fgate, *wd, *wg, wu)


def front_kernel(at_dir, me_ref, buf_hbm, fup_hbm, fgate_hbm, *rest):
    pieces, groups = halves_plan(256)
    gpieces, ggroups = halves_plan(CH)
    wd_refs, wg_refs, rest = rest[:5], rest[5:10], rest[10:]
    (
        part_hbm, du_ref, buf_ref, rows_ref, wd_ref, wg_ref, fup_ref, fgate_ref, dg_ref, part_ref,
        sems, out_sems,
    ) = rest
    me = me_ref[0]
    stream = Stream(sems, 4)
    first = stream.add(buf_hbm, buf_ref)
    ids = add_shards(stream, wd_refs[:1], pieces[:1], wd_ref)
    stream.add(fup_hbm.at[at_dir], fup_ref)
    act = stream.add(fgate_hbm.at[at_dir], fgate_ref)
    ids += add_shards(stream, wd_refs[1:], pieces[1:], wd_ref.at[pl.ds(256, FF - 256)])
    grad_ids = add_shards(stream, wg_refs, gpieces, wg_ref)
    stream.wait(first)
    unpack_rows(buf_ref, rows_ref)
    stream.wait(act)

    def store(lo, dg, du):
        dg_ref[:, pl.ds(lo, 256)] = dg
        du_ref[:, pl.ds(lo, 256)] = du

    hidden_stage(stream, groups, ids, me, rows_ref, wd_ref, fup_ref, fgate_ref, store)
    outs = []
    for n, (shift, members) in enumerate(ggroups):
        for m in members:
            stream.wait(grad_ids[m])
        part_ref[n] = dot(dg_ref[...], wg_ref[n * CH : (n + 1) * CH], NT)
        outs.append(pltpu.make_async_copy(part_ref.at[n], part_hbm.at[(me + shift) & 3], out_sems.at[n]))
        outs[-1].start()
    for copy in outs:
        copy.wait()


def front_pass(at_dir, me, buf, fup, fgate, wd, wg):
    return pl.pallas_call(
        functools.partial(front_kernel, at_dir),
        in_specs=[IN_SMEM] + [IN_HBM] * 13,
        out_specs=[IN_HBM, IN_VMEM],
        out_shape=(
            jax.ShapeDtypeStruct((NCH, SLOTS, CH), F32),
            jax.ShapeDtypeStruct((SLOTS, FF), BF),
        ),
        scratch_shapes=[
            pltpu.VMEM((MAIN, NCH * PCH), BF),
            pltpu.VMEM((SLOTS, D), BF),
            pltpu.VMEM((FF, D), BF),
            pltpu.VMEM((D, FF), BF),
            pltpu.VMEM((SLOTS, FF), F32),
            pltpu.VMEM((SLOTS, FF), F32),
            pltpu.VMEM((SLOTS, FF), BF),
            pltpu.VMEM((NCH, SLOTS, CH), F32),
            pltpu.SemaphoreType.DMA((13,)),
            pltpu.SemaphoreType.DMA((NCH,)),
        ],
        compiler_params=pltpu.CompilerParams(vmem_limit_bytes=60 << 20),
        cost_estimate=pl.CostEstimate(flops=2_100_000_000, bytes_accessed=20_000_000, transcendentals=0),
        name="front_pass",
    )(me, buf, fup, fgate, *wd, *wg)


def back_kernel(du_hbm, part_hbm, wu_hbm, out_ref, du_ref, part_ref, wu_ref, sems):
    stream = Stream(sems, 4)
    stream.add(du_hbm, du_ref)
    for k in range(NCH):
        stream.add(wu_hbm.at[pl.ds(k * CH, CH)], wu_ref.at[k])
        stream.add(part_hbm.at[k], part_ref.at[k])
    for k in range(NCH):
        stream.wait(2 * k + 2)
        total = part_ref[k] + dot(du_ref[...], wu_ref[k], NT)
        put_chunk(total.astype(BF), out_ref, None, k * PCH)


def back_pass(du, part, wu):
    return pl.pallas_call(
        back_kernel,
        in_specs=[IN_HBM] * 3,
        out_specs=IN_VMEM,
        out_shape=jax.ShapeDtypeStruct((MAIN, NCH * PCH), BF),
        scratch_shapes=[
            pltpu.VMEM((SLOTS, FF), BF),
            pltpu.VMEM((NCH, SLOTS, CH), F32),
            pltpu.VMEM((NCH, CH, FF), BF),
            pltpu.SemaphoreType.DMA((1 + 2 * NCH,)),
        ],
        compiler_params=pltpu.CompilerParams(vmem_limit_bytes=60 << 20),
        cost_estimate=pl.CostEstimate(flops=1_060_000_000, bytes_accessed=10_000_000, transcendentals=0),
        name="back_pass",
    )(du, part, wu)


def down_term(h_ref, buf_ref, rows_ref):
    r = lax.broadcasted_iota(I32, (128, MAIN), 0)
    c = lax.broadcasted_iota(I32, (128, MAIN), 1)
    spread = ones_where(c == (r & 15) * 8 + (r >> 4))
    for rep in range(4):
        lo = rep * SLOTS
        block = slice(rep * MAIN, (rep + 1) * MAIN)
        rows_ref[lo : lo + MAIN, :] = buf_ref[block, 0:CH]
        nin = dot(spread, buf_ref[block, CH:PCH]).astype(BF)
        for k in range(PIECES):
            rows_ref[lo + MAIN : lo + SLOTS, k * 128 : (k + 1) * 128] = nin[k * 16 : (k + 1) * 16, :]
    return dot(h_ref[...], rows_ref[...])


def down_first_kernel(h_ref, buf_ref, out_ref, rows_ref):
    out_ref[...] = down_term(h_ref, buf_ref, rows_ref)


def down_first(h, buf):
    return pl.pallas_call(
        down_first_kernel,
        grid=(NCH,),
        in_specs=[
            pl.BlockSpec((256, 4 * SLOTS), lambda j: (0, 0)),
            pl.BlockSpec((4 * MAIN, PCH), lambda j: (0, j)),
        ],
        out_specs=pl.BlockSpec((256, CH), lambda j: (0, j)),
        out_shape=jax.ShapeDtypeStruct((256, D), F32),
        scratch_shapes=[pltpu.VMEM((4 * SLOTS, CH), BF)],
        compiler_params=pltpu.CompilerParams(vmem_limit_bytes=60 << 20),
        cost_estimate=pl.CostEstimate(flops=1_060_000_000, bytes_accessed=8_000_000, transcendentals=0),
        name="down_first",
    )(h, buf)


def down_last_kernel(h_hbm, buf_hbm, sum_hbm, out_hbm, h_ref, buf_ref, sum_ref, out_ref, rows_ref, sems, out_sems):
    stream = Stream(sems, 9)
    stream.add(h_hbm, h_ref)
    for j in range(NCH):
        stream.add(buf_hbm.at[:, pl.ds(j * PCH, PCH)], buf_ref.at[j])
        stream.add(sum_hbm.at[:, pl.ds(j * CH, CH)], sum_ref.at[j])
    outs = []
    for j in range(NCH):
        stream.wait(2 + 2 * j)
        out_ref[j] = (sum_ref[j] + down_term(h_ref, buf_ref.at[j], rows_ref.at[j % 2])).astype(BF)
        outs.append(pltpu.make_async_copy(out_ref.at[j], out_hbm.at[:, pl.ds(j * CH, CH)], out_sems.at[j]))
        outs[-1].start()
    for copy in outs:
        copy.wait()


def down_last(h, buf, total):
    return pl.pallas_call(
        down_last_kernel,
        in_specs=[IN_HBM] * 3,
        out_specs=IN_HBM,
        out_shape=jax.ShapeDtypeStruct((256, D), BF),
        scratch_shapes=[
            pltpu.VMEM((256, 4 * SLOTS), BF),
            pltpu.VMEM((NCH, 4 * MAIN, PCH), BF),
            pltpu.VMEM((NCH, 256, CH), F32),
            pltpu.VMEM((NCH, 256, CH), BF),
            pltpu.VMEM((2, 4 * SLOTS, CH), BF),
            pltpu.SemaphoreType.DMA((9,)),
            pltpu.SemaphoreType.DMA((NCH,)),
        ],
        compiler_params=pltpu.CompilerParams(vmem_limit_bytes=60 << 20),
        cost_estimate=pl.CostEstimate(flops=1_060_000_000, bytes_accessed=10_000_000, transcendentals=0),
        name="down_last",
    )(h, buf, total)


def exchange(buf):
    return lax.all_to_all(
        buf.reshape(EXP, 8, NCH * PCH), "expert", split_axis=0, concat_axis=0, tiled=True
    ).reshape(MAIN, NCH * PCH)


def slot_targets(routes):
    flat = routes.reshape(2, TOK * 2)
    n = TOK * 2
    row = lax.broadcasted_iota(I32, (n, n), 0)
    col = lax.broadcasted_iota(I32, (n, n), 1)
    same = jnp.logical_and(flat[:, :, None] == flat[:, None, :], (col < row)[None])
    return (flat * CAP + jnp.sum(same.astype(I32), axis=2)).reshape(2, TOK, 2)


def shift_dp(value, step, sections):
    pairs = [(s * 4 + i, s * 4 + (i + step) % 4) for s in sections for i in range(4)]
    return lax.ppermute(value, ("pipe", "dp"), pairs)


def tie(value, *others):
    return lax.optimization_barrier((value,) + others)[0]


def per_device(
    seed_grads, expert_routes, route_weights, saved_gate, saved_up, w_gate, w_up, w_down
):
    section = lax.axis_index("pipe")
    dp = lax.axis_index("dp").astype(I32)
    me = dp.reshape(1)
    first_up = section < 2
    first = jnp.where(first_up, 1, 0).astype(I32)
    order = jnp.stack([first, 1 - first])
    every, outer, inner = (0, 1, 2, 3), (0, 3), (1, 2)

    def gather(x):
        return lax.all_gather(x, "dp", axis=0, tiled=True)

    def near(x, sections):
        return shift_dp(x, 1, sections), shift_dp(x, -1, sections)

    def hop(top, low, sections):
        return shift_dp(top, 1, sections), shift_dp(low, -1, sections)

    def far(left, right, sections):
        half = left.shape[0] // 2
        return hop(left[:half], right[half:], sections)

    wd_own, wg_own, wu_own = w_down[0, 0], w_gate[0, 0], w_up[0, 0]
    wd_near = near(wd_own, every)

    def ordered(x):
        return jnp.where(first_up, x[1], x[0]), jnp.where(first_up, x[0], x[1])

    targets = slot_targets(expert_routes[:, 0])
    tgt = ordered(targets)
    wts = ordered(route_weights[:, 0])
    tgt_t = [t.T for t in tgt]
    wts_t = [w.T for w in wts]
    cur = jnp.where(first_up, seed_grads[1], seed_grads[0])
    fup, fgate, hidden = prep(order, saved_gate[:, 0, 0, 0], saved_up[:, 0, 0, 0])

    wg_near = near(tie(wg_own, hidden, *wd_near), inner)

    edge = jnp.logical_or(section == 0, section == 3)
    keep_edge = edge.astype(I32).reshape(1)
    old = cur
    moves = [[(0, 1), (3, 2)], [(1, 2), (2, 1)], [(2, 3), (1, 0)]]
    results = []
    for step in range(4):
        at = step // 2
        keep = keep_edge if step == 1 else 1 - keep_edge if step == 3 else 0 * keep_edge
        outgoing = pre(keep, tgt_t[at], wts_t[at], old, cur)
        if step == 1:
            outgoing = tie(outgoing, *wg)
        old = cur
        buf = exchange(outgoing)
        if step == 0:
            halves = tie(wd_near[0], buf)[:128], tie(wd_near[1], buf)[128:]
            wd_outer = (wd_own,) + wd_near + hop(*halves, outer)
            dgu = hidden_pass(at, me, buf, fup, fgate, wd_outer)
            ready = tie(dgu, *wg_near)
            others = [shift_dp(ready, step_dp, outer) for step_dp in (1, -1, 2)]
            sent = own_grads(me, dgu, *others, wg_own, wu_own)
            wd = (wd_own,) + wd_near + hop(*halves, inner)
            sent = tie(sent, *wd)
            wu_full = gather(tie(wu_own, sent))
            wg = (wg_own,) + wg_near + far(*[tie(w, sent) for w in wg_near], inner)
            home = lax.all_to_all(
                sent.reshape(4 * EXP, 8, PCH), ("dp", "expert"), split_axis=0, concat_axis=0, tiled=True
            ).reshape(4, MAIN, PCH)
            result = post(tgt[at], cur, home)
        else:
            if step == 1:
                wg_full = (gather(tie(wg_own, buf)),)
                all_first = gather(buf)
                hidden_all = lax.all_gather(tie(hidden, buf), "dp", axis=0)
                part, du = front_pass(at, me, buf, fup, fgate, wd, wg)
                packed = back_pass(du, part, wu_full)
            elif step == 2:
                packed = expert_pass(at, me, buf, fup, fgate, wd, wg, wu_full)
            else:
                all_second = gather(buf)
                packed = expert_pass(at, me, buf, fup, fgate, wd_outer, wg_full, wu_full)
            result = post(tgt[at], cur, exchange(packed))
        results.append(result)
        if step < 3:
            cur = lax.ppermute(result, "pipe", moves[step])

    res_first = jnp.where(edge, results[0], results[1])
    res_second = jnp.where(edge, results[3], results[2])
    input_grads = jnp.where(
        first_up, jnp.stack([res_second, res_first]), jnp.stack([res_first, res_second])
    )[:, None]

    hidden_mine = lax.dynamic_slice_in_dim(hidden_all, dp * 256, 256, axis=3)
    hidden_t = hidden_mine.transpose(1, 3, 0, 2).reshape(2, 256, 4 * SLOTS)
    down_grads = down_last(hidden_t[1], all_second, down_first(hidden_t[0], all_first))
    return input_grads, down_grads[None, None]


def solution(mesh):
    return jax.shard_map(
        per_device,
        mesh=mesh,
        in_specs=(
            P(None, ("expert", "dp"), None),
            P(None, "pipe", ("expert", "dp"), None),
            P(None, "pipe", ("expert", "dp"), None),
            P(None, "pipe", "dp", "expert", None, None),
            P(None, "pipe", "dp", "expert", None, None),
            P("pipe", "expert", "dp", None),
            P("pipe", "expert", "dp", None),
            P("pipe", "expert", "dp", None),
        ),
        out_specs=(P(None, "pipe", ("expert", "dp"), None), P("pipe", "expert", "dp", None)),
        check_vma=False,
    )
```

```python
import functools
import jax
import jax.numpy as jnp
from jax import lax
from jax.experimental import pallas as pl
from jax.experimental.pallas import tpu as pltpu
from jax.sharding import PartitionSpec as P

BF = jnp.bfloat16
F32 = jnp.float32
I32 = jnp.int32
D = 3584
FF = 1024
TOK = 64
EXP = 16
CAP = 9
SLOTS = 144
MAIN = 128
CH = 896
PCH = 1024
NCH = 4
PIECES = 7
NT = (((1,), (1,)), ((), ()))
NN = (((1,), (0,)), ((), ()))


IN_HBM = pl.BlockSpec(memory_space=pl.ANY)
IN_SMEM = pl.BlockSpec(memory_space=pltpu.SMEM)
IN_VMEM = pl.BlockSpec(memory_space=pltpu.VMEM)


def dot(a, b, dims=NN):
    return lax.dot_general(a, b, dims, preferred_element_type=F32)


def ones_where(mask):
    return jnp.where(mask, 1.0, 0.0).astype(BF)


def prep_kernel(order_ref, gate_ref, up_ref, fup_ref, fgate_ref, hidden_ref):
    row = lax.broadcasted_iota(I32, (SLOTS, SLOTS), 0)
    col = lax.broadcasted_iota(I32, (SLOTS, SLOTS), 1)
    slot = jnp.where(row < MAIN, (row >> 3) * CAP + (row & 7), (row - MAIN) * CAP + 8)
    perm = ones_where(col == slot)
    gate = dot(perm, gate_ref[0])
    up = dot(perm, up_ref[0])
    sig = 1.0 / (1.0 + jnp.exp(-gate))
    act = gate * sig
    fup_ref[0] = act
    fgate_ref[0] = up * sig * (1.0 + gate * (1.0 - sig))
    hidden_ref[0] = (act * up).astype(BF)


def prep(order, gate, up):
    spec_in = pl.BlockSpec((1, SLOTS, FF), lambda i, o: (o[i], 0, 0))
    spec_out = pl.BlockSpec((1, SLOTS, FF), lambda i, o: (i, 0, 0))
    return pl.pallas_call(
        prep_kernel,
        out_shape=(
            jax.ShapeDtypeStruct((2, SLOTS, FF), F32),
            jax.ShapeDtypeStruct((2, SLOTS, FF), F32),
            jax.ShapeDtypeStruct((2, SLOTS, FF), BF),
        ),
        grid_spec=pltpu.PrefetchScalarGridSpec(
            num_scalar_prefetch=1,
            grid=(2,),
            in_specs=[spec_in, spec_in],
            out_specs=[spec_out, spec_out, spec_out],
        ),
        compiler_params=pltpu.CompilerParams(vmem_limit_bytes=24 << 20),
        cost_estimate=pl.CostEstimate(flops=170_000_000, bytes_accessed=4_700_000, transcendentals=300_000),
        name="prep",
    )(order, gate, up)


def pre_kernel(pick_ref, t_ref, w_ref, old_ref, new_ref, out_ref):
    keep = pick_ref[0] > 0
    c = lax.broadcasted_iota(I32, (MAIN, TOK), 0)
    e9 = (c >> 3) * CAP
    t0 = t_ref[0:1, :]
    t1 = t_ref[1:2, :]
    w0 = w_ref[0:1, :]
    w1 = w_ref[1:2, :]

    def pick(slot):
        m0 = t0 == slot
        m1 = t1 == slot
        scale = jnp.sum(jnp.where(m0, w0, 0.0) + jnp.where(m1, w1, 0.0), axis=1, keepdims=True)
        return ones_where(jnp.logical_or(m0, m1)), scale

    main, scale_main = pick(e9 + (c & 7))
    last, scale_last = pick(e9 + 8)
    piece = lax.broadcasted_iota(I32, (MAIN, 128), 0) & 7
    for j in range(NCH):
        cols = slice(j * CH, (j + 1) * CH)
        x = jnp.where(keep, old_ref[:, cols], new_ref[:, cols])
        out_ref[:, j * PCH : j * PCH + CH] = (dot(main, x) * scale_main).astype(BF)
        full = dot(last, x)
        part = jnp.zeros((MAIN, 128), F32)
        for k in range(PIECES):
            part = jnp.where(piece == k, full[:, k * 128 : (k + 1) * 128], part)
        out_ref[:, j * PCH + CH : (j + 1) * PCH] = (part * scale_last).astype(BF)


def pre(keep, targets_t, weights_t, old, new):
    return pl.pallas_call(
        pre_kernel,
        in_specs=[IN_SMEM] + [IN_VMEM] * 4,
        out_shape=jax.ShapeDtypeStruct((MAIN, NCH * PCH), BF),
        compiler_params=pltpu.CompilerParams(vmem_limit_bytes=16 << 20),
        cost_estimate=pl.CostEstimate(flops=120_000_000, bytes_accessed=1_600_000, transcendentals=0),
        name="pre",
    )(keep, targets_t, weights_t, old, new)


def post_kernel(t_ref, cur_ref, buf_ref, out_ref):
    c = lax.broadcasted_iota(I32, (TOK, MAIN), 1)
    e9 = (c >> 3) * CAP
    s = c & 7
    t0 = t_ref[:, 0:1]
    t1 = t_ref[:, 1:2]

    def pick(slot):
        return jnp.logical_or(t0 == slot, t1 == slot)

    main = ones_where(pick(e9 + s))
    last = pick(e9 + 8)
    tail = jnp.concatenate(
        [ones_where(jnp.logical_and(last, s == k)) for k in range(PIECES)], axis=0
    )
    for j in range(NCH):
        if len(buf_ref.shape) == 3:
            packed = buf_ref[j]
        else:
            packed = buf_ref[:, j * PCH : (j + 1) * PCH]
        acc = dot(main, packed[:, :CH])
        nin = dot(tail, packed[:, CH:])
        for k in range(PIECES):
            lo = j * CH + k * 128
            out_ref[:, lo : lo + 128] = (
                cur_ref[:, lo : lo + 128].astype(F32)
                + (acc[:, k * 128 : (k + 1) * 128] + nin[k * TOK : (k + 1) * TOK, :])
            ).astype(BF)


def post(targets, cur, buf):
    return pl.pallas_call(
        post_kernel,
        out_shape=jax.ShapeDtypeStruct((TOK, D), BF),
        compiler_params=pltpu.CompilerParams(vmem_limit_bytes=16 << 20),
        cost_estimate=pl.CostEstimate(flops=120_000_000, bytes_accessed=2_000_000, transcendentals=0),
        name="post",
    )(targets, cur, buf)


def unpack_rows(buf_ref, rows_ref):
    r = lax.broadcasted_iota(I32, (128, MAIN), 0)
    c = lax.broadcasted_iota(I32, (128, MAIN), 1)
    spread = ones_where(c == (r & 15) * 8 + (r >> 4))
    for j in range(NCH):
        rows_ref[0:MAIN, j * CH : (j + 1) * CH] = buf_ref[:, j * PCH : j * PCH + CH]
        nin = dot(spread, buf_ref[:, j * PCH + CH : (j + 1) * PCH]).astype(BF)
        for k in range(PIECES):
            lo = j * CH + k * 128
            rows_ref[MAIN:SLOTS, lo : lo + 128] = nin[k * 16 : (k + 1) * 16, :]


def put_chunk(grads, out_ref, lead, base):
    c = lax.broadcasted_iota(I32, (MAIN, 128), 0)
    r = lax.broadcasted_iota(I32, (MAIN, 128), 1)
    fold = ones_where(r == (c & 7) * 16 + (c >> 3))
    pieces = [grads[MAIN:SLOTS, k * 128 : (k + 1) * 128] for k in range(PIECES)]
    pieces.append(jnp.zeros((16, 128), BF))
    tail = dot(fold, jnp.concatenate(pieces, axis=0)).astype(BF)
    if lead is None:
        out_ref[:, pl.ds(base, CH)] = grads[0:MAIN]
        out_ref[:, pl.ds(base + CH, 128)] = tail
    else:
        out_ref[lead, :, 0:CH] = grads[0:MAIN]
        out_ref[lead, :, CH:PCH] = tail


def hidden_part(rows_ref, wd, fup_ref, fgate_ref, lo, width):
    d_hidden = dot(rows_ref[...], wd, NT)
    cols = pl.ds(lo, width)
    return (d_hidden * fgate_ref[:, cols]).astype(BF), (d_hidden * fup_ref[:, cols]).astype(BF)


def halves_plan(shard):
    half = shard // 2
    pieces = [(0, 0, shard)]
    groups = [(0, [0])]
    for shift, parts in ((3, False), (1, False), (2, True)):
        mine = []
        for row, width in ((0, half), (half, half)) if parts else ((0, shard),):
            mine.append(len(pieces))
            pieces.append((shift, row, width))
        groups.append((shift, mine))
    return pieces, groups


class Stream:
    def __init__(self, sems, ahead):
        self.sems, self.ahead, self.todo, self.flying, self.done = sems, ahead, [], [], 0

    def add(self, src, dst):
        self.todo.append((src, dst))
        return len(self.todo) - 1

    def start(self, upto):
        while len(self.flying) < min(upto, len(self.todo)):
            n = len(self.flying)
            copy = pltpu.make_async_copy(*self.todo[n], self.sems.at[n])
            copy.start()
            self.flying.append(copy)

    def wait(self, n):
        self.start(n + 1 + self.ahead)
        while self.done <= n:
            self.flying[self.done].wait()
            self.done += 1


def hidden_stage(stream, groups, ids, me, rows_ref, wd_ref, fup_ref, fgate_ref, store):
    for n, (shift, members) in enumerate(groups):
        for m in members:
            stream.wait(ids[m])
        lo = pl.multiple_of(((me + shift) & 3) * 256, 128)
        dg, du = hidden_part(rows_ref, wd_ref[n * 256 : (n + 1) * 256], fup_ref, fgate_ref, lo, 256)
        store(lo, dg, du)


def add_shards(stream, srcs, pieces, dst_ref):
    at = 0
    ids = []
    for src, (_, _, width) in zip(srcs, pieces):
        ids.append(stream.add(src, dst_ref.at[pl.ds(at, width)]))
        at += width
    return ids


def near_kernel(at_dir, me_ref, buf_hbm, fup_hbm, fgate_hbm, *rest):
    wd_refs, (rows_hbm, dgu_hbm, buf_ref, rows_ref, wd_ref, fup_ref, fgate_ref, dgu_ref, sems, out_sems) = rest[:3], rest[3:]
    pieces, groups = halves_plan(256)
    pieces, groups = pieces[:3], groups[:3]
    stream = Stream(sems, 4)
    first = stream.add(buf_hbm, buf_ref)
    ids = add_shards(stream, wd_refs[:1], pieces[:1], wd_ref)
    stream.add(fup_hbm.at[at_dir], fup_ref)
    act = stream.add(fgate_hbm.at[at_dir], fgate_ref)
    ids += add_shards(stream, wd_refs[1:], pieces[1:], wd_ref.at[pl.ds(256, 512)])
    stream.wait(first)
    unpack_rows(buf_ref, rows_ref)
    rows_copy = pltpu.make_async_copy(rows_ref, rows_hbm, out_sems.at[0])
    rows_copy.start()
    stream.wait(act)

    def store(lo, dg, du):
        dgu_ref[0, :, pl.ds(lo, 256)] = dg
        dgu_ref[1, :, pl.ds(lo, 256)] = du

    far = pl.multiple_of(((me_ref[0] + 2) & 3) * 256, 256)
    store(far, jnp.zeros((SLOTS, 256), BF), jnp.zeros((SLOTS, 256), BF))
    hidden_stage(stream, groups, ids, me_ref[0], rows_ref, wd_ref, fup_ref, fgate_ref, store)
    dgu_copy = pltpu.make_async_copy(dgu_ref, dgu_hbm, out_sems.at[1])
    dgu_copy.start()
    rows_copy.wait()
    dgu_copy.wait()


def hidden_near(at_dir, me, buf, fup, fgate, wd):
    return pl.pallas_call(
        functools.partial(near_kernel, at_dir),
        in_specs=[IN_SMEM] + [IN_HBM] * 6,
        out_specs=[IN_HBM, IN_HBM],
        out_shape=(
            jax.ShapeDtypeStruct((SLOTS, D), BF),
            jax.ShapeDtypeStruct((2, SLOTS, FF), BF),
        ),
        scratch_shapes=[
            pltpu.VMEM((MAIN, NCH * PCH), BF),
            pltpu.VMEM((SLOTS, D), BF),
            pltpu.VMEM((768, D), BF),
            pltpu.VMEM((SLOTS, FF), F32),
            pltpu.VMEM((SLOTS, FF), F32),
            pltpu.VMEM((2, SLOTS, FF), BF),
            pltpu.SemaphoreType.DMA((6,)),
            pltpu.SemaphoreType.DMA((2,)),
        ],
        compiler_params=pltpu.CompilerParams(vmem_limit_bytes=60 << 20),
        cost_estimate=pl.CostEstimate(flops=800_000_000, bytes_accessed=10_000_000, transcendentals=0),
        name="hidden_near",
    )(me, buf, fup, fgate, *wd)


def far_kernel(at_dir, me_ref, rows_hbm, fup_hbm, fgate_hbm, near_hbm, top_hbm, low_hbm, dgu_ref, rows_ref, wd_ref, fup_ref, fgate_ref, sems):
    lo = pl.multiple_of(((me_ref[0] + 2) & 3) * 256, 256)
    cols = pl.ds(lo, 256)
    stream = Stream(sems, 7)
    stream.add(rows_hbm, rows_ref)
    stream.add(top_hbm, wd_ref.at[pl.ds(0, 128)])
    stream.add(low_hbm, wd_ref.at[pl.ds(128, 128)])
    stream.add(fup_hbm.at[at_dir, :, cols], fup_ref)
    stream.add(fgate_hbm.at[at_dir, :, cols], fgate_ref)
    last = stream.add(near_hbm, dgu_ref)
    stream.wait(last - 1)
    d_hidden = dot(rows_ref[...], wd_ref[...], NT)
    dg = (d_hidden * fgate_ref[...]).astype(BF)
    du = (d_hidden * fup_ref[...]).astype(BF)
    stream.wait(last)
    dgu_ref[0, :, cols] = dg
    dgu_ref[1, :, cols] = du


def hidden_far(at_dir, me, rows, fup, fgate, near, top, low):
    return pl.pallas_call(
        functools.partial(far_kernel, at_dir),
        in_specs=[IN_SMEM] + [IN_HBM] * 6,
        out_specs=IN_VMEM,
        out_shape=jax.ShapeDtypeStruct((2, SLOTS, FF), BF),
        scratch_shapes=[
            pltpu.VMEM((SLOTS, D), BF),
            pltpu.VMEM((256, D), BF),
            pltpu.VMEM((SLOTS, 256), F32),
            pltpu.VMEM((SLOTS, 256), F32),
            pltpu.SemaphoreType.DMA((6,)),
        ],
        compiler_params=pltpu.CompilerParams(vmem_limit_bytes=60 << 20),
        cost_estimate=pl.CostEstimate(flops=270_000_000, bytes_accessed=5_000_000, transcendentals=0),
        name="hidden_far",
    )(me, rows, fup, fgate, near, top, low)


def own_grads_kernel(me_ref, own, left, right, far, wg_hbm, wu_hbm, out_hbm, out_ref, d_ref, wg_ref, wu_ref, sems, out_sems):
    srcs = [own, left, right, far]
    stream = Stream(sems, 10)
    stream.add(wg_hbm, wg_ref)
    for n in range(4):
        stream.add(srcs[n].at[0], d_ref.at[0, pl.ds(n * SLOTS, SLOTS)])
    stream.add(wu_hbm, wu_ref)
    for n in range(4):
        stream.add(srcs[n].at[1], d_ref.at[1, pl.ds(n * SLOTS, SLOTS)])
    stream.wait(4)
    total = dot(d_ref[0], wg_ref[...], NT)
    stream.wait(9)
    total = (total + dot(d_ref[1], wu_ref[...], NT)).astype(BF)
    outs = []
    for n, shift in enumerate((0, 3, 1, 2)):
        put_chunk(total[n * SLOTS : (n + 1) * SLOTS], out_ref, n, None)
        outs.append(pltpu.make_async_copy(out_ref.at[n], out_hbm.at[(me_ref[0] + shift) & 3], out_sems.at[n]))
        outs[-1].start()
    for copy in outs:
        copy.wait()


def own_grads(me, own, left, right, far, wg, wu):
    return pl.pallas_call(
        own_grads_kernel,
        in_specs=[IN_SMEM] + [IN_HBM] * 6,
        out_specs=IN_HBM,
        out_shape=jax.ShapeDtypeStruct((4, MAIN, PCH), BF),
        scratch_shapes=[
            pltpu.VMEM((4, MAIN, PCH), BF),
            pltpu.VMEM((2, 4 * SLOTS, FF), BF),
            pltpu.VMEM((CH, FF), BF),
            pltpu.VMEM((CH, FF), BF),
            pltpu.SemaphoreType.DMA((10,)),
            pltpu.SemaphoreType.DMA((4,)),
        ],
        compiler_params=pltpu.CompilerParams(vmem_limit_bytes=60 << 20),
        cost_estimate=pl.CostEstimate(flops=2_120_000_000, bytes_accessed=8_000_000, transcendentals=0),
        name="own_grads",
    )(me, own, left, right, far, wg, wu)


def expert_kernel(at_dir, whole, me_ref, buf_hbm, fup_hbm, fgate_hbm, *rest):
    pieces, groups = halves_plan(256)
    wd_refs, rest = rest[: len(pieces)], rest[len(pieces) :]
    me = me_ref[0]
    gpieces, ggroups = halves_plan(CH)
    count = 1 if whole else len(gpieces)
    g_src, wu_full, rest = rest[:count], rest[count], rest[count + 1 :]
    if whole:
        gpieces, ggroups = [(k, 0, CH) for k in range(4)], [(k, [k]) for k in range(4)]
        starts = [k * CH for k in range(4)]
        g_src = [g_src[0].at[pl.ds(row, CH)] for row in starts]
    else:
        starts = [pl.multiple_of(((me + shift) & 3) * CH + row, 64) for shift, row, _ in gpieces]
    u_src = [wu_full.at[pl.ds(row, width)] for row, (_, _, width) in zip(starts, gpieces)]
    out_ref, buf_ref, rows_ref, wd_ref, wg_ref, wu_ref, fup_ref, fgate_ref, dg_ref, du_ref, sems = rest
    stream = Stream(sems, 4)
    first = stream.add(buf_hbm, buf_ref)
    ids = add_shards(stream, wd_refs[:1], pieces[:1], wd_ref)
    stream.add(fup_hbm.at[at_dir], fup_ref)
    act = stream.add(fgate_hbm.at[at_dir], fgate_ref)
    ids += add_shards(stream, wd_refs[1:], pieces[1:], wd_ref.at[pl.ds(256, FF - 256)])
    grad_ids = []
    at = 0
    for n, (_, _, width) in enumerate(gpieces):
        place = pl.ds(at, width)
        grad_ids.append((stream.add(g_src[n], wg_ref.at[place]), stream.add(u_src[n], wu_ref.at[place])))
        at += width
    stream.wait(first)
    unpack_rows(buf_ref, rows_ref)
    stream.wait(act)

    def store(lo, dg, du):
        dg_ref[:, pl.ds(lo, 256)] = dg
        du_ref[:, pl.ds(lo, 256)] = du

    hidden_stage(stream, groups, ids, me, rows_ref, wd_ref, fup_ref, fgate_ref, store)
    for n, (shift, members) in enumerate(ggroups):
        for m in members:
            stream.wait(grad_ids[m][1])
        at = slice(n * CH, (n + 1) * CH)
        total = dot(dg_ref[...], wg_ref[at], NT) + dot(du_ref[...], wu_ref[at], NT)
        base = shift * PCH if whole else pl.multiple_of(((me + shift) & 3) * PCH, 128)
        put_chunk(total.astype(BF), out_ref, None, base)


def expert_pass(at_dir, me, buf, fup, fgate, wd, wg, wu):
    whole = len(wg) == 1
    copies = 3 + len(wd) + 2 * (4 if whole else len(wg))
    return pl.pallas_call(
        functools.partial(expert_kernel, at_dir, whole),
        in_specs=[IN_SMEM] + [IN_HBM] * (4 + len(wd) + len(wg)),
        out_specs=IN_VMEM,
        out_shape=jax.ShapeDtypeStruct((MAIN, NCH * PCH), BF),
        scratch_shapes=[
            pltpu.VMEM((MAIN, NCH * PCH), BF),
            pltpu.VMEM((SLOTS, D), BF),
            pltpu.VMEM((FF, D), BF),
            pltpu.VMEM((D, FF), BF),
            pltpu.VMEM((D, FF), BF),
            pltpu.VMEM((SLOTS, FF), F32),
            pltpu.VMEM((SLOTS, FF), F32),
            pltpu.VMEM((SLOTS, FF), BF),
            pltpu.VMEM((SLOTS, FF), BF),
            pltpu.SemaphoreType.DMA((copies,)),
        ],
        compiler_params=pltpu.CompilerParams(vmem_limit_bytes=60 << 20),
        cost_estimate=pl.CostEstimate(flops=3_200_000_000, bytes_accessed=28_000_000, transcendentals=0),
        name="expert_pass",
    )(me, buf, fup, fgate, *wd, *wg, wu)


def front_kernel(at_dir, me_ref, buf_hbm, fup_hbm, fgate_hbm, *rest):
    pieces, groups = halves_plan(256)
    gpieces, ggroups = halves_plan(CH)
    wd_refs, wg_refs, rest = rest[:5], rest[5:10], rest[10:]
    (
        part_hbm, du_ref, buf_ref, rows_ref, wd_ref, wg_ref, fup_ref, fgate_ref, dg_ref, part_ref,
        sems, out_sems,
    ) = rest
    me = me_ref[0]
    stream = Stream(sems, 4)
    first = stream.add(buf_hbm, buf_ref)
    ids = add_shards(stream, wd_refs[:1], pieces[:1], wd_ref)
    stream.add(fup_hbm.at[at_dir], fup_ref)
    act = stream.add(fgate_hbm.at[at_dir], fgate_ref)
    ids += add_shards(stream, wd_refs[1:], pieces[1:], wd_ref.at[pl.ds(256, FF - 256)])
    grad_ids = add_shards(stream, wg_refs, gpieces, wg_ref)
    stream.wait(first)
    unpack_rows(buf_ref, rows_ref)
    stream.wait(act)

    def store(lo, dg, du):
        dg_ref[:, pl.ds(lo, 256)] = dg
        du_ref[:, pl.ds(lo, 256)] = du

    hidden_stage(stream, groups, ids, me, rows_ref, wd_ref, fup_ref, fgate_ref, store)
    outs = []
    for n, (shift, members) in enumerate(ggroups):
        for m in members:
            stream.wait(grad_ids[m])
        part_ref[n] = dot(dg_ref[...], wg_ref[n * CH : (n + 1) * CH], NT)
        outs.append(pltpu.make_async_copy(part_ref.at[n], part_hbm.at[(me + shift) & 3], out_sems.at[n]))
        outs[-1].start()
    for copy in outs:
        copy.wait()


def front_pass(at_dir, me, buf, fup, fgate, wd, wg):
    return pl.pallas_call(
        functools.partial(front_kernel, at_dir),
        in_specs=[IN_SMEM] + [IN_HBM] * 13,
        out_specs=[IN_HBM, IN_VMEM],
        out_shape=(
            jax.ShapeDtypeStruct((NCH, SLOTS, CH), F32),
            jax.ShapeDtypeStruct((SLOTS, FF), BF),
        ),
        scratch_shapes=[
            pltpu.VMEM((MAIN, NCH * PCH), BF),
            pltpu.VMEM((SLOTS, D), BF),
            pltpu.VMEM((FF, D), BF),
            pltpu.VMEM((D, FF), BF),
            pltpu.VMEM((SLOTS, FF), F32),
            pltpu.VMEM((SLOTS, FF), F32),
            pltpu.VMEM((SLOTS, FF), BF),
            pltpu.VMEM((NCH, SLOTS, CH), F32),
            pltpu.SemaphoreType.DMA((13,)),
            pltpu.SemaphoreType.DMA((NCH,)),
        ],
        compiler_params=pltpu.CompilerParams(vmem_limit_bytes=60 << 20),
        cost_estimate=pl.CostEstimate(flops=2_100_000_000, bytes_accessed=20_000_000, transcendentals=0),
        name="front_pass",
    )(me, buf, fup, fgate, *wd, *wg)


def back_kernel(du_hbm, part_hbm, wu_hbm, out_ref, du_ref, part_ref, wu_ref, sems):
    stream = Stream(sems, 4)
    stream.add(du_hbm, du_ref)
    for k in range(NCH):
        stream.add(wu_hbm.at[pl.ds(k * CH, CH)], wu_ref.at[k])
        stream.add(part_hbm.at[k], part_ref.at[k])
    for k in range(NCH):
        stream.wait(2 * k + 2)
        total = part_ref[k] + dot(du_ref[...], wu_ref[k], NT)
        put_chunk(total.astype(BF), out_ref, None, k * PCH)


def back_pass(du, part, wu):
    return pl.pallas_call(
        back_kernel,
        in_specs=[IN_HBM] * 3,
        out_specs=IN_VMEM,
        out_shape=jax.ShapeDtypeStruct((MAIN, NCH * PCH), BF),
        scratch_shapes=[
            pltpu.VMEM((SLOTS, FF), BF),
            pltpu.VMEM((NCH, SLOTS, CH), F32),
            pltpu.VMEM((NCH, CH, FF), BF),
            pltpu.SemaphoreType.DMA((1 + 2 * NCH,)),
        ],
        compiler_params=pltpu.CompilerParams(vmem_limit_bytes=60 << 20),
        cost_estimate=pl.CostEstimate(flops=1_060_000_000, bytes_accessed=10_000_000, transcendentals=0),
        name="back_pass",
    )(du, part, wu)


def down_term(h_ref, buf_ref, rows_ref):
    r = lax.broadcasted_iota(I32, (128, MAIN), 0)
    c = lax.broadcasted_iota(I32, (128, MAIN), 1)
    spread = ones_where(c == (r & 15) * 8 + (r >> 4))
    for rep in range(4):
        lo = rep * SLOTS
        block = slice(rep * MAIN, (rep + 1) * MAIN)
        rows_ref[lo : lo + MAIN, :] = buf_ref[block, 0:CH]
        nin = dot(spread, buf_ref[block, CH:PCH]).astype(BF)
        for k in range(PIECES):
            rows_ref[lo + MAIN : lo + SLOTS, k * 128 : (k + 1) * 128] = nin[k * 16 : (k + 1) * 16, :]
    return dot(h_ref[...], rows_ref[...])


def down_first_kernel(h_ref, buf_ref, out_ref, rows_ref):
    out_ref[...] = down_term(h_ref, buf_ref, rows_ref)


def down_first(h, buf):
    return pl.pallas_call(
        down_first_kernel,
        grid=(NCH,),
        in_specs=[
            pl.BlockSpec((256, 4 * SLOTS), lambda j: (0, 0)),
            pl.BlockSpec((4 * MAIN, PCH), lambda j: (0, j)),
        ],
        out_specs=pl.BlockSpec((256, CH), lambda j: (0, j)),
        out_shape=jax.ShapeDtypeStruct((256, D), F32),
        scratch_shapes=[pltpu.VMEM((4 * SLOTS, CH), BF)],
        compiler_params=pltpu.CompilerParams(vmem_limit_bytes=60 << 20),
        cost_estimate=pl.CostEstimate(flops=1_060_000_000, bytes_accessed=8_000_000, transcendentals=0),
        name="down_first",
    )(h, buf)


def down_last_kernel(h_hbm, buf_hbm, sum_hbm, out_hbm, h_ref, buf_ref, sum_ref, out_ref, rows_ref, sems, out_sems):
    stream = Stream(sems, 9)
    stream.add(h_hbm, h_ref)
    for j in range(NCH):
        stream.add(buf_hbm.at[:, pl.ds(j * PCH, PCH)], buf_ref.at[j])
        stream.add(sum_hbm.at[:, pl.ds(j * CH, CH)], sum_ref.at[j])
    outs = []
    for j in range(NCH):
        stream.wait(2 + 2 * j)
        out_ref[j] = (sum_ref[j] + down_term(h_ref, buf_ref.at[j], rows_ref.at[j % 2])).astype(BF)
        outs.append(pltpu.make_async_copy(out_ref.at[j], out_hbm.at[:, pl.ds(j * CH, CH)], out_sems.at[j]))
        outs[-1].start()
    for copy in outs:
        copy.wait()


def down_last(h, buf, total):
    return pl.pallas_call(
        down_last_kernel,
        in_specs=[IN_HBM] * 3,
        out_specs=IN_HBM,
        out_shape=jax.ShapeDtypeStruct((256, D), BF),
        scratch_shapes=[
            pltpu.VMEM((256, 4 * SLOTS), BF),
            pltpu.VMEM((NCH, 4 * MAIN, PCH), BF),
            pltpu.VMEM((NCH, 256, CH), F32),
            pltpu.VMEM((NCH, 256, CH), BF),
            pltpu.VMEM((2, 4 * SLOTS, CH), BF),
            pltpu.SemaphoreType.DMA((9,)),
            pltpu.SemaphoreType.DMA((NCH,)),
        ],
        compiler_params=pltpu.CompilerParams(vmem_limit_bytes=60 << 20),
        cost_estimate=pl.CostEstimate(flops=1_060_000_000, bytes_accessed=10_000_000, transcendentals=0),
        name="down_last",
    )(h, buf, total)


def exchange(buf):
    return lax.all_to_all(
        buf.reshape(EXP, 8, NCH * PCH), "expert", split_axis=0, concat_axis=0, tiled=True
    ).reshape(MAIN, NCH * PCH)


def slot_targets(routes):
    flat = routes.reshape(2, TOK * 2)
    n = TOK * 2
    row = lax.broadcasted_iota(I32, (n, n), 0)
    col = lax.broadcasted_iota(I32, (n, n), 1)
    same = jnp.logical_and(flat[:, :, None] == flat[:, None, :], (col < row)[None])
    return (flat * CAP + jnp.sum(same.astype(I32), axis=2)).reshape(2, TOK, 2)


def shift_dp(value, step, sections):
    pairs = [(s * 4 + i, s * 4 + (i + step) % 4) for s in sections for i in range(4)]
    return lax.ppermute(value, ("pipe", "dp"), pairs)


def tie(value, *others):
    return lax.optimization_barrier((value,) + others)[0]


def per_device(
    seed_grads, expert_routes, route_weights, saved_gate, saved_up, w_gate, w_up, w_down
):
    section = lax.axis_index("pipe")
    dp = lax.axis_index("dp").astype(I32)
    me = dp.reshape(1)
    first_up = section < 2
    first = jnp.where(first_up, 1, 0).astype(I32)
    order = jnp.stack([first, 1 - first])
    every, outer, inner = (0, 1, 2, 3), (0, 3), (1, 2)

    def gather(x):
        return lax.all_gather(x, "dp", axis=0, tiled=True)

    def near(x, sections):
        return shift_dp(x, 1, sections), shift_dp(x, -1, sections)

    def hop(top, low, sections):
        return shift_dp(top, 1, sections), shift_dp(low, -1, sections)

    def far(left, right, sections):
        half = left.shape[0] // 2
        return hop(left[:half], right[half:], sections)

    wd_own, wg_own, wu_own = w_down[0, 0], w_gate[0, 0], w_up[0, 0]
    wd_near = near(wd_own, every)

    def ordered(x):
        return jnp.where(first_up, x[1], x[0]), jnp.where(first_up, x[0], x[1])

    targets = slot_targets(expert_routes[:, 0])
    tgt = ordered(targets)
    wts = ordered(route_weights[:, 0])
    tgt_t = [t.T for t in tgt]
    wts_t = [w.T for w in wts]
    cur = jnp.where(first_up, seed_grads[1], seed_grads[0])
    fup, fgate, hidden = prep(order, saved_gate[:, 0, 0, 0], saved_up[:, 0, 0, 0])

    wg_near = near(tie(wg_own, hidden, *wd_near), inner)

    edge = jnp.logical_or(section == 0, section == 3)
    keep_edge = edge.astype(I32).reshape(1)
    old = cur
    moves = [[(0, 1), (3, 2)], [(1, 2), (2, 1)], [(2, 3), (1, 0)]]
    results = []
    for step in range(4):
        at = step // 2
        keep = keep_edge if step == 1 else 1 - keep_edge if step == 3 else 0 * keep_edge
        outgoing = pre(keep, tgt_t[at], wts_t[at], old, cur)
        if step == 1:
            outgoing = tie(outgoing, *wg)
        old = cur
        buf = exchange(outgoing)
        if step == 0:
            halves = tie(wd_near[0], buf)[:128], tie(wd_near[1], buf)[128:]
            wd_outer = (wd_own,) + wd_near + hop(*halves, outer)
            rows, dgu_part = hidden_near(at, me, buf, fup, fgate, wd_outer[:3])
            dgu = hidden_far(at, me, rows, fup, fgate, dgu_part, *wd_outer[3:])
            ready = tie(dgu, *wg_near)
            others = [shift_dp(ready, step_dp, outer) for step_dp in (1, -1, 2)]
            sent = own_grads(me, dgu, *others, wg_own, wu_own)
            wd = (wd_own,) + wd_near + hop(*[tie(h, dgu_part) for h in halves], inner)
            sent = tie(sent, *wd)
            wu_full = gather(tie(wu_own, sent))
            wg = (wg_own,) + wg_near + far(*[tie(w, sent) for w in wg_near], inner)
            home = lax.all_to_all(
                sent.reshape(4 * EXP, 8, PCH), ("dp", "expert"), split_axis=0, concat_axis=0, tiled=True
            ).reshape(4, MAIN, PCH)
            result = post(tgt[at], cur, home)
        else:
            if step == 1:
                wg_full = (gather(tie(wg_own, buf)),)
                all_first = gather(buf)
                hidden_all = lax.all_gather(tie(hidden, buf), "dp", axis=0)
                part, du = front_pass(at, me, buf, fup, fgate, wd, wg)
                packed = back_pass(du, part, wu_full)
            elif step == 2:
                packed = expert_pass(at, me, buf, fup, fgate, wd, wg, wu_full)
            else:
                all_second = gather(buf)
                packed = expert_pass(at, me, buf, fup, fgate, wd_outer, wg_full, wu_full)
            result = post(tgt[at], cur, exchange(packed))
        results.append(result)
        if step < 3:
            cur = lax.ppermute(result, "pipe", moves[step])

    res_first = jnp.where(edge, results[0], results[1])
    res_second = jnp.where(edge, results[3], results[2])
    input_grads = jnp.where(
        first_up, jnp.stack([res_second, res_first]), jnp.stack([res_first, res_second])
    )[:, None]

    hidden_mine = lax.dynamic_slice_in_dim(hidden_all, dp * 256, 256, axis=3)
    hidden_t = hidden_mine.transpose(1, 3, 0, 2).reshape(2, 256, 4 * SLOTS)
    down_grads = down_last(hidden_t[1], all_second, down_first(hidden_t[0], all_first))
    return input_grads, down_grads[None, None]


def solution(mesh):
    return jax.shard_map(
        per_device,
        mesh=mesh,
        in_specs=(
            P(None, ("expert", "dp"), None),
            P(None, "pipe", ("expert", "dp"), None),
            P(None, "pipe", ("expert", "dp"), None),
            P(None, "pipe", "dp", "expert", None, None),
            P(None, "pipe", "dp", "expert", None, None),
            P("pipe", "expert", "dp", None),
            P("pipe", "expert", "dp", None),
            P("pipe", "expert", "dp", None),
        ),
        out_specs=(P(None, "pipe", ("expert", "dp"), None), P("pipe", "expert", "dp", None)),
        check_vma=False,
    )
```

```python
import functools
import jax
import jax.numpy as jnp
from jax import lax
from jax.experimental import pallas as pl
from jax.experimental.pallas import tpu as pltpu
from jax.sharding import PartitionSpec as P

BF = jnp.bfloat16
F32 = jnp.float32
I32 = jnp.int32
D = 3584
FF = 1024
TOK = 64
EXP = 16
CAP = 9
SLOTS = 144
MAIN = 128
CH = 896
PCH = 1024
NCH = 4
PIECES = 7
NT = (((1,), (1,)), ((), ()))
NN = (((1,), (0,)), ((), ()))


IN_HBM = pl.BlockSpec(memory_space=pl.ANY)
IN_SMEM = pl.BlockSpec(memory_space=pltpu.SMEM)
IN_VMEM = pl.BlockSpec(memory_space=pltpu.VMEM)


def dot(a, b, dims=NN):
    return lax.dot_general(a, b, dims, preferred_element_type=F32)


def ones_where(mask):
    return jnp.where(mask, 1.0, 0.0).astype(BF)


def prep_kernel(order_ref, gate_ref, up_ref, fup_ref, fgate_ref, hidden_ref):
    row = lax.broadcasted_iota(I32, (SLOTS, SLOTS), 0)
    col = lax.broadcasted_iota(I32, (SLOTS, SLOTS), 1)
    slot = jnp.where(row < MAIN, (row >> 3) * CAP + (row & 7), (row - MAIN) * CAP + 8)
    perm = ones_where(col == slot)
    gate = dot(perm, gate_ref[0])
    up = dot(perm, up_ref[0])
    sig = 1.0 / (1.0 + jnp.exp(-gate))
    act = gate * sig
    fup_ref[0] = act
    fgate_ref[0] = up * sig * (1.0 + gate * (1.0 - sig))
    hidden_ref[0] = (act * up).astype(BF)


def prep(order, gate, up):
    spec_in = pl.BlockSpec((1, SLOTS, FF), lambda i, o: (o[i], 0, 0))
    spec_out = pl.BlockSpec((1, SLOTS, FF), lambda i, o: (i, 0, 0))
    return pl.pallas_call(
        prep_kernel,
        out_shape=(
            jax.ShapeDtypeStruct((2, SLOTS, FF), F32),
            jax.ShapeDtypeStruct((2, SLOTS, FF), F32),
            jax.ShapeDtypeStruct((2, SLOTS, FF), BF),
        ),
        grid_spec=pltpu.PrefetchScalarGridSpec(
            num_scalar_prefetch=1,
            grid=(2,),
            in_specs=[spec_in, spec_in],
            out_specs=[spec_out, spec_out, spec_out],
        ),
        compiler_params=pltpu.CompilerParams(vmem_limit_bytes=24 << 20),
        cost_estimate=pl.CostEstimate(flops=170_000_000, bytes_accessed=4_700_000, transcendentals=300_000),
        name="prep",
    )(order, gate, up)


def pre_kernel(pick_ref, t_ref, w_ref, old_ref, new_ref, out_ref):
    keep = pick_ref[0] > 0
    c = lax.broadcasted_iota(I32, (MAIN, TOK), 0)
    e9 = (c >> 3) * CAP
    t0 = t_ref[0:1, :]
    t1 = t_ref[1:2, :]
    w0 = w_ref[0:1, :]
    w1 = w_ref[1:2, :]

    def pick(slot):
        m0 = t0 == slot
        m1 = t1 == slot
        scale = jnp.sum(jnp.where(m0, w0, 0.0) + jnp.where(m1, w1, 0.0), axis=1, keepdims=True)
        return ones_where(jnp.logical_or(m0, m1)), scale

    main, scale_main = pick(e9 + (c & 7))
    last, scale_last = pick(e9 + 8)
    piece = lax.broadcasted_iota(I32, (MAIN, 128), 0) & 7
    for j in range(NCH):
        cols = slice(j * CH, (j + 1) * CH)
        x = jnp.where(keep, old_ref[:, cols], new_ref[:, cols])
        out_ref[:, j * PCH : j * PCH + CH] = (dot(main, x) * scale_main).astype(BF)
        full = dot(last, x)
        part = jnp.zeros((MAIN, 128), F32)
        for k in range(PIECES):
            part = jnp.where(piece == k, full[:, k * 128 : (k + 1) * 128], part)
        out_ref[:, j * PCH + CH : (j + 1) * PCH] = (part * scale_last).astype(BF)


def pre(keep, targets_t, weights_t, old, new):
    return pl.pallas_call(
        pre_kernel,
        in_specs=[IN_SMEM] + [IN_VMEM] * 4,
        out_shape=jax.ShapeDtypeStruct((MAIN, NCH * PCH), BF),
        compiler_params=pltpu.CompilerParams(vmem_limit_bytes=16 << 20),
        cost_estimate=pl.CostEstimate(flops=120_000_000, bytes_accessed=1_600_000, transcendentals=0),
        name="pre",
    )(keep, targets_t, weights_t, old, new)


def post_kernel(t_ref, cur_ref, buf_ref, out_ref):
    c = lax.broadcasted_iota(I32, (TOK, MAIN), 1)
    e9 = (c >> 3) * CAP
    s = c & 7
    t0 = t_ref[:, 0:1]
    t1 = t_ref[:, 1:2]

    def pick(slot):
        return jnp.logical_or(t0 == slot, t1 == slot)

    main = ones_where(pick(e9 + s))
    last = pick(e9 + 8)
    tail = jnp.concatenate(
        [ones_where(jnp.logical_and(last, s == k)) for k in range(PIECES)], axis=0
    )
    for j in range(NCH):
        if len(buf_ref.shape) == 3:
            packed = buf_ref[j]
        else:
            packed = buf_ref[:, j * PCH : (j + 1) * PCH]
        acc = dot(main, packed[:, :CH])
        nin = dot(tail, packed[:, CH:])
        for k in range(PIECES):
            lo = j * CH + k * 128
            out_ref[:, lo : lo + 128] = (
                cur_ref[:, lo : lo + 128].astype(F32)
                + (acc[:, k * 128 : (k + 1) * 128] + nin[k * TOK : (k + 1) * TOK, :])
            ).astype(BF)


def post(targets, cur, buf):
    return pl.pallas_call(
        post_kernel,
        out_shape=jax.ShapeDtypeStruct((TOK, D), BF),
        compiler_params=pltpu.CompilerParams(vmem_limit_bytes=16 << 20),
        cost_estimate=pl.CostEstimate(flops=120_000_000, bytes_accessed=2_000_000, transcendentals=0),
        name="post",
    )(targets, cur, buf)


def unpack_rows(buf_ref, rows_ref):
    r = lax.broadcasted_iota(I32, (128, MAIN), 0)
    c = lax.broadcasted_iota(I32, (128, MAIN), 1)
    spread = ones_where(c == (r & 15) * 8 + (r >> 4))
    for j in range(NCH):
        rows_ref[0:MAIN, j * CH : (j + 1) * CH] = buf_ref[:, j * PCH : j * PCH + CH]
        nin = dot(spread, buf_ref[:, j * PCH + CH : (j + 1) * PCH]).astype(BF)
        for k in range(PIECES):
            lo = j * CH + k * 128
            rows_ref[MAIN:SLOTS, lo : lo + 128] = nin[k * 16 : (k + 1) * 16, :]


def put_chunk(grads, out_ref, lead, base):
    c = lax.broadcasted_iota(I32, (MAIN, 128), 0)
    r = lax.broadcasted_iota(I32, (MAIN, 128), 1)
    fold = ones_where(r == (c & 7) * 16 + (c >> 3))
    pieces = [grads[MAIN:SLOTS, k * 128 : (k + 1) * 128] for k in range(PIECES)]
    pieces.append(jnp.zeros((16, 128), BF))
    tail = dot(fold, jnp.concatenate(pieces, axis=0)).astype(BF)
    if lead is None:
        out_ref[:, pl.ds(base, CH)] = grads[0:MAIN]
        out_ref[:, pl.ds(base + CH, 128)] = tail
    else:
        out_ref[lead, :, 0:CH] = grads[0:MAIN]
        out_ref[lead, :, CH:PCH] = tail


def hidden_part(rows_ref, wd, fup_ref, fgate_ref, lo, width):
    d_hidden = dot(rows_ref[...], wd, NT)
    cols = pl.ds(lo, width)
    return (d_hidden * fgate_ref[:, cols]).astype(BF), (d_hidden * fup_ref[:, cols]).astype(BF)


def halves_plan(shard):
    half = shard // 2
    pieces = [(0, 0, shard)]
    groups = [(0, [0])]
    for shift, parts in ((3, False), (1, False), (2, True)):
        mine = []
        for row, width in ((0, half), (half, half)) if parts else ((0, shard),):
            mine.append(len(pieces))
            pieces.append((shift, row, width))
        groups.append((shift, mine))
    return pieces, groups


class Stream:
    def __init__(self, sems, ahead):
        self.sems, self.ahead, self.todo, self.flying, self.done = sems, ahead, [], [], 0

    def add(self, src, dst):
        self.todo.append((src, dst))
        return len(self.todo) - 1

    def start(self, upto):
        while len(self.flying) < min(upto, len(self.todo)):
            n = len(self.flying)
            copy = pltpu.make_async_copy(*self.todo[n], self.sems.at[n])
            copy.start()
            self.flying.append(copy)

    def wait(self, n):
        self.start(n + 1 + self.ahead)
        while self.done <= n:
            self.flying[self.done].wait()
            self.done += 1


def hidden_stage(stream, groups, ids, me, rows_ref, wd_ref, fup_ref, fgate_ref, store):
    for n, (shift, members) in enumerate(groups):
        for m in members:
            stream.wait(ids[m])
        lo = pl.multiple_of(((me + shift) & 3) * 256, 128)
        dg, du = hidden_part(rows_ref, wd_ref[n * 256 : (n + 1) * 256], fup_ref, fgate_ref, lo, 256)
        store(lo, dg, du)


def add_shards(stream, srcs, pieces, dst_ref):
    at = 0
    ids = []
    for src, (_, _, width) in zip(srcs, pieces):
        ids.append(stream.add(src, dst_ref.at[pl.ds(at, width)]))
        at += width
    return ids


def near_kernel(at_dir, me_ref, buf_hbm, fup_hbm, fgate_hbm, *rest):
    wd_refs, (rows_hbm, dgu_hbm, buf_ref, rows_ref, wd_ref, fup_ref, fgate_ref, dgu_ref, sems, out_sems) = rest[:3], rest[3:]
    pieces, groups = halves_plan(256)
    pieces, groups = pieces[:3], groups[:3]
    stream = Stream(sems, 4)
    first = stream.add(buf_hbm, buf_ref)
    ids = add_shards(stream, wd_refs[:1], pieces[:1], wd_ref)
    stream.add(fup_hbm.at[at_dir], fup_ref)
    act = stream.add(fgate_hbm.at[at_dir], fgate_ref)
    ids += add_shards(stream, wd_refs[1:], pieces[1:], wd_ref.at[pl.ds(256, 512)])
    stream.wait(first)
    unpack_rows(buf_ref, rows_ref)
    rows_copy = pltpu.make_async_copy(rows_ref, rows_hbm, out_sems.at[0])
    rows_copy.start()
    stream.wait(act)

    def store(lo, dg, du):
        dgu_ref[0, :, pl.ds(lo, 256)] = dg
        dgu_ref[1, :, pl.ds(lo, 256)] = du

    far = pl.multiple_of(((me_ref[0] + 2) & 3) * 256, 256)
    store(far, jnp.zeros((SLOTS, 256), BF), jnp.zeros((SLOTS, 256), BF))
    hidden_stage(stream, groups, ids, me_ref[0], rows_ref, wd_ref, fup_ref, fgate_ref, store)
    dgu_copy = pltpu.make_async_copy(dgu_ref, dgu_hbm, out_sems.at[1])
    dgu_copy.start()
    rows_copy.wait()
    dgu_copy.wait()


def hidden_near(at_dir, me, buf, fup, fgate, wd):
    return pl.pallas_call(
        functools.partial(near_kernel, at_dir),
        in_specs=[IN_SMEM] + [IN_HBM] * 6,
        out_specs=[IN_HBM, IN_HBM],
        out_shape=(
            jax.ShapeDtypeStruct((SLOTS, D), BF),
            jax.ShapeDtypeStruct((2, SLOTS, FF), BF),
        ),
        scratch_shapes=[
            pltpu.VMEM((MAIN, NCH * PCH), BF),
            pltpu.VMEM((SLOTS, D), BF),
            pltpu.VMEM((768, D), BF),
            pltpu.VMEM((SLOTS, FF), F32),
            pltpu.VMEM((SLOTS, FF), F32),
            pltpu.VMEM((2, SLOTS, FF), BF),
            pltpu.SemaphoreType.DMA((6,)),
            pltpu.SemaphoreType.DMA((2,)),
        ],
        compiler_params=pltpu.CompilerParams(vmem_limit_bytes=60 << 20),
        cost_estimate=pl.CostEstimate(flops=800_000_000, bytes_accessed=10_000_000, transcendentals=0),
        name="hidden_near",
    )(me, buf, fup, fgate, *wd)


def far_kernel(at_dir, me_ref, rows_hbm, fup_hbm, fgate_hbm, near_hbm, top_hbm, low_hbm, dgu_ref, rows_ref, wd_ref, fup_ref, fgate_ref, sems):
    lo = pl.multiple_of(((me_ref[0] + 2) & 3) * 256, 256)
    cols = pl.ds(lo, 256)
    stream = Stream(sems, 7)
    stream.add(rows_hbm, rows_ref)
    stream.add(top_hbm, wd_ref.at[pl.ds(0, 128)])
    stream.add(low_hbm, wd_ref.at[pl.ds(128, 128)])
    stream.add(fup_hbm.at[at_dir, :, cols], fup_ref)
    stream.add(fgate_hbm.at[at_dir, :, cols], fgate_ref)
    last = stream.add(near_hbm, dgu_ref)
    stream.wait(last - 1)
    d_hidden = dot(rows_ref[...], wd_ref[...], NT)
    dg = (d_hidden * fgate_ref[...]).astype(BF)
    du = (d_hidden * fup_ref[...]).astype(BF)
    stream.wait(last)
    dgu_ref[0, :, cols] = dg
    dgu_ref[1, :, cols] = du


def hidden_far(at_dir, me, rows, fup, fgate, near, top, low):
    return pl.pallas_call(
        functools.partial(far_kernel, at_dir),
        in_specs=[IN_SMEM] + [IN_HBM] * 6,
        out_specs=IN_VMEM,
        out_shape=jax.ShapeDtypeStruct((2, SLOTS, FF), BF),
        scratch_shapes=[
            pltpu.VMEM((SLOTS, D), BF),
            pltpu.VMEM((256, D), BF),
            pltpu.VMEM((SLOTS, 256), F32),
            pltpu.VMEM((SLOTS, 256), F32),
            pltpu.SemaphoreType.DMA((6,)),
        ],
        compiler_params=pltpu.CompilerParams(vmem_limit_bytes=60 << 20),
        cost_estimate=pl.CostEstimate(flops=270_000_000, bytes_accessed=5_000_000, transcendentals=0),
        name="hidden_far",
    )(me, rows, fup, fgate, near, top, low)


def own_grads_kernel(me_ref, own, left, right, far, wg_hbm, wu_hbm, out_hbm, out_ref, d_ref, wg_ref, wu_ref, sems, out_sems):
    srcs = [own, left, right, far]
    stream = Stream(sems, 10)
    stream.add(wg_hbm, wg_ref)
    for n in range(4):
        stream.add(srcs[n].at[0], d_ref.at[0, pl.ds(n * SLOTS, SLOTS)])
    stream.add(wu_hbm, wu_ref)
    for n in range(4):
        stream.add(srcs[n].at[1], d_ref.at[1, pl.ds(n * SLOTS, SLOTS)])
    stream.wait(4)
    total = dot(d_ref[0], wg_ref[...], NT)
    stream.wait(9)
    total = (total + dot(d_ref[1], wu_ref[...], NT)).astype(BF)
    outs = []
    for n, shift in enumerate((0, 3, 1, 2)):
        put_chunk(total[n * SLOTS : (n + 1) * SLOTS], out_ref, n, None)
        outs.append(pltpu.make_async_copy(out_ref.at[n], out_hbm.at[(me_ref[0] + shift) & 3], out_sems.at[n]))
        outs[-1].start()
    for copy in outs:
        copy.wait()


def own_grads(me, own, left, right, far, wg, wu):
    return pl.pallas_call(
        own_grads_kernel,
        in_specs=[IN_SMEM] + [IN_HBM] * 6,
        out_specs=IN_HBM,
        out_shape=jax.ShapeDtypeStruct((4, MAIN, PCH), BF),
        scratch_shapes=[
            pltpu.VMEM((4, MAIN, PCH), BF),
            pltpu.VMEM((2, 4 * SLOTS, FF), BF),
            pltpu.VMEM((CH, FF), BF),
            pltpu.VMEM((CH, FF), BF),
            pltpu.SemaphoreType.DMA((10,)),
            pltpu.SemaphoreType.DMA((4,)),
        ],
        compiler_params=pltpu.CompilerParams(vmem_limit_bytes=60 << 20),
        cost_estimate=pl.CostEstimate(flops=2_120_000_000, bytes_accessed=8_000_000, transcendentals=0),
        name="own_grads",
    )(me, own, left, right, far, wg, wu)


def expert_kernel(at_dir, whole, me_ref, buf_hbm, fup_hbm, fgate_hbm, *rest):
    pieces, groups = halves_plan(256)
    wd_refs, rest = rest[: len(pieces)], rest[len(pieces) :]
    me = me_ref[0]
    gpieces, ggroups = halves_plan(CH)
    count = 1 if whole else len(gpieces)
    g_src, wu_full, rest = rest[:count], rest[count], rest[count + 1 :]
    if whole:
        gpieces, ggroups = [(k, 0, CH) for k in range(4)], [(k, [k]) for k in range(4)]
        starts = [k * CH for k in range(4)]
        g_src = [g_src[0].at[pl.ds(row, CH)] for row in starts]
    else:
        starts = [pl.multiple_of(((me + shift) & 3) * CH + row, 64) for shift, row, _ in gpieces]
    u_src = [wu_full.at[pl.ds(row, width)] for row, (_, _, width) in zip(starts, gpieces)]
    out_ref, buf_ref, rows_ref, wd_ref, wg_ref, wu_ref, fup_ref, fgate_ref, dg_ref, du_ref, sems = rest
    stream = Stream(sems, 4)
    first = stream.add(buf_hbm, buf_ref)
    ids = add_shards(stream, wd_refs[:1], pieces[:1], wd_ref)
    stream.add(fup_hbm.at[at_dir], fup_ref)
    act = stream.add(fgate_hbm.at[at_dir], fgate_ref)
    ids += add_shards(stream, wd_refs[1:], pieces[1:], wd_ref.at[pl.ds(256, FF - 256)])
    grad_ids = []
    at = 0
    for n, (_, _, width) in enumerate(gpieces):
        place = pl.ds(at, width)
        grad_ids.append((stream.add(g_src[n], wg_ref.at[place]), stream.add(u_src[n], wu_ref.at[place])))
        at += width
    stream.wait(first)
    unpack_rows(buf_ref, rows_ref)
    stream.wait(act)

    def store(lo, dg, du):
        dg_ref[:, pl.ds(lo, 256)] = dg
        du_ref[:, pl.ds(lo, 256)] = du

    hidden_stage(stream, groups, ids, me, rows_ref, wd_ref, fup_ref, fgate_ref, store)
    for n, (shift, members) in enumerate(ggroups):
        for m in members:
            stream.wait(grad_ids[m][1])
        at = slice(n * CH, (n + 1) * CH)
        total = dot(dg_ref[...], wg_ref[at], NT) + dot(du_ref[...], wu_ref[at], NT)
        base = shift * PCH if whole else pl.multiple_of(((me + shift) & 3) * PCH, 128)
        put_chunk(total.astype(BF), out_ref, None, base)


def expert_pass(at_dir, me, buf, fup, fgate, wd, wg, wu):
    whole = len(wg) == 1
    copies = 3 + len(wd) + 2 * (4 if whole else len(wg))
    return pl.pallas_call(
        functools.partial(expert_kernel, at_dir, whole),
        in_specs=[IN_SMEM] + [IN_HBM] * (4 + len(wd) + len(wg)),
        out_specs=IN_VMEM,
        out_shape=jax.ShapeDtypeStruct((MAIN, NCH * PCH), BF),
        scratch_shapes=[
            pltpu.VMEM((MAIN, NCH * PCH), BF),
            pltpu.VMEM((SLOTS, D), BF),
            pltpu.VMEM((FF, D), BF),
            pltpu.VMEM((D, FF), BF),
            pltpu.VMEM((D, FF), BF),
            pltpu.VMEM((SLOTS, FF), F32),
            pltpu.VMEM((SLOTS, FF), F32),
            pltpu.VMEM((SLOTS, FF), BF),
            pltpu.VMEM((SLOTS, FF), BF),
            pltpu.SemaphoreType.DMA((copies,)),
        ],
        compiler_params=pltpu.CompilerParams(vmem_limit_bytes=60 << 20),
        cost_estimate=pl.CostEstimate(flops=3_200_000_000, bytes_accessed=28_000_000, transcendentals=0),
        name="expert_pass",
    )(me, buf, fup, fgate, *wd, *wg, wu)


def front_kernel(at_dir, me_ref, buf_hbm, fup_hbm, fgate_hbm, *rest):
    pieces, groups = halves_plan(256)
    gpieces, ggroups = halves_plan(CH)
    wd_refs, wg_refs, rest = rest[:5], rest[5:10], rest[10:]
    (
        part_hbm, du_ref, buf_ref, rows_ref, wd_ref, wg_ref, fup_ref, fgate_ref, dg_ref, part_ref,
        sems, out_sems,
    ) = rest
    me = me_ref[0]
    stream = Stream(sems, 4)
    first = stream.add(buf_hbm, buf_ref)
    ids = add_shards(stream, wd_refs[:1], pieces[:1], wd_ref)
    stream.add(fup_hbm.at[at_dir], fup_ref)
    act = stream.add(fgate_hbm.at[at_dir], fgate_ref)
    ids += add_shards(stream, wd_refs[1:], pieces[1:], wd_ref.at[pl.ds(256, FF - 256)])
    grad_ids = add_shards(stream, wg_refs, gpieces, wg_ref)
    stream.wait(first)
    unpack_rows(buf_ref, rows_ref)
    stream.wait(act)

    def store(lo, dg, du):
        dg_ref[:, pl.ds(lo, 256)] = dg
        du_ref[:, pl.ds(lo, 256)] = du

    hidden_stage(stream, groups, ids, me, rows_ref, wd_ref, fup_ref, fgate_ref, store)
    outs = []
    for n, (shift, members) in enumerate(ggroups):
        for m in members:
            stream.wait(grad_ids[m])
        part_ref[n] = dot(dg_ref[...], wg_ref[n * CH : (n + 1) * CH], NT)
        outs.append(pltpu.make_async_copy(part_ref.at[n], part_hbm.at[(me + shift) & 3], out_sems.at[n]))
        outs[-1].start()
    for copy in outs:
        copy.wait()


def front_pass(at_dir, me, buf, fup, fgate, wd, wg):
    return pl.pallas_call(
        functools.partial(front_kernel, at_dir),
        in_specs=[IN_SMEM] + [IN_HBM] * 13,
        out_specs=[IN_HBM, IN_VMEM],
        out_shape=(
            jax.ShapeDtypeStruct((NCH, SLOTS, CH), F32),
            jax.ShapeDtypeStruct((SLOTS, FF), BF),
        ),
        scratch_shapes=[
            pltpu.VMEM((MAIN, NCH * PCH), BF),
            pltpu.VMEM((SLOTS, D), BF),
            pltpu.VMEM((FF, D), BF),
            pltpu.VMEM((D, FF), BF),
            pltpu.VMEM((SLOTS, FF), F32),
            pltpu.VMEM((SLOTS, FF), F32),
            pltpu.VMEM((SLOTS, FF), BF),
            pltpu.VMEM((NCH, SLOTS, CH), F32),
            pltpu.SemaphoreType.DMA((13,)),
            pltpu.SemaphoreType.DMA((NCH,)),
        ],
        compiler_params=pltpu.CompilerParams(vmem_limit_bytes=60 << 20),
        cost_estimate=pl.CostEstimate(flops=2_100_000_000, bytes_accessed=20_000_000, transcendentals=0),
        name="front_pass",
    )(me, buf, fup, fgate, *wd, *wg)


def back_kernel(du_hbm, part_hbm, wu_hbm, out_ref, du_ref, part_ref, wu_ref, sems):
    stream = Stream(sems, 4)
    stream.add(du_hbm, du_ref)
    for k in range(NCH):
        stream.add(wu_hbm.at[pl.ds(k * CH, CH)], wu_ref.at[k])
        stream.add(part_hbm.at[k], part_ref.at[k])
    for k in range(NCH):
        stream.wait(2 * k + 2)
        total = part_ref[k] + dot(du_ref[...], wu_ref[k], NT)
        put_chunk(total.astype(BF), out_ref, None, k * PCH)


def back_pass(du, part, wu):
    return pl.pallas_call(
        back_kernel,
        in_specs=[IN_HBM] * 3,
        out_specs=IN_VMEM,
        out_shape=jax.ShapeDtypeStruct((MAIN, NCH * PCH), BF),
        scratch_shapes=[
            pltpu.VMEM((SLOTS, FF), BF),
            pltpu.VMEM((NCH, SLOTS, CH), F32),
            pltpu.VMEM((NCH, CH, FF), BF),
            pltpu.SemaphoreType.DMA((1 + 2 * NCH,)),
        ],
        compiler_params=pltpu.CompilerParams(vmem_limit_bytes=60 << 20),
        cost_estimate=pl.CostEstimate(flops=1_060_000_000, bytes_accessed=10_000_000, transcendentals=0),
        name="back_pass",
    )(du, part, wu)


def down_term(h_ref, buf_ref, rows_ref):
    r = lax.broadcasted_iota(I32, (128, MAIN), 0)
    c = lax.broadcasted_iota(I32, (128, MAIN), 1)
    spread = ones_where(c == (r & 15) * 8 + (r >> 4))
    for rep in range(4):
        lo = rep * SLOTS
        block = slice(rep * MAIN, (rep + 1) * MAIN)
        rows_ref[lo : lo + MAIN, :] = buf_ref[block, 0:CH]
        nin = dot(spread, buf_ref[block, CH:PCH]).astype(BF)
        for k in range(PIECES):
            rows_ref[lo + MAIN : lo + SLOTS, k * 128 : (k + 1) * 128] = nin[k * 16 : (k + 1) * 16, :]
    return dot(h_ref[...], rows_ref[...])


def down_first_kernel(h_ref, buf_ref, out_ref, rows_ref):
    out_ref[...] = down_term(h_ref, buf_ref, rows_ref)


def down_first(h, buf):
    return pl.pallas_call(
        down_first_kernel,
        grid=(NCH,),
        in_specs=[
            pl.BlockSpec((256, 4 * SLOTS), lambda j: (0, 0)),
            pl.BlockSpec((4 * MAIN, PCH), lambda j: (0, j)),
        ],
        out_specs=pl.BlockSpec((256, CH), lambda j: (0, j)),
        out_shape=jax.ShapeDtypeStruct((256, D), F32),
        scratch_shapes=[pltpu.VMEM((4 * SLOTS, CH), BF)],
        compiler_params=pltpu.CompilerParams(vmem_limit_bytes=60 << 20),
        cost_estimate=pl.CostEstimate(flops=1_060_000_000, bytes_accessed=8_000_000, transcendentals=0),
        name="down_first",
    )(h, buf)


def down_last_kernel(h_hbm, buf_hbm, sum_hbm, out_hbm, h_ref, buf_ref, sum_ref, out_ref, rows_ref, sems, out_sems):
    stream = Stream(sems, 9)
    stream.add(h_hbm, h_ref)
    for j in range(NCH):
        stream.add(buf_hbm.at[:, pl.ds(j * PCH, PCH)], buf_ref.at[j])
        stream.add(sum_hbm.at[:, pl.ds(j * CH, CH)], sum_ref.at[j])
    outs = []
    for j in range(NCH):
        stream.wait(2 + 2 * j)
        out_ref[j] = (sum_ref[j] + down_term(h_ref, buf_ref.at[j], rows_ref.at[j % 2])).astype(BF)
        outs.append(pltpu.make_async_copy(out_ref.at[j], out_hbm.at[:, pl.ds(j * CH, CH)], out_sems.at[j]))
        outs[-1].start()
    for copy in outs:
        copy.wait()


def down_last(h, buf, total):
    return pl.pallas_call(
        down_last_kernel,
        in_specs=[IN_HBM] * 3,
        out_specs=IN_HBM,
        out_shape=jax.ShapeDtypeStruct((256, D), BF),
        scratch_shapes=[
            pltpu.VMEM((256, 4 * SLOTS), BF),
            pltpu.VMEM((NCH, 4 * MAIN, PCH), BF),
            pltpu.VMEM((NCH, 256, CH), F32),
            pltpu.VMEM((NCH, 256, CH), BF),
            pltpu.VMEM((2, 4 * SLOTS, CH), BF),
            pltpu.SemaphoreType.DMA((9,)),
            pltpu.SemaphoreType.DMA((NCH,)),
        ],
        compiler_params=pltpu.CompilerParams(vmem_limit_bytes=60 << 20),
        cost_estimate=pl.CostEstimate(flops=1_060_000_000, bytes_accessed=10_000_000, transcendentals=0),
        name="down_last",
    )(h, buf, total)


def exchange(buf):
    return lax.all_to_all(
        buf.reshape(EXP, 8, NCH * PCH), "expert", split_axis=0, concat_axis=0, tiled=True
    ).reshape(MAIN, NCH * PCH)


def slot_targets(routes):
    flat = routes.reshape(2, TOK * 2)
    n = TOK * 2
    row = lax.broadcasted_iota(I32, (n, n), 0)
    col = lax.broadcasted_iota(I32, (n, n), 1)
    same = jnp.logical_and(flat[:, :, None] == flat[:, None, :], (col < row)[None])
    return (flat * CAP + jnp.sum(same.astype(I32), axis=2)).reshape(2, TOK, 2)


def shift_dp(value, step, sections):
    pairs = [(s * 4 + i, s * 4 + (i + step) % 4) for s in sections for i in range(4)]
    return lax.ppermute(value, ("pipe", "dp"), pairs)


def tie(value, *others):
    return lax.optimization_barrier((value,) + others)[0]


def per_device(
    seed_grads, expert_routes, route_weights, saved_gate, saved_up, w_gate, w_up, w_down
):
    section = lax.axis_index("pipe")
    dp = lax.axis_index("dp").astype(I32)
    me = dp.reshape(1)
    first_up = section < 2
    first = jnp.where(first_up, 1, 0).astype(I32)
    order = jnp.stack([first, 1 - first])
    every, outer, inner = (0, 1, 2, 3), (0, 3), (1, 2)

    def gather(x):
        return lax.all_gather(x, "dp", axis=0, tiled=True)

    def near(x, sections):
        return shift_dp(x, 1, sections), shift_dp(x, -1, sections)

    def hop(top, low, sections):
        return shift_dp(top, 1, sections), shift_dp(low, -1, sections)

    def far(left, right, sections):
        half = left.shape[0] // 2
        return hop(left[:half], right[half:], sections)

    wd_own, wg_own, wu_own = w_down[0, 0], w_gate[0, 0], w_up[0, 0]
    wd_near = near(wd_own, every)

    def ordered(x):
        return jnp.where(first_up, x[1], x[0]), jnp.where(first_up, x[0], x[1])

    targets = slot_targets(expert_routes[:, 0])
    tgt = ordered(targets)
    wts = ordered(route_weights[:, 0])
    tgt_t = [t.T for t in tgt]
    wts_t = [w.T for w in wts]
    cur = jnp.where(first_up, seed_grads[1], seed_grads[0])
    fup, fgate, hidden = prep(order, saved_gate[:, 0, 0, 0], saved_up[:, 0, 0, 0])

    wg_near = near(tie(wg_own, hidden, *wd_near), inner)

    edge = jnp.logical_or(section == 0, section == 3)
    keep_edge = edge.astype(I32).reshape(1)
    old = cur
    moves = [[(0, 1), (3, 2)], [(1, 2), (2, 1)], [(2, 3), (1, 0)]]
    results = []
    for step in range(4):
        at = step // 2
        keep = keep_edge if step == 1 else 1 - keep_edge if step == 3 else 0 * keep_edge
        outgoing = pre(keep, tgt_t[at], wts_t[at], old, cur)
        if step == 1:
            outgoing = tie(outgoing, *wg)
        old = cur
        buf = exchange(outgoing)
        if step == 0:
            halves = tie(wd_near[0], buf)[:128], tie(wd_near[1], buf)[128:]
            wd_outer = (wd_own,) + wd_near + hop(*halves, outer)
            rows, dgu_part = hidden_near(at, me, buf, fup, fgate, wd_outer[:3])
            dgu = hidden_far(at, me, rows, fup, fgate, dgu_part, *wd_outer[3:])
            ready = tie(dgu, *wg_near)
            others = [shift_dp(ready, step_dp, outer) for step_dp in (1, -1, 2)]
            wg_halves = tie(wg_near[0], others[0])[: CH // 2], tie(wg_near[1], others[0])[CH // 2 :]
            far_dgu, top, low = lax.optimization_barrier((others[2],) + wg_halves)
            sent = own_grads(me, dgu, *others[:2], far_dgu, wg_own, wu_own)
            wd = (wd_own,) + wd_near + hop(*[tie(h, dgu_part) for h in halves], inner)
            sent = tie(sent, *wd)
            wu_full = gather(tie(wu_own, sent))
            wg = (wg_own,) + wg_near + hop(tie(top, sent), tie(low, sent), inner)
            home = lax.all_to_all(
                sent.reshape(4 * EXP, 8, PCH), ("dp", "expert"), split_axis=0, concat_axis=0, tiled=True
            ).reshape(4, MAIN, PCH)
            result = post(tgt[at], cur, home)
        else:
            if step == 1:
                wg_full = (gather(tie(wg_own, buf)),)
                all_first = gather(buf)
                hidden_all = lax.all_gather(tie(hidden, buf), "dp", axis=0)
                part, du = front_pass(at, me, buf, fup, fgate, wd, wg)
                packed = back_pass(du, part, wu_full)
            elif step == 2:
                packed = expert_pass(at, me, buf, fup, fgate, wd, wg, wu_full)
            else:
                all_second = gather(buf)
                packed = expert_pass(at, me, buf, fup, fgate, wd_outer, wg_full, wu_full)
            result = post(tgt[at], cur, exchange(packed))
        results.append(result)
        if step < 3:
            cur = lax.ppermute(result, "pipe", moves[step])

    res_first = jnp.where(edge, results[0], results[1])
    res_second = jnp.where(edge, results[3], results[2])
    input_grads = jnp.where(
        first_up, jnp.stack([res_second, res_first]), jnp.stack([res_first, res_second])
    )[:, None]

    hidden_mine = lax.dynamic_slice_in_dim(hidden_all, dp * 256, 256, axis=3)
    hidden_t = hidden_mine.transpose(1, 3, 0, 2).reshape(2, 256, 4 * SLOTS)
    down_grads = down_last(hidden_t[1], all_second, down_first(hidden_t[0], all_first))
    return input_grads, down_grads[None, None]


def solution(mesh):
    return jax.shard_map(
        per_device,
        mesh=mesh,
        in_specs=(
            P(None, ("expert", "dp"), None),
            P(None, "pipe", ("expert", "dp"), None),
            P(None, "pipe", ("expert", "dp"), None),
            P(None, "pipe", "dp", "expert", None, None),
            P(None, "pipe", "dp", "expert", None, None),
            P("pipe", "expert", "dp", None),
            P("pipe", "expert", "dp", None),
            P("pipe", "expert", "dp", None),
        ),
        out_specs=(P(None, "pipe", ("expert", "dp"), None), P("pipe", "expert", "dp", None)),
        check_vma=False,
    )
```

```python
import functools
import jax
import jax.numpy as jnp
from jax import lax
from jax.experimental import pallas as pl
from jax.experimental.pallas import tpu as pltpu
from jax.sharding import PartitionSpec as P

BF = jnp.bfloat16
F32 = jnp.float32
I32 = jnp.int32
D = 3584
FF = 1024
TOK = 64
EXP = 16
CAP = 9
SLOTS = 144
MAIN = 128
CH = 896
PCH = 1024
NCH = 4
PIECES = 7
NT = (((1,), (1,)), ((), ()))
NN = (((1,), (0,)), ((), ()))


IN_HBM = pl.BlockSpec(memory_space=pl.ANY)
IN_SMEM = pl.BlockSpec(memory_space=pltpu.SMEM)
IN_VMEM = pl.BlockSpec(memory_space=pltpu.VMEM)


def dot(a, b, dims=NN):
    return lax.dot_general(a, b, dims, preferred_element_type=F32)


def ones_where(mask):
    return jnp.where(mask, 1.0, 0.0).astype(BF)


def prep_kernel(order_ref, gate_ref, up_ref, fup_ref, fgate_ref, hidden_ref):
    row = lax.broadcasted_iota(I32, (SLOTS, SLOTS), 0)
    col = lax.broadcasted_iota(I32, (SLOTS, SLOTS), 1)
    slot = jnp.where(row < MAIN, (row >> 3) * CAP + (row & 7), (row - MAIN) * CAP + 8)
    perm = ones_where(col == slot)
    gate = dot(perm, gate_ref[0])
    up = dot(perm, up_ref[0])
    sig = 1.0 / (1.0 + jnp.exp(-gate))
    act = gate * sig
    fup_ref[0] = act
    fgate_ref[0] = up * sig * (1.0 + gate * (1.0 - sig))
    hidden_ref[0] = (act * up).astype(BF)


def prep(order, gate, up):
    spec_in = pl.BlockSpec((1, SLOTS, FF), lambda i, o: (o[i], 0, 0))
    spec_out = pl.BlockSpec((1, SLOTS, FF), lambda i, o: (i, 0, 0))
    return pl.pallas_call(
        prep_kernel,
        out_shape=(
            jax.ShapeDtypeStruct((2, SLOTS, FF), F32),
            jax.ShapeDtypeStruct((2, SLOTS, FF), F32),
            jax.ShapeDtypeStruct((2, SLOTS, FF), BF),
        ),
        grid_spec=pltpu.PrefetchScalarGridSpec(
            num_scalar_prefetch=1,
            grid=(2,),
            in_specs=[spec_in, spec_in],
            out_specs=[spec_out, spec_out, spec_out],
        ),
        compiler_params=pltpu.CompilerParams(vmem_limit_bytes=24 << 20),
        cost_estimate=pl.CostEstimate(flops=170_000_000, bytes_accessed=4_700_000, transcendentals=300_000),
        name="prep",
    )(order, gate, up)


def pre_kernel(pick_ref, t_ref, w_ref, old_ref, new_ref, out_ref):
    keep = pick_ref[0] > 0
    c = lax.broadcasted_iota(I32, (MAIN, TOK), 0)
    e9 = (c >> 3) * CAP
    t0 = t_ref[0:1, :]
    t1 = t_ref[1:2, :]
    w0 = w_ref[0:1, :]
    w1 = w_ref[1:2, :]

    def pick(slot):
        m0 = t0 == slot
        m1 = t1 == slot
        scale = jnp.sum(jnp.where(m0, w0, 0.0) + jnp.where(m1, w1, 0.0), axis=1, keepdims=True)
        return ones_where(jnp.logical_or(m0, m1)), scale

    main, scale_main = pick(e9 + (c & 7))
    last, scale_last = pick(e9 + 8)
    piece = lax.broadcasted_iota(I32, (MAIN, 128), 0) & 7
    for j in range(NCH):
        cols = slice(j * CH, (j + 1) * CH)
        x = jnp.where(keep, old_ref[:, cols], new_ref[:, cols])
        out_ref[:, j * PCH : j * PCH + CH] = (dot(main, x) * scale_main).astype(BF)
        full = dot(last, x)
        part = jnp.zeros((MAIN, 128), F32)
        for k in range(PIECES):
            part = jnp.where(piece == k, full[:, k * 128 : (k + 1) * 128], part)
        out_ref[:, j * PCH + CH : (j + 1) * PCH] = (part * scale_last).astype(BF)


def pre(keep, targets_t, weights_t, old, new):
    return pl.pallas_call(
        pre_kernel,
        in_specs=[IN_SMEM] + [IN_VMEM] * 4,
        out_shape=jax.ShapeDtypeStruct((MAIN, NCH * PCH), BF),
        compiler_params=pltpu.CompilerParams(vmem_limit_bytes=16 << 20),
        cost_estimate=pl.CostEstimate(flops=120_000_000, bytes_accessed=1_600_000, transcendentals=0),
        name="pre",
    )(keep, targets_t, weights_t, old, new)


def post_kernel(t_ref, cur_ref, buf_ref, out_ref):
    c = lax.broadcasted_iota(I32, (TOK, MAIN), 1)
    e9 = (c >> 3) * CAP
    s = c & 7
    t0 = t_ref[:, 0:1]
    t1 = t_ref[:, 1:2]

    def pick(slot):
        return jnp.logical_or(t0 == slot, t1 == slot)

    main = ones_where(pick(e9 + s))
    last = pick(e9 + 8)
    tail = jnp.concatenate(
        [ones_where(jnp.logical_and(last, s == k)) for k in range(PIECES)], axis=0
    )
    for j in range(NCH):
        if len(buf_ref.shape) == 3:
            packed = buf_ref[j]
        else:
            packed = buf_ref[:, j * PCH : (j + 1) * PCH]
        acc = dot(main, packed[:, :CH])
        nin = dot(tail, packed[:, CH:])
        for k in range(PIECES):
            lo = j * CH + k * 128
            out_ref[:, lo : lo + 128] = (
                cur_ref[:, lo : lo + 128].astype(F32)
                + (acc[:, k * 128 : (k + 1) * 128] + nin[k * TOK : (k + 1) * TOK, :])
            ).astype(BF)


def post(targets, cur, buf):
    return pl.pallas_call(
        post_kernel,
        out_shape=jax.ShapeDtypeStruct((TOK, D), BF),
        compiler_params=pltpu.CompilerParams(vmem_limit_bytes=16 << 20),
        cost_estimate=pl.CostEstimate(flops=120_000_000, bytes_accessed=2_000_000, transcendentals=0),
        name="post",
    )(targets, cur, buf)


def unpack_rows(buf_ref, rows_ref):
    r = lax.broadcasted_iota(I32, (128, MAIN), 0)
    c = lax.broadcasted_iota(I32, (128, MAIN), 1)
    spread = ones_where(c == (r & 15) * 8 + (r >> 4))
    for j in range(NCH):
        rows_ref[0:MAIN, j * CH : (j + 1) * CH] = buf_ref[:, j * PCH : j * PCH + CH]
        nin = dot(spread, buf_ref[:, j * PCH + CH : (j + 1) * PCH]).astype(BF)
        for k in range(PIECES):
            lo = j * CH + k * 128
            rows_ref[MAIN:SLOTS, lo : lo + 128] = nin[k * 16 : (k + 1) * 16, :]


def put_chunk(grads, out_ref, lead, base):
    c = lax.broadcasted_iota(I32, (MAIN, 128), 0)
    r = lax.broadcasted_iota(I32, (MAIN, 128), 1)
    fold = ones_where(r == (c & 7) * 16 + (c >> 3))
    pieces = [grads[MAIN:SLOTS, k * 128 : (k + 1) * 128] for k in range(PIECES)]
    pieces.append(jnp.zeros((16, 128), BF))
    tail = dot(fold, jnp.concatenate(pieces, axis=0)).astype(BF)
    if lead is None:
        out_ref[:, pl.ds(base, CH)] = grads[0:MAIN]
        out_ref[:, pl.ds(base + CH, 128)] = tail
    else:
        out_ref[lead, :, 0:CH] = grads[0:MAIN]
        out_ref[lead, :, CH:PCH] = tail


def hidden_part(rows_ref, wd, fup_ref, fgate_ref, lo, width):
    d_hidden = dot(rows_ref[...], wd, NT)
    cols = pl.ds(lo, width)
    return (d_hidden * fgate_ref[:, cols]).astype(BF), (d_hidden * fup_ref[:, cols]).astype(BF)


def halves_plan(shard):
    half = shard // 2
    pieces = [(0, 0, shard)]
    groups = [(0, [0])]
    for shift, parts in ((3, False), (1, False), (2, True)):
        mine = []
        for row, width in ((0, half), (half, half)) if parts else ((0, shard),):
            mine.append(len(pieces))
            pieces.append((shift, row, width))
        groups.append((shift, mine))
    return pieces, groups


class Stream:
    def __init__(self, sems, ahead):
        self.sems, self.ahead, self.todo, self.flying, self.done = sems, ahead, [], [], 0

    def add(self, src, dst):
        self.todo.append((src, dst))
        return len(self.todo) - 1

    def start(self, upto):
        while len(self.flying) < min(upto, len(self.todo)):
            n = len(self.flying)
            copy = pltpu.make_async_copy(*self.todo[n], self.sems.at[n])
            copy.start()
            self.flying.append(copy)

    def wait(self, n):
        self.start(n + 1 + self.ahead)
        while self.done <= n:
            self.flying[self.done].wait()
            self.done += 1


def hidden_stage(stream, groups, ids, me, rows_ref, wd_ref, fup_ref, fgate_ref, store):
    for n, (shift, members) in enumerate(groups):
        for m in members:
            stream.wait(ids[m])
        lo = pl.multiple_of(((me + shift) & 3) * 256, 128)
        dg, du = hidden_part(rows_ref, wd_ref[n * 256 : (n + 1) * 256], fup_ref, fgate_ref, lo, 256)
        store(lo, dg, du)


def add_shards(stream, srcs, pieces, dst_ref):
    at = 0
    ids = []
    for src, (_, _, width) in zip(srcs, pieces):
        ids.append(stream.add(src, dst_ref.at[pl.ds(at, width)]))
        at += width
    return ids


def near_kernel(at_dir, me_ref, buf_hbm, fup_hbm, fgate_hbm, *rest):
    wd_refs, (rows_hbm, dgu_hbm, buf_ref, rows_ref, wd_ref, fup_ref, fgate_ref, dgu_ref, sems, out_sems) = rest[:3], rest[3:]
    pieces, groups = halves_plan(256)
    pieces, groups = pieces[:3], groups[:3]
    stream = Stream(sems, 4)
    first = stream.add(buf_hbm, buf_ref)
    ids = add_shards(stream, wd_refs[:1], pieces[:1], wd_ref)
    stream.add(fup_hbm.at[at_dir], fup_ref)
    act = stream.add(fgate_hbm.at[at_dir], fgate_ref)
    ids += add_shards(stream, wd_refs[1:], pieces[1:], wd_ref.at[pl.ds(256, 512)])
    stream.wait(first)
    unpack_rows(buf_ref, rows_ref)
    rows_copy = pltpu.make_async_copy(rows_ref, rows_hbm, out_sems.at[0])
    rows_copy.start()
    stream.wait(act)

    def store(lo, dg, du):
        dgu_ref[0, :, pl.ds(lo, 256)] = dg
        dgu_ref[1, :, pl.ds(lo, 256)] = du

    far = pl.multiple_of(((me_ref[0] + 2) & 3) * 256, 256)
    store(far, jnp.zeros((SLOTS, 256), BF), jnp.zeros((SLOTS, 256), BF))
    hidden_stage(stream, groups, ids, me_ref[0], rows_ref, wd_ref, fup_ref, fgate_ref, store)
    dgu_copy = pltpu.make_async_copy(dgu_ref, dgu_hbm, out_sems.at[1])
    dgu_copy.start()
    rows_copy.wait()
    dgu_copy.wait()


def hidden_near(at_dir, me, buf, fup, fgate, wd):
    return pl.pallas_call(
        functools.partial(near_kernel, at_dir),
        in_specs=[IN_SMEM] + [IN_HBM] * 6,
        out_specs=[IN_HBM, IN_HBM],
        out_shape=(
            jax.ShapeDtypeStruct((SLOTS, D), BF),
            jax.ShapeDtypeStruct((2, SLOTS, FF), BF),
        ),
        scratch_shapes=[
            pltpu.VMEM((MAIN, NCH * PCH), BF),
            pltpu.VMEM((SLOTS, D), BF),
            pltpu.VMEM((768, D), BF),
            pltpu.VMEM((SLOTS, FF), F32),
            pltpu.VMEM((SLOTS, FF), F32),
            pltpu.VMEM((2, SLOTS, FF), BF),
            pltpu.SemaphoreType.DMA((6,)),
            pltpu.SemaphoreType.DMA((2,)),
        ],
        compiler_params=pltpu.CompilerParams(vmem_limit_bytes=60 << 20),
        cost_estimate=pl.CostEstimate(flops=800_000_000, bytes_accessed=10_000_000, transcendentals=0),
        name="hidden_near",
    )(me, buf, fup, fgate, *wd)


def far_kernel(at_dir, me_ref, rows_hbm, fup_hbm, fgate_hbm, near_hbm, top_hbm, low_hbm, dgu_ref, rows_ref, wd_ref, fup_ref, fgate_ref, sems):
    lo = pl.multiple_of(((me_ref[0] + 2) & 3) * 256, 256)
    cols = pl.ds(lo, 256)
    stream = Stream(sems, 7)
    stream.add(rows_hbm, rows_ref)
    stream.add(top_hbm, wd_ref.at[pl.ds(0, 128)])
    stream.add(low_hbm, wd_ref.at[pl.ds(128, 128)])
    stream.add(fup_hbm.at[at_dir, :, cols], fup_ref)
    stream.add(fgate_hbm.at[at_dir, :, cols], fgate_ref)
    last = stream.add(near_hbm, dgu_ref)
    stream.wait(last - 1)
    d_hidden = dot(rows_ref[...], wd_ref[...], NT)
    dg = (d_hidden * fgate_ref[...]).astype(BF)
    du = (d_hidden * fup_ref[...]).astype(BF)
    stream.wait(last)
    dgu_ref[0, :, cols] = dg
    dgu_ref[1, :, cols] = du


def hidden_far(at_dir, me, rows, fup, fgate, near, top, low):
    return pl.pallas_call(
        functools.partial(far_kernel, at_dir),
        in_specs=[IN_SMEM] + [IN_HBM] * 6,
        out_specs=IN_VMEM,
        out_shape=jax.ShapeDtypeStruct((2, SLOTS, FF), BF),
        scratch_shapes=[
            pltpu.VMEM((SLOTS, D), BF),
            pltpu.VMEM((256, D), BF),
            pltpu.VMEM((SLOTS, 256), F32),
            pltpu.VMEM((SLOTS, 256), F32),
            pltpu.SemaphoreType.DMA((6,)),
        ],
        compiler_params=pltpu.CompilerParams(vmem_limit_bytes=60 << 20),
        cost_estimate=pl.CostEstimate(flops=270_000_000, bytes_accessed=5_000_000, transcendentals=0),
        name="hidden_far",
    )(me, rows, fup, fgate, near, top, low)


def own_grads_kernel(me_ref, own, left, right, far, wg_hbm, wu_hbm, out_hbm, out_ref, d_ref, wg_ref, wu_ref, sems, out_sems):
    srcs = [own, left, right, far]
    stream = Stream(sems, 10)
    stream.add(wg_hbm, wg_ref)
    for n in range(4):
        stream.add(srcs[n].at[0], d_ref.at[0, pl.ds(n * SLOTS, SLOTS)])
    stream.add(wu_hbm, wu_ref)
    for n in range(4):
        stream.add(srcs[n].at[1], d_ref.at[1, pl.ds(n * SLOTS, SLOTS)])
    stream.wait(4)
    total = dot(d_ref[0], wg_ref[...], NT)
    stream.wait(9)
    total = (total + dot(d_ref[1], wu_ref[...], NT)).astype(BF)
    outs = []
    for n, shift in enumerate((0, 3, 1, 2)):
        put_chunk(total[n * SLOTS : (n + 1) * SLOTS], out_ref, n, None)
        outs.append(pltpu.make_async_copy(out_ref.at[n], out_hbm.at[(me_ref[0] + shift) & 3], out_sems.at[n]))
        outs[-1].start()
    for copy in outs:
        copy.wait()


def own_grads(me, own, left, right, far, wg, wu):
    return pl.pallas_call(
        own_grads_kernel,
        in_specs=[IN_SMEM] + [IN_HBM] * 6,
        out_specs=IN_HBM,
        out_shape=jax.ShapeDtypeStruct((4, MAIN, PCH), BF),
        scratch_shapes=[
            pltpu.VMEM((4, MAIN, PCH), BF),
            pltpu.VMEM((2, 4 * SLOTS, FF), BF),
            pltpu.VMEM((CH, FF), BF),
            pltpu.VMEM((CH, FF), BF),
            pltpu.SemaphoreType.DMA((10,)),
            pltpu.SemaphoreType.DMA((4,)),
        ],
        compiler_params=pltpu.CompilerParams(vmem_limit_bytes=60 << 20),
        cost_estimate=pl.CostEstimate(flops=2_120_000_000, bytes_accessed=8_000_000, transcendentals=0),
        name="own_grads",
    )(me, own, left, right, far, wg, wu)


def expert_kernel(at_dir, whole, me_ref, buf_hbm, fup_hbm, fgate_hbm, *rest):
    pieces, groups = halves_plan(256)
    wd_refs, rest = rest[: len(pieces)], rest[len(pieces) :]
    me = me_ref[0]
    gpieces, ggroups = halves_plan(CH)
    count = 1 if whole else len(gpieces)
    g_src, wu_full, rest = rest[:count], rest[count], rest[count + 1 :]
    if whole:
        gpieces, ggroups = [(k, 0, CH) for k in range(4)], [(k, [k]) for k in range(4)]
        starts = [k * CH for k in range(4)]
        g_src = [g_src[0].at[pl.ds(row, CH)] for row in starts]
    else:
        starts = [pl.multiple_of(((me + shift) & 3) * CH + row, 64) for shift, row, _ in gpieces]
    u_src = [wu_full.at[pl.ds(row, width)] for row, (_, _, width) in zip(starts, gpieces)]
    out_ref, buf_ref, rows_ref, wd_ref, wg_ref, wu_ref, fup_ref, fgate_ref, dg_ref, du_ref, sems = rest
    stream = Stream(sems, 4)
    first = stream.add(buf_hbm, buf_ref)
    ids = add_shards(stream, wd_refs[:1], pieces[:1], wd_ref)
    stream.add(fup_hbm.at[at_dir], fup_ref)
    act = stream.add(fgate_hbm.at[at_dir], fgate_ref)
    ids += add_shards(stream, wd_refs[1:], pieces[1:], wd_ref.at[pl.ds(256, FF - 256)])
    grad_ids = []
    at = 0
    for n, (_, _, width) in enumerate(gpieces):
        place = pl.ds(at, width)
        grad_ids.append((stream.add(g_src[n], wg_ref.at[place]), stream.add(u_src[n], wu_ref.at[place])))
        at += width
    stream.wait(first)
    unpack_rows(buf_ref, rows_ref)
    stream.wait(act)

    def store(lo, dg, du):
        dg_ref[:, pl.ds(lo, 256)] = dg
        du_ref[:, pl.ds(lo, 256)] = du

    hidden_stage(stream, groups, ids, me, rows_ref, wd_ref, fup_ref, fgate_ref, store)
    for n, (shift, members) in enumerate(ggroups):
        for m in members:
            stream.wait(grad_ids[m][1])
        at = slice(n * CH, (n + 1) * CH)
        total = dot(dg_ref[...], wg_ref[at], NT) + dot(du_ref[...], wu_ref[at], NT)
        base = shift * PCH if whole else pl.multiple_of(((me + shift) & 3) * PCH, 128)
        put_chunk(total.astype(BF), out_ref, None, base)


def expert_pass(at_dir, me, buf, fup, fgate, wd, wg, wu):
    whole = len(wg) == 1
    copies = 3 + len(wd) + 2 * (4 if whole else len(wg))
    return pl.pallas_call(
        functools.partial(expert_kernel, at_dir, whole),
        in_specs=[IN_SMEM] + [IN_HBM] * (4 + len(wd) + len(wg)),
        out_specs=IN_VMEM,
        out_shape=jax.ShapeDtypeStruct((MAIN, NCH * PCH), BF),
        scratch_shapes=[
            pltpu.VMEM((MAIN, NCH * PCH), BF),
            pltpu.VMEM((SLOTS, D), BF),
            pltpu.VMEM((FF, D), BF),
            pltpu.VMEM((D, FF), BF),
            pltpu.VMEM((D, FF), BF),
            pltpu.VMEM((SLOTS, FF), F32),
            pltpu.VMEM((SLOTS, FF), F32),
            pltpu.VMEM((SLOTS, FF), BF),
            pltpu.VMEM((SLOTS, FF), BF),
            pltpu.SemaphoreType.DMA((copies,)),
        ],
        compiler_params=pltpu.CompilerParams(vmem_limit_bytes=48 << 20),
        cost_estimate=pl.CostEstimate(flops=3_200_000_000, bytes_accessed=28_000_000, transcendentals=0),
        name="expert_pass",
    )(me, buf, fup, fgate, *wd, *wg, wu)


def front_kernel(at_dir, me_ref, buf_hbm, fup_hbm, fgate_hbm, *rest):
    pieces, groups = halves_plan(256)
    gpieces, ggroups = halves_plan(CH)
    wd_refs, wg_refs, rest = rest[:5], rest[5:10], rest[10:]
    (
        part_hbm, du_ref, buf_ref, rows_ref, wd_ref, wg_ref, fup_ref, fgate_ref, dg_ref, part_ref,
        sems, out_sems,
    ) = rest
    me = me_ref[0]
    stream = Stream(sems, 4)
    first = stream.add(buf_hbm, buf_ref)
    ids = add_shards(stream, wd_refs[:1], pieces[:1], wd_ref)
    stream.add(fup_hbm.at[at_dir], fup_ref)
    act = stream.add(fgate_hbm.at[at_dir], fgate_ref)
    ids += add_shards(stream, wd_refs[1:], pieces[1:], wd_ref.at[pl.ds(256, FF - 256)])
    grad_ids = add_shards(stream, wg_refs, gpieces, wg_ref)
    stream.wait(first)
    unpack_rows(buf_ref, rows_ref)
    stream.wait(act)

    def store(lo, dg, du):
        dg_ref[:, pl.ds(lo, 256)] = dg
        du_ref[:, pl.ds(lo, 256)] = du

    hidden_stage(stream, groups, ids, me, rows_ref, wd_ref, fup_ref, fgate_ref, store)
    outs = []
    for n, (shift, members) in enumerate(ggroups):
        for m in members:
            stream.wait(grad_ids[m])
        part_ref[n] = dot(dg_ref[...], wg_ref[n * CH : (n + 1) * CH], NT)
        outs.append(pltpu.make_async_copy(part_ref.at[n], part_hbm.at[(me + shift) & 3], out_sems.at[n]))
        outs[-1].start()
    for copy in outs:
        copy.wait()


def front_pass(at_dir, me, buf, fup, fgate, wd, wg):
    return pl.pallas_call(
        functools.partial(front_kernel, at_dir),
        in_specs=[IN_SMEM] + [IN_HBM] * 13,
        out_specs=[IN_HBM, IN_VMEM],
        out_shape=(
            jax.ShapeDtypeStruct((NCH, SLOTS, CH), F32),
            jax.ShapeDtypeStruct((SLOTS, FF), BF),
        ),
        scratch_shapes=[
            pltpu.VMEM((MAIN, NCH * PCH), BF),
            pltpu.VMEM((SLOTS, D), BF),
            pltpu.VMEM((FF, D), BF),
            pltpu.VMEM((D, FF), BF),
            pltpu.VMEM((SLOTS, FF), F32),
            pltpu.VMEM((SLOTS, FF), F32),
            pltpu.VMEM((SLOTS, FF), BF),
            pltpu.VMEM((NCH, SLOTS, CH), F32),
            pltpu.SemaphoreType.DMA((13,)),
            pltpu.SemaphoreType.DMA((NCH,)),
        ],
        compiler_params=pltpu.CompilerParams(vmem_limit_bytes=60 << 20),
        cost_estimate=pl.CostEstimate(flops=2_100_000_000, bytes_accessed=20_000_000, transcendentals=0),
        name="front_pass",
    )(me, buf, fup, fgate, *wd, *wg)


def back_kernel(du_hbm, part_hbm, wu_hbm, out_ref, du_ref, part_ref, wu_ref, sems):
    stream = Stream(sems, 4)
    stream.add(du_hbm, du_ref)
    for k in range(NCH):
        stream.add(wu_hbm.at[pl.ds(k * CH, CH)], wu_ref.at[k])
        stream.add(part_hbm.at[k], part_ref.at[k])
    for k in range(NCH):
        stream.wait(2 * k + 2)
        total = part_ref[k] + dot(du_ref[...], wu_ref[k], NT)
        put_chunk(total.astype(BF), out_ref, None, k * PCH)


def back_pass(du, part, wu):
    return pl.pallas_call(
        back_kernel,
        in_specs=[IN_HBM] * 3,
        out_specs=IN_VMEM,
        out_shape=jax.ShapeDtypeStruct((MAIN, NCH * PCH), BF),
        scratch_shapes=[
            pltpu.VMEM((SLOTS, FF), BF),
            pltpu.VMEM((NCH, SLOTS, CH), F32),
            pltpu.VMEM((NCH, CH, FF), BF),
            pltpu.SemaphoreType.DMA((1 + 2 * NCH,)),
        ],
        compiler_params=pltpu.CompilerParams(vmem_limit_bytes=60 << 20),
        cost_estimate=pl.CostEstimate(flops=1_060_000_000, bytes_accessed=10_000_000, transcendentals=0),
        name="back_pass",
    )(du, part, wu)


def down_term(h_ref, buf_ref, rows_ref):
    r = lax.broadcasted_iota(I32, (128, MAIN), 0)
    c = lax.broadcasted_iota(I32, (128, MAIN), 1)
    spread = ones_where(c == (r & 15) * 8 + (r >> 4))
    for rep in range(4):
        lo = rep * SLOTS
        block = slice(rep * MAIN, (rep + 1) * MAIN)
        rows_ref[lo : lo + MAIN, :] = buf_ref[block, 0:CH]
        nin = dot(spread, buf_ref[block, CH:PCH]).astype(BF)
        for k in range(PIECES):
            rows_ref[lo + MAIN : lo + SLOTS, k * 128 : (k + 1) * 128] = nin[k * 16 : (k + 1) * 16, :]
    return dot(h_ref[...], rows_ref[...])


def down_first_kernel(h_ref, buf_ref, out_ref, rows_ref):
    out_ref[...] = down_term(h_ref, buf_ref, rows_ref).astype(BF)


def down_first(h, buf):
    return pl.pallas_call(
        down_first_kernel,
        grid=(NCH,),
        in_specs=[
            pl.BlockSpec((256, 4 * SLOTS), lambda j: (0, 0)),
            pl.BlockSpec((4 * MAIN, PCH), lambda j: (0, j)),
        ],
        out_specs=pl.BlockSpec((256, CH), lambda j: (0, j)),
        out_shape=jax.ShapeDtypeStruct((256, D), BF),
        scratch_shapes=[pltpu.VMEM((4 * SLOTS, CH), BF)],
        compiler_params=pltpu.CompilerParams(vmem_limit_bytes=60 << 20),
        cost_estimate=pl.CostEstimate(flops=1_060_000_000, bytes_accessed=8_000_000, transcendentals=0),
        name="down_first",
    )(h, buf)


def down_last_kernel(h_hbm, buf_hbm, sum_hbm, out_hbm, h_ref, buf_ref, sum_ref, out_ref, rows_ref, sems, out_sems):
    stream = Stream(sems, 9)
    stream.add(h_hbm, h_ref)
    for j in range(NCH):
        stream.add(buf_hbm.at[:, pl.ds(j * PCH, PCH)], buf_ref.at[j])
        stream.add(sum_hbm.at[:, pl.ds(j * CH, CH)], sum_ref.at[j])
    outs = []
    for j in range(NCH):
        stream.wait(2 + 2 * j)
        out_ref[j] = (sum_ref[j].astype(F32) + down_term(h_ref, buf_ref.at[j], rows_ref.at[j % 2])).astype(BF)
        outs.append(pltpu.make_async_copy(out_ref.at[j], out_hbm.at[:, pl.ds(j * CH, CH)], out_sems.at[j]))
        outs[-1].start()
    for copy in outs:
        copy.wait()


def down_last(h, buf, total):
    return pl.pallas_call(
        down_last_kernel,
        in_specs=[IN_HBM] * 3,
        out_specs=IN_HBM,
        out_shape=jax.ShapeDtypeStruct((256, D), BF),
        scratch_shapes=[
            pltpu.VMEM((256, 4 * SLOTS), BF),
            pltpu.VMEM((NCH, 4 * MAIN, PCH), BF),
            pltpu.VMEM((NCH, 256, CH), BF),
            pltpu.VMEM((NCH, 256, CH), BF),
            pltpu.VMEM((2, 4 * SLOTS, CH), BF),
            pltpu.SemaphoreType.DMA((9,)),
            pltpu.SemaphoreType.DMA((NCH,)),
        ],
        compiler_params=pltpu.CompilerParams(vmem_limit_bytes=60 << 20),
        cost_estimate=pl.CostEstimate(flops=1_060_000_000, bytes_accessed=10_000_000, transcendentals=0),
        name="down_last",
    )(h, buf, total)


def exchange(buf):
    return lax.all_to_all(
        buf.reshape(EXP, 8, NCH * PCH), "expert", split_axis=0, concat_axis=0, tiled=True
    ).reshape(MAIN, NCH * PCH)


def slot_targets(routes):
    flat = routes.reshape(2, TOK * 2)
    n = TOK * 2
    row = lax.broadcasted_iota(I32, (n, n), 0)
    col = lax.broadcasted_iota(I32, (n, n), 1)
    same = jnp.logical_and(flat[:, :, None] == flat[:, None, :], (col < row)[None])
    return (flat * CAP + jnp.sum(same.astype(I32), axis=2)).reshape(2, TOK, 2)


def shift_dp(value, step, sections):
    pairs = [(s * 4 + i, s * 4 + (i + step) % 4) for s in sections for i in range(4)]
    return lax.ppermute(value, ("pipe", "dp"), pairs)


def tie(value, *others):
    return lax.optimization_barrier((value,) + others)[0]


def per_device(
    seed_grads, expert_routes, route_weights, saved_gate, saved_up, w_gate, w_up, w_down
):
    section = lax.axis_index("pipe")
    dp = lax.axis_index("dp").astype(I32)
    me = dp.reshape(1)
    first_up = section < 2
    first = jnp.where(first_up, 1, 0).astype(I32)
    order = jnp.stack([first, 1 - first])
    every, outer, inner = (0, 1, 2, 3), (0, 3), (1, 2)

    def gather(x):
        return lax.all_gather(x, "dp", axis=0, tiled=True)

    def near(x, sections):
        return shift_dp(x, 1, sections), shift_dp(x, -1, sections)

    def hop(top, low, sections):
        return shift_dp(top, 1, sections), shift_dp(low, -1, sections)

    def far(left, right, sections):
        half = left.shape[0] // 2
        return hop(left[:half], right[half:], sections)

    wd_own, wg_own, wu_own = w_down[0, 0], w_gate[0, 0], w_up[0, 0]
    wd_near = near(wd_own, every)

    def ordered(x):
        return jnp.where(first_up, x[1], x[0]), jnp.where(first_up, x[0], x[1])

    targets = slot_targets(expert_routes[:, 0])
    tgt = ordered(targets)
    wts = ordered(route_weights[:, 0])
    tgt_t = [t.T for t in tgt]
    wts_t = [w.T for w in wts]
    cur = jnp.where(first_up, seed_grads[1], seed_grads[0])
    fup, fgate, hidden = prep(order, saved_gate[:, 0, 0, 0], saved_up[:, 0, 0, 0])

    wg_near = near(tie(wg_own, hidden, *wd_near), inner)

    edge = jnp.logical_or(section == 0, section == 3)
    keep_edge = edge.astype(I32).reshape(1)
    old = cur
    moves = [[(0, 1), (3, 2)], [(1, 2), (2, 1)], [(2, 3), (1, 0)]]
    results = []
    for step in range(4):
        at = step // 2
        keep = keep_edge if step == 1 else 1 - keep_edge if step == 3 else 0 * keep_edge
        outgoing = pre(keep, tgt_t[at], wts_t[at], old, cur)
        if step == 1:
            outgoing = tie(outgoing, *wg)
        old = cur
        buf = exchange(outgoing)
        if step == 0:
            halves = tie(wd_near[0], buf)[:128], tie(wd_near[1], buf)[128:]
            wd_outer = (wd_own,) + wd_near + hop(*halves, outer)
            rows, dgu_part = hidden_near(at, me, buf, fup, fgate, wd_outer[:3])
            dgu = hidden_far(at, me, rows, fup, fgate, dgu_part, *wd_outer[3:])
            ready = tie(dgu, *wg_near)
            others = [shift_dp(ready, step_dp, outer) for step_dp in (1, -1, 2)]
            wg_halves = tie(wg_near[0], others[0])[: CH // 2], tie(wg_near[1], others[0])[CH // 2 :]
            far_dgu, top, low = lax.optimization_barrier((others[2],) + wg_halves)
            sent = own_grads(me, dgu, *others[:2], far_dgu, wg_own, wu_own)
            wd = (wd_own,) + wd_near + hop(*[tie(h, dgu_part) for h in halves], inner)
            sent = tie(sent, *wd)
            wu_full = gather(tie(wu_own, sent))
            wg = (wg_own,) + wg_near + hop(tie(top, sent), tie(low, sent), inner)
            home = lax.all_to_all(
                sent.reshape(4 * EXP, 8, PCH), ("dp", "expert"), split_axis=0, concat_axis=0, tiled=True
            ).reshape(4, MAIN, PCH)
            result = post(tgt[at], cur, home)
        else:
            if step == 1:
                wg_full = (gather(tie(wg_own, buf)),)
                all_first = gather(buf)
                hidden_all = lax.all_gather(tie(hidden, buf), "dp", axis=0)
                part, du = front_pass(at, me, buf, fup, fgate, wd, wg)
                packed = back_pass(du, part, wu_full)
            elif step == 2:
                packed = expert_pass(at, me, buf, fup, fgate, wd, wg, wu_full)
            else:
                all_second = gather(buf)
                packed = expert_pass(at, me, buf, fup, fgate, wd_outer, wg_full, wu_full)
            result = post(tgt[at], cur, exchange(packed))
        results.append(result)
        if step < 3:
            cur = lax.ppermute(result, "pipe", moves[step])

    res_first = jnp.where(edge, results[0], results[1])
    res_second = jnp.where(edge, results[3], results[2])
    input_grads = jnp.where(
        first_up, jnp.stack([res_second, res_first]), jnp.stack([res_first, res_second])
    )[:, None]

    hidden_mine = lax.dynamic_slice_in_dim(hidden_all, dp * 256, 256, axis=3)
    hidden_t = hidden_mine.transpose(1, 3, 0, 2).reshape(2, 256, 4 * SLOTS)
    down_grads = down_last(hidden_t[1], all_second, down_first(hidden_t[0], all_first))
    return input_grads, down_grads[None, None]


def solution(mesh):
    return jax.shard_map(
        per_device,
        mesh=mesh,
        in_specs=(
            P(None, ("expert", "dp"), None),
            P(None, "pipe", ("expert", "dp"), None),
            P(None, "pipe", ("expert", "dp"), None),
            P(None, "pipe", "dp", "expert", None, None),
            P(None, "pipe", "dp", "expert", None, None),
            P("pipe", "expert", "dp", None),
            P("pipe", "expert", "dp", None),
            P("pipe", "expert", "dp", None),
        ),
        out_specs=(P(None, "pipe", ("expert", "dp"), None), P("pipe", "expert", "dp", None)),
        check_vma=False,
    )
```
